32 devices in a mesh: dp: 8 (over y, x, core), fsdp: 4 (over z).
Axes of the slice: x: 2, y: 2, z: 4, core: 2. Of those that a mesh axis runs over, the one named last changes fastest.
Arguments:
- inputs: bfloat16 [32, 1024, 1024], P(('dp', 'fsdp')), may hold values from -6 to 6
- cotangent: bfloat16 [32, 1024, 1024], P(('dp', 'fsdp')), may hold values from -6 to 6
- frames: int32 [32], P(('dp', 'fsdp')), may hold values from 204 to 1024, as said below
- w_qkv: float32 [1024, 3072], P(('dp', 'fsdp')), may hold values from -0.1875 to 0.1875
- w_out: float32 [1024, 1024], P(('dp', 'fsdp')), may hold values from -1.5 to 1.5
- w_up: float32 [1024, 4096], P(('dp', 'fsdp')), may hold values from -0.1875 to 0.1875
- w_down: float32 [4096, 1024], P(('dp', 'fsdp')), may hold values from -0.09375 to 0.09375
- norm_gains: float32 [2, 1024], P(None, ('dp', 'fsdp')), may hold values from 0.8 to 6
- first_qkv: float32 [1024, 3072], P(('dp', 'fsdp')), may hold values from -6.1035156e-05 to 6.1035156e-05
- first_out: float32 [1024, 1024], P(('dp', 'fsdp')), may hold values from -6.1035156e-05 to 6.1035156e-05
- first_up: float32 [1024, 4096], P(('dp', 'fsdp')), may hold values from -1.9073486e-05 to 1.9073486e-05
- first_down: float32 [4096, 1024], P(('dp', 'fsdp')), may hold values from -3.0517578e-05 to 3.0517578e-05
- first_gains: float32 [2, 1024], P(None, ('dp', 'fsdp')), may hold values from -0.00024414062 to 0.00024414062
- second_qkv: float32 [1024, 3072], P(('dp', 'fsdp')), may hold values from 5.722046e-10 to 2.2649764e-09
- second_out: float32 [1024, 1024], P(('dp', 'fsdp')), may hold values from 5.722046e-10 to 2.2649764e-09
- second_up: float32 [1024, 4096], P(('dp', 'fsdp')), may hold values from 2.9802324e-11 to 1.192093e-10
- second_down: float32 [4096, 1024], P(('dp', 'fsdp')), may hold values from 5.960465e-11 to 2.384186e-10
- second_gains: float32 [2, 1024], P(None, ('dp', 'fsdp')), may hold values from 6.3180923e-09 to 2.503395e-08
- shadow_qkv: float32 [1024, 3072], P(('dp', 'fsdp')), may hold values from -0.1875 to 0.1875
- shadow_out: float32 [1024, 1024], P(('dp', 'fsdp')), may hold values from -1.5 to 1.5
- shadow_up: float32 [1024, 4096], P(('dp', 'fsdp')), may hold values from -0.1875 to 0.1875
- shadow_down: float32 [4096, 1024], P(('dp', 'fsdp')), may hold values from -0.09375 to 0.09375
- shadow_gains: float32 [2, 1024], P(None, ('dp', 'fsdp')), may hold values from 0.5 to 1.5
Outputs:
- out_layer: bfloat16 [32, 1024, 1024], P(('dp', 'fsdp'))
- grad_input: float32 [32, 1024, 1024], P(('dp', 'fsdp'))
- grad_norm: float32 [], replicated
- qkv_new: float32 [1024, 3072], P(('dp', 'fsdp'))
- out_new: float32 [1024, 1024], P(('dp', 'fsdp'))
- up_new: float32 [1024, 4096], P(('dp', 'fsdp'))
- down_new: float32 [4096, 1024], P(('dp', 'fsdp'))
- gains_new: float32 [2, 1024], P(None, ('dp', 'fsdp'))
- qkv_first: float32 [1024, 3072], P(('dp', 'fsdp'))
- out_first: float32 [1024, 1024], P(('dp', 'fsdp'))
- up_first: float32 [1024, 4096], P(('dp', 'fsdp'))
- down_first: float32 [4096, 1024], P(('dp', 'fsdp'))
- gains_first: float32 [2, 1024], P(None, ('dp', 'fsdp'))
- qkv_second: float32 [1024, 3072], P(('dp', 'fsdp'))
- out_second: float32 [1024, 1024], P(('dp', 'fsdp'))
- up_second: float32 [1024, 4096], P(('dp', 'fsdp'))
- down_second: float32 [4096, 1024], P(('dp', 'fsdp'))
- gains_second: float32 [2, 1024], P(None, ('dp', 'fsdp'))
- qkv_shadow: float32 [1024, 3072], P(('dp', 'fsdp'))
- out_shadow: float32 [1024, 1024], P(('dp', 'fsdp'))
- up_shadow: float32 [1024, 4096], P(('dp', 'fsdp'))
- down_shadow: float32 [4096, 1024], P(('dp', 'fsdp'))
- gains_shadow: float32 [2, 1024], P(None, ('dp', 'fsdp'))
The draws below stay inside these ranges and needn't reach their ends.
Inputs may be any that keep to these rules, and one draw needn't show every extreme that they name: Each utterance's count of valid frames; some utterance has exactly 1024.
All inputs are finite; a program needn't handle non-finite values.
Results may differ from the reference program's by a relative error of at most 0.012.
The reference program's roundings to bfloat16 on the way count: a program that leaves them out, or rounds other values in their place, can miss the bound.
Values may be sent and summed in bfloat16 or wider, within the bound.
No kernel may reach another device: no remote copies, remote signals or barrier semaphores. Data moves between devices by JAX's collectives and lax.ppermute only.
A program may use at most 320 MiB of HBM per device.

```python
import math
import jax
import jax.numpy as jnp
from jax import lax

D = 1024
HEAD_DIM = 64
FF = 4096
LEN = 1024
STEP = 7
ITEMS = 32
FANO = 16


def draw_frames(key, part):
    counts = jax.random.randint(jax.random.fold_in(key, 11), (ITEMS,), LEN // 5, LEN + 1)
    chosen = jax.random.randint(jax.random.fold_in(key, 12), (), 0, ITEMS)
    return jnp.where(jnp.arange(ITEMS) == chosen, LEN, counts).astype(jnp.int32)


def draw_norm_gains(key, part):
    factor = jax.random.uniform(jax.random.fold_in(key, 21), (2, D), jnp.float32, 0.8, 1.2)
    along = jnp.arange(D).astype(jnp.float32) / (D - 1)
    rising = 1.0 + 2.0 * along
    return (rising[None, :] * factor).astype(jnp.float32)


def level_of(key, dims, pieces, least, largest):
    def one(dim, shards_of):
        draws = jax.random.uniform(jax.random.fold_in(jax.random.fold_in(key, 6), dim), (shards_of,), jnp.float32, least / len(pieces), largest / len(pieces))
        return jnp.repeat(jnp.exp(draws), dims[dim] // shards_of).reshape((-1,) + (1,) * (len(dims) - dim - 1))

    level = one(*pieces[0])
    for cut in pieces[1:]:
        level = level * one(*cut)
    return level


def scatter_about(key, shape, spread, limit, pieces=(), kind=jnp.bfloat16):
    array = jax.random.normal(key, shape, jnp.float32) * spread
    if len(pieces) > 0:
        array = level_of(key, shape, pieces, -0.22, 0.18) * array
    return jnp.clip(array, min=-limit, max=limit).astype(kind)


def setup_inputs(seed: int = 0) -> dict:
    key_list = jax.random.split(jax.random.key(seed), 24)
    return {
        "inputs": scatter_about(key_list[0], (ITEMS, LEN, D), 1.0, 6.0, ((0, 32),)),
        "cotangent": scatter_about(key_list[1], (ITEMS, LEN, D), 1.0, 6.0, ((0, 32),)),
        "frames": draw_frames(jax.random.fold_in(key_list[23], 71), 0),
        "w_qkv": scatter_about(key_list[3], (D, 3 * D), D ** -0.5, 0.1875, ((0, 32),), jnp.float32),
        "w_out": scatter_about(key_list[4], (D, D), FANO ** -0.5, 1.5, ((0, 32),), jnp.float32),
        "w_up": scatter_about(key_list[5], (D, FF), D ** -0.5, 0.1875, ((0, 32),), jnp.float32),
        "w_down": scatter_about(key_list[6], (FF, D), FF ** -0.5, 0.09375, ((0, 32),), jnp.float32),
        "norm_gains": draw_norm_gains(jax.random.fold_in(key_list[23], 71), 0),
        "first_qkv": scatter_about(key_list[8], (D, 3 * D), (0.033 * (2 * D * FF) ** -0.5), 6.103515625e-05, ((0, 32),), jnp.float32),
        "first_out": scatter_about(key_list[9], (D, D), (0.033 * (2 * D * FF) ** -0.5), 6.103515625e-05, ((0, 32),), jnp.float32),
        "first_up": scatter_about(key_list[10], (D, FF), (0.01 * (2 * D * FF) ** -0.5), 1.9073486328125e-05, ((0, 32),), jnp.float32),
        "first_down": scatter_about(key_list[11], (FF, D), (0.014 * (2 * D * FF) ** -0.5), 3.0517578125e-05, ((0, 32),), jnp.float32),
        "first_gains": scatter_about(key_list[12], (2, D), (0.11 * (2 * D * FF) ** -0.5), 0.00024414062, ((1, 32),), jnp.float32),
        "second_qkv": jnp.clip(jnp.exp(math.log(2.2649764286342133e-09) - 1.375823 * jax.random.uniform(key_list[13], (D, 3 * D), jnp.float32) ** level_of(key_list[13], (D, 3 * D), ((0, 32),), -0.2, 0.2)), 5.722046170220096e-10, 2.2649764286342133e-09),
        "second_out": jnp.clip(jnp.exp(math.log(2.2649764286342133e-09) - 1.375823 * jax.random.uniform(key_list[14], (D, D), jnp.float32) ** level_of(key_list[14], (D, D), ((0, 32),), -0.2, 0.2)), 5.722046170220096e-10, 2.2649764286342133e-09),
        "second_up": jnp.clip(jnp.exp(math.log(1.1920929521291868e-10) - 1.3862944 * jax.random.uniform(key_list[15], (D, FF), jnp.float32) ** level_of(key_list[15], (D, FF), ((0, 32),), -0.2, 0.2)), 2.980232380322967e-11, 1.1920929521291868e-10),
        "second_down": jnp.clip(jnp.exp(math.log(2.3841859042583735e-10) - 1.3862944 * jax.random.uniform(key_list[16], (FF, D), jnp.float32) ** level_of(key_list[16], (FF, D), ((0, 32),), -0.2, 0.2)), 5.960464760645934e-11, 2.3841859042583735e-10),
        "second_gains": jnp.clip(jnp.exp(math.log(2.5033950024067053e-08) - 1.3768156 * jax.random.uniform(key_list[17], (2, D), jnp.float32) ** level_of(key_list[17], (2, D), ((1, 32),), -0.2, 0.2)), 6.318092271584419e-09, 2.5033950024067053e-08),
        "shadow_qkv": scatter_about(key_list[18], (D, 3 * D), D ** -0.5, 0.1875, ((0, 32),), jnp.float32),
        "shadow_out": scatter_about(key_list[19], (D, D), FANO ** -0.5, 1.5, ((0, 32),), jnp.float32),
        "shadow_up": scatter_about(key_list[20], (D, FF), D ** -0.5, 0.1875, ((0, 32),), jnp.float32),
        "shadow_down": scatter_about(key_list[21], (FF, D), FF ** -0.5, 0.09375, ((0, 32),), jnp.float32),
        "shadow_gains": jnp.clip(1.0 + 0.1 * jax.random.normal(key_list[22], (2, D), jnp.float32), 0.5, 1.5),
    }


@jax.custom_vjp
def low(v):
    return lax.optimization_barrier(v.astype(jnp.bfloat16)).astype(jnp.float32)

@jax.custom_vjp
def low_back(v):
    return v

def low_keep(v):
    return (low(v), None)

def low_pass(kept, grad):
    return (grad,)

def back_keep(v):
    return (v, None)

def back_low(kept, grad):
    return (low(grad),)
low.defvjp(low_keep, low_pass)
low_back.defvjp(back_keep, back_low)
NORM_EPS = 1e-06
ADAM_EPS = 1e-08
BETA_ONE = 0.9
BETA_TWO = 0.95
SHADOW_KEEP = 0.8
CLIP_NORM = 1.0
PRECISE = lax.Precision.HIGHEST

def norm_apply(residual, gain_row):
    rms_inv = lax.rsqrt(lax.optimization_barrier(jnp.mean(residual * residual, axis=-1, keepdims=True)) + NORM_EPS)
    return residual * rms_inv * gain_row

def block_forward(residual, valid_count, w_qkv, w_out, w_up, w_down, norm_gains):
    length, model_width = residual.shape
    head_count = model_width // HEAD_DIM
    gains_low = low(norm_gains)
    normed_one = low(norm_apply(residual, gains_low[0]))
    qkv_vals = low_back(low(jnp.dot(normed_one, low(w_qkv), precision=PRECISE, preferred_element_type=jnp.float32)))
    queries = qkv_vals[:, :model_width].reshape(length, head_count, HEAD_DIM)
    key_vecs = qkv_vals[:, model_width:2 * model_width].reshape(length, head_count, HEAD_DIM)
    val_vecs = qkv_vals[:, 2 * model_width:].reshape(length, head_count, HEAD_DIM)
    positions = jnp.arange(length).astype(jnp.int32)
    allowed = (positions[None, :] <= positions[:, None]) & (positions[None, :] < valid_count)
    scores = low_back(jnp.einsum('qhd,khd->hqk', queries, key_vecs, precision=PRECISE) * HEAD_DIM ** (-0.5))
    scores = jnp.where(allowed[None], scores, -1e+30)
    attn_probs = low(jax.nn.softmax(scores, axis=-1))
    attn_out = low_back(low(jnp.einsum('hqk,khd->qhd', attn_probs, val_vecs, precision=PRECISE).reshape(length, model_width)))
    middle = residual + low_back(jnp.dot(attn_out, low(w_out), precision=PRECISE, preferred_element_type=jnp.float32))
    normed_two = low(norm_apply(middle, gains_low[1]))
    pre_act = low_back(jnp.dot(normed_two, low(w_up), precision=PRECISE, preferred_element_type=jnp.float32))
    activation = low(jax.nn.gelu(pre_act))
    return middle + low_back(jnp.dot(activation, low(w_down), precision=PRECISE, preferred_element_type=jnp.float32))

def adam_step(weight, first, second, gradient, clip_factor, step_rate, decay_rate, shadow):
    clipped = gradient * clip_factor
    first_new = BETA_ONE * first + (1.0 - BETA_ONE) * clipped
    second_new = BETA_TWO * second + (1.0 - BETA_TWO) * clipped * clipped
    first_hat = first_new / (1.0 - BETA_ONE ** STEP)
    second_hat = second_new / (1.0 - BETA_TWO ** STEP)
    weight_new = weight - step_rate * (first_hat / (jnp.sqrt(second_hat) + ADAM_EPS) + decay_rate * weight)
    shadow_new = SHADOW_KEEP * shadow + (1.0 - SHADOW_KEEP) * weight_new
    return (weight_new, first_new, second_new, shadow_new)

def reference(inputs, cotangent, frames, w_qkv, w_out, w_up, w_down, norm_gains, first_qkv, first_out, first_up, first_down, first_gains, second_qkv, second_out, second_up, second_down, second_gains, shadow_qkv, shadow_out, shadow_up, shadow_down, shadow_gains):
    masters = (w_qkv, w_out, w_up, w_down, norm_gains)

    def one_item(totals, packed):
        item_in, item_cot, valid_count = packed
        positions = jnp.arange(item_in.shape[0]).astype(jnp.int32)
        valid_mask = (positions < valid_count).astype(jnp.float32)

        def apply_layer(residual, *weights):
            return block_forward(residual, valid_count, *weights)
        result, pull = jax.vjp(apply_layer, item_in.astype(jnp.float32), *masters)
        gradients = pull(item_cot.astype(jnp.float32) * valid_mask[:, None])
        totals = tuple((total_grad + grad_piece for total_grad, grad_piece in zip(totals, gradients[1:])))
        return (totals, (result.astype(jnp.bfloat16), gradients[0]))
    initial = tuple((jnp.zeros_like(master) for master in masters))
    gradients, (out_layer, grad_input) = lax.scan(one_item, initial, (inputs, cotangent, frames))
    total_sq = sum((jnp.sum(grad_piece * grad_piece) for grad_piece in gradients))
    grad_norm = jnp.sqrt(total_sq)
    clip_factor = jnp.minimum(1.0, CLIP_NORM / grad_norm)
    rates = (0.6 / D ** 0.5, 0.6 / FANO ** 0.5, 0.6 / D ** 0.5, 0.6 / FF ** 0.5, 1.0)
    decays = (0.1, 0.1, 0.1, 0.1, 0.0)
    firsts = (first_qkv, first_out, first_up, first_down, first_gains)
    seconds = (second_qkv, second_out, second_up, second_down, second_gains)
    shadows = (shadow_qkv, shadow_out, shadow_up, shadow_down, shadow_gains)
    updated = [adam_step(masters[index], firsts[index], seconds[index], gradients[index], clip_factor, rates[index], decays[index], shadows[index]) for index in range(5)]
    return (out_layer, grad_input, grad_norm, updated[0][0], updated[1][0], updated[2][0], updated[3][0], updated[4][0], updated[0][1], updated[1][1], updated[2][1], updated[3][1], updated[4][1], updated[0][2], updated[1][2], updated[2][2], updated[3][2], updated[4][2], updated[0][3], updated[1][3], updated[2][3], updated[3][3], updated[4][3])
```

```python
import functools

import jax
import jax.numpy as jnp
import numpy as np
from jax import lax
from jax.experimental import pallas as pl
from jax.experimental.pallas import tpu as pltpu
from jax.sharding import PartitionSpec as P

D = 1024
HEAD_DIM = 64
FF = 4096
STEP = 7
FANO = 16

NORM_EPS = 1e-06
ADAM_EPS = 1e-08
BETA_ONE = 0.9
BETA_TWO = 0.95
SHADOW_KEEP = 0.8
CLIP_NORM = 1.0

AXES = ("dp", "fsdp")
CHUNKS = 4
GROUPS = 2
LANES = 128
VMEM = 62 << 20
f32 = jnp.float32
bf16 = jnp.bfloat16
NT = (((1,), (1,)), ((), ()))
TN = (((0,), (0,)), ((), ()))
GELU_A = 0.7978845608028654
GELU_B = 0.044715


def full(shape, single=False):
    rank = len(shape)
    mode = dict(pipeline_mode=pl.Buffered(1)) if single else {}
    return pl.BlockSpec(shape, lambda *_: (0,) * rank, **mode)


def params():
    return pltpu.CompilerParams(vmem_limit_bytes=VMEM)


def cost(flops, nbytes, trans=0):
    return pl.CostEstimate(flops=flops, bytes_accessed=nbytes, transcendentals=trans)


class Plan:
    def __init__(self, mesh):
        self.ndp, self.nfs = mesh.shape["dp"], mesh.shape["fsdp"]
        self.ndev = self.ndp * self.nfs
        self.bits = self.ndp.bit_length() - 1
        others = list(range(1, self.bits))
        half = len(others) // 2
        self.order = (others, others[half:] + others[:half])
        self.block = D // self.ndp
        tab = np.zeros((self.ndp, self.ndp), np.int32)
        for me in range(self.ndp):
            for rel in range(self.ndp):
                core = (me & 1) ^ (rel >> (self.bits - 1))
                nat = core
                for s, bit in enumerate(self.order[core]):
                    r = (rel >> (self.bits - 2 - s)) & 1
                    nat |= (((me >> bit) & 1) ^ r) << bit
                tab[me, rel] = nat
        self.tab = tab

    def pairs(self, flip):
        out = []
        for d in range(self.ndp):
            for f in range(self.nfs):
                out.append((d * self.nfs + f, flip(d) * self.nfs + f))
        return out

    def core_pairs(self):
        return self.pairs(lambda d: d ^ 1)

    def mix_pairs(self, s):
        return self.pairs(lambda d: d ^ (1 << self.order[d & 1][s]))

    def gather(self, held):
        pieces = [held]
        for s in reversed(range(self.bits - 1)):
            pieces = pieces + (yield pieces, self.mix_pairs(s))
        return pieces + (yield pieces, self.core_pairs())

    def scatter(self, sent, kept):
        (got,) = yield [sent], self.core_pairs()
        for s in range(self.bits - 1):
            rows = kept.shape[0] // 2
            total = lambda lo: (
                kept[lo : lo + rows].astype(f32) + got[lo : lo + rows].astype(f32)
            ).astype(bf16)
            sent, kept = total(rows), total(0)
            (got,) = yield [sent], self.mix_pairs(s)
        return kept.astype(f32) + got.astype(f32)


def tie(tree):
    leaves, form = jax.tree.flatten(tree)
    place = pl.BlockSpec(memory_space=pl.ANY)
    count = len(leaves)
    tied = pl.pallas_call(
        lambda *refs: None,
        in_specs=[place] * count,
        out_specs=[place] * count,
        out_shape=[jax.ShapeDtypeStruct(v.shape, v.dtype) for v in leaves],
        input_output_aliases={i: i for i in range(count)},
        name="tie",
    )(*leaves)
    return jax.tree.unflatten(form, tied)


class Flow:
    def __init__(self):
        self.live, self.flying, self.done = {}, {}, {}

    def add(self, name, transfer):
        self.live[name] = transfer

    def step(self, x, names):
        names = [n for n in names if n not in self.done]
        came = {n: self.flying.pop(n) for n in names if n in self.flying}
        x, came = tie((x, came))
        for n in names:
            try:
                if n in came:
                    arrays, pairs = self.live[n].send(came[n])
                else:
                    arrays, pairs = next(self.live[n])
                    x, arrays = tie((x, arrays))
                self.flying[n] = [lax.ppermute(v, AXES, pairs) for v in arrays]
            except StopIteration as stop:
                self.done[n] = stop.value
        return x

    def until(self, x, names):
        while any(n not in self.done for n in names):
            x = self.step(x, names)
        return x


def natural(dst, cols, pieces, src_cols, tab, block):
    j = 0
    for piece in pieces:
        for i in range(piece.shape[0] // block):
            row = pl.multiple_of(tab[j] * block, block)
            dst[pl.ds(row, block), cols] = piece[i * block : (i + 1) * block, src_cols]
            j += 1


def relative(sent, kept, cols, src, src_cols, tab, block):
    half = src.shape[0] // block // 2
    for j in range(2 * half):
        row = pl.multiple_of(tab[j] * block, block)
        out = kept if j < half else sent
        i = j % half
        out[i * block : (i + 1) * block, cols] = src[pl.ds(row, block), src_cols]


def qkv_kernel(count, block, tab, x_ref, *refs):
    gains, weights = refs[:count], refs[count : 2 * count]
    qkv_ref, u_ref, gain_ref, u_t_ref, w_nat, g_nat = refs[2 * count :]

    @pl.when(pl.program_id(0) == 0)
    def _():
        natural(g_nat, slice(None), gains, slice(None), tab, block)
        rows = g_nat[...].astype(f32).T
        gain_ref[...] = rows[:8]
        x = x_ref[...].astype(f32)
        r = lax.rsqrt(jnp.mean(x * x, axis=1, keepdims=True) + NORM_EPS)
        u = (x * r * rows[0:1]).astype(bf16)
        u_ref[...] = u
        u_t_ref[...] = u.T

    natural(w_nat, slice(None), weights, slice(None), tab, block)
    qkv_ref[...] = jnp.dot(u_ref[...], w_nat[...], preferred_element_type=f32).astype(bf16)


def project_qkv(tab, x, pieces, block):
    length, width = x.shape
    wide = 512
    count = len(pieces)
    columns = pieces[0].shape[1] - LANES
    last = columns // LANES
    return pl.pallas_call(
        functools.partial(qkv_kernel, count, block),
        grid_spec=pltpu.PrefetchScalarGridSpec(
            num_scalar_prefetch=1,
            grid=(columns // wide,),
            in_specs=[full((length, width), True)]
            + [pl.BlockSpec((p.shape[0], LANES), lambda j, t: (0, last)) for p in pieces]
            + [pl.BlockSpec((p.shape[0], wide), lambda j, t: (0, j)) for p in pieces],
            out_specs=[
                pl.BlockSpec((length, wide), lambda j, t: (0, j)),
                full((length, width)),
                full((8, width)),
                full((width, length)),
            ],
            scratch_shapes=[pltpu.VMEM((width, wide), bf16), pltpu.VMEM((width, LANES), bf16)],
        ),
        out_shape=[
            jax.ShapeDtypeStruct((length, columns), bf16),
            jax.ShapeDtypeStruct((length, width), bf16),
            jax.ShapeDtypeStruct((8, width), f32),
            jax.ShapeDtypeStruct((width, length), bf16),
        ],
        compiler_params=params(),
        cost_estimate=cost(2 * length * width * columns, 20 << 20),
        name="qkv",
    )(tab, x, *pieces, *pieces)


def attend_kernel(rows_of, n_ref, q_ref, k_ref, v_ref, o_ref, lse_ref):
    n = n_ref[0]
    length = q_ref.shape[0]
    lane = lax.broadcasted_iota(jnp.int32, (1, LANES), 1)
    masks = [(lane < HEAD_DIM).astype(bf16), (lane >= HEAD_DIM).astype(bf16)]
    v_t = v_ref[...].T
    for i in range(length // rows_of):
        rows = pl.ds(i * rows_of, rows_of)
        keys = (i + 1) * rows_of

        def run(limited):
            q = q_ref[rows, :] * bf16(HEAD_DIM**-0.5)
            k = k_ref[0:keys, :]
            parts = []
            for h in range(2):
                s = lax.dot_general(k, q * masks[h], NT, preferred_element_type=f32)
                if limited:
                    key = lax.broadcasted_iota(jnp.int32, (keys, rows_of), 0)
                    query = lax.broadcasted_iota(jnp.int32, (keys, rows_of), 1) + i * rows_of
                    s = jnp.where((key <= query) & (key < n), s, -1e30)
                else:
                    key = lax.broadcasted_iota(jnp.int32, (rows_of, rows_of), 0)
                    query = lax.broadcasted_iota(jnp.int32, (rows_of, rows_of), 1)
                    tail = jnp.where(key <= query, s[keys - rows_of :], -1e30)
                    s = tail if i == 0 else jnp.concatenate([s[: keys - rows_of], tail], axis=0)
                peak = jnp.max(s, axis=0, keepdims=True)
                e = jnp.exp(s - peak)
                total = jnp.sum(e, axis=0, keepdims=True)
                p = (e * (1.0 / total)).astype(bf16)
                v_h = v_t[h * HEAD_DIM : (h + 1) * HEAD_DIM, 0:keys]
                parts.append(jnp.dot(v_h, p, preferred_element_type=f32))
                query = lax.broadcasted_iota(jnp.int32, (1, rows_of), 1) + i * rows_of
                lse_ref[0, h : h + 1, rows] = jnp.where(query < n, peak + jnp.log(total), 1e30)
            o_ref[rows, :] = jnp.concatenate(parts, axis=0).astype(bf16).T

        @pl.when(n >= keys)
        def _():
            run(False)

        @pl.when(n < keys)
        def _():
            run(True)


def attend(frames, qkv, at, pairs):
    length, width = qkv.shape[0], pairs * LANES
    every = qkv.shape[1] // 3 // LANES
    part = lambda c: pl.BlockSpec((length, LANES), lambda j, n: (0, j + at + c * every))
    return pl.pallas_call(
        functools.partial(attend_kernel, 512),
        grid_spec=pltpu.PrefetchScalarGridSpec(
            num_scalar_prefetch=1,
            grid=(pairs,),
            in_specs=[part(0), part(1), part(2)],
            out_specs=[
                pl.BlockSpec((length, LANES), lambda j, n: (0, j)),
                pl.BlockSpec((1, 2, length), lambda j, n: (j, 0, 0)),
            ],
        ),
        out_shape=[
            jax.ShapeDtypeStruct((length, width), bf16),
            jax.ShapeDtypeStruct((pairs, 2, length), f32),
        ],
        compiler_params=params(),
        cost_estimate=cost(16 * length * length * width, 8 << 20, length * length * 16),
        name="attend",
    )(frames, qkv, qkv, qkv)


def mid_kernel(count, groups, block, tab, x_ref, gain_ref, *refs):
    o_refs, refs = refs[:groups], refs[groups:]
    weights = refs[:count]
    mid_ref, u_ref, u_t_ref, w_nat = refs[count:]

    @pl.when(pl.program_id(0) == 0)
    def _():
        natural(w_nat, slice(None), weights, slice(None), tab, block)

    o = jnp.concatenate([ref[...] for ref in o_refs], axis=1)
    mid = x_ref[...].astype(f32) + jnp.dot(o, w_nat[...], preferred_element_type=f32)
    r = lax.rsqrt(jnp.mean(mid * mid, axis=1, keepdims=True) + NORM_EPS)
    u = (mid * r * gain_ref[1:2, :]).astype(bf16)
    mid_ref[...] = mid
    u_ref[...] = u
    u_t_ref[...] = u.T


def middle(tab, o, x, gains, pieces, block):
    length, width = x.shape
    rows = 256
    row = pl.BlockSpec((rows, width), lambda i, t: (i, 0))
    return pl.pallas_call(
        functools.partial(mid_kernel, len(pieces), len(o), block),
        grid_spec=pltpu.PrefetchScalarGridSpec(
            num_scalar_prefetch=1,
            grid=(length // rows,),
            in_specs=[row, full((8, width))]
            + [pl.BlockSpec((rows, v.shape[1]), lambda i, t: (i, 0)) for v in o]
            + [full(p.shape) for p in pieces],
            out_specs=[row, row, pl.BlockSpec((width, rows), lambda i, t: (0, i))],
            scratch_shapes=[pltpu.VMEM((width, width), bf16)],
        ),
        out_shape=[
            jax.ShapeDtypeStruct((length, width), f32),
            jax.ShapeDtypeStruct((length, width), bf16),
            jax.ShapeDtypeStruct((width, length), bf16),
        ],
        compiler_params=params(),
        cost_estimate=cost(2 * length * width * width, 16 << 20),
        name="middle",
    )(tab, x, gains, *o, *pieces)


def gelu_both(z):
    sq = z * z
    t = jnp.tanh(z * (GELU_A + (GELU_A * GELU_B) * sq))
    half = 0.5 + 0.5 * t
    slope = half + (0.5 * z) * (1.0 - t * t) * (GELU_A + (3 * GELU_A * GELU_B) * sq)
    return z * half, slope


def mlp_kernel(count, block, first, last, steps, tab, u_ref, u_t_ref, g_ref, *refs):
    ups, downs = refs[:count], refs[count : 2 * count]
    refs = refs[2 * count :]
    held_out = refs[0]
    held_du = None if first else refs[1]
    out_ref, du_ref, sent, kept, up_nat, down_nat, out_acc, du_acc, a_s, dz_s, grad, sems = refs[
        (1 if first else 2) :
    ]
    width = u_ref.shape[1]
    wide = 512
    everything = slice(None)
    step = pl.program_id(0)
    load_out = pltpu.make_async_copy(held_out, out_acc, sems.at[0])
    load_du = None if first else pltpu.make_async_copy(held_du, du_acc, sems.at[1])

    @pl.when(step == 0)
    def _():
        load_out.start()
        if first:
            du_acc[...] = jnp.zeros_like(du_acc)
        else:
            load_du.start()

    natural(up_nat, everything, ups, everything, tab, block)
    natural(down_nat, everything, downs, everything, tab, block)
    for f in range(width // wide):
        cols = slice(f * wide, (f + 1) * wide)
        z = jnp.dot(u_ref[...], up_nat[:, cols], preferred_element_type=f32)
        a, slope = gelu_both(z)
        da = lax.dot_general(g_ref[...], down_nat[cols, :], NT, preferred_element_type=f32)
        a_s[...] = a.astype(bf16)
        dz_s[...] = (da * slope).astype(bf16)
        if f == 0:

            @pl.when(step == 0)
            def _():
                load_out.wait()
                if not first:
                    load_du.wait()

        out_acc[...] += jnp.dot(a_s[...], down_nat[cols, :], preferred_element_type=f32)
        du_acc[...] += lax.dot_general(dz_s[...], up_nat[:, cols], NT, preferred_element_type=f32)
        grad[:, cols] = jnp.dot(u_t_ref[...], dz_s[...], preferred_element_type=f32).astype(bf16)
        down = lax.dot_general(a_s[...], g_ref[...], TN, preferred_element_type=f32)
        grad[cols, width:] = down.astype(bf16)
    relative(sent, kept, everything, grad, everything, tab, block)

    @pl.when(step == steps - 1)
    def _():
        if last:
            out_ref[...] = out_acc[...].astype(bf16)
            save_out = None
        else:
            save_out = pltpu.make_async_copy(out_acc, out_ref, sems.at[0])
            save_out.start()
        save_du = pltpu.make_async_copy(du_acc, du_ref, sems.at[1])
        save_du.start()
        if save_out is not None:
            save_out.wait()
        save_du.wait()


def feed_forward(tab, u, u_t, g, pieces, held, block, first, last):
    length, width = u.shape
    steps = pieces[0].shape[1] // (2 * width)
    half = width // 2
    anywhere = pl.BlockSpec(memory_space=pl.ANY)
    count = len(pieces)
    held_inputs = held[:1] if first else held
    alias = {}
    base = 1 + 3 + 2 * count
    if not first:
        alias = {base + 1: 1}
        if not last:
            alias[base] = 0
    acc = jax.ShapeDtypeStruct((length, width), f32)
    return pl.pallas_call(
        functools.partial(mlp_kernel, count, block, first, last, steps),
        grid_spec=pltpu.PrefetchScalarGridSpec(
            num_scalar_prefetch=1,
            grid=(steps,),
            in_specs=[
                full((length, width), True),
                full((width, length), True),
                full((length, width), True),
            ]
            + [pl.BlockSpec((p.shape[0], width), lambda j, t: (0, 2 * j)) for p in pieces]
            + [pl.BlockSpec((p.shape[0], width), lambda j, t: (0, 2 * j + 1)) for p in pieces]
            + [anywhere] * len(held_inputs),
            out_specs=[
                full((length, width)) if last else anywhere,
                anywhere,
                pl.BlockSpec((half, 2 * width), lambda j, t: (0, j)),
                pl.BlockSpec((half, 2 * width), lambda j, t: (0, j)),
            ],
            scratch_shapes=[
                pltpu.VMEM((width, width), bf16),
                pltpu.VMEM((width, width), bf16),
                pltpu.VMEM((length, width), f32),
                pltpu.VMEM((length, width), f32),
                pltpu.VMEM((length, 512), bf16),
                pltpu.VMEM((length, 512), bf16),
                pltpu.VMEM((width, 2 * width), bf16),
                pltpu.SemaphoreType.DMA((2,)),
            ],
        ),
        out_shape=[
            jax.ShapeDtypeStruct((length, width), bf16) if last else acc,
            acc,
            jax.ShapeDtypeStruct((half, 2 * width * steps), bf16),
            jax.ShapeDtypeStruct((half, 2 * width * steps), bf16),
        ],
        input_output_aliases=alias,
        compiler_params=params(),
        cost_estimate=cost(12 * length * width * width * steps, 24 << 20),
        name="feed_forward",
    )(tab, u, u_t, g, *pieces, *pieces, *held_inputs)


def norm_back(v, gain, du):
    r = lax.rsqrt(jnp.mean(v * v, axis=1, keepdims=True) + NORM_EPS)
    up = du * gain
    return r * up - v * (r * r * r * jnp.mean(up * v, axis=1, keepdims=True))


def dmid_kernel(count, groups, block, steps, tab, n_ref, du_ref, mid_ref, cot_ref, gain_ref, *refs):
    o_refs, refs = refs[:groups], refs[groups:]
    weights = refs[:count]
    dmid_ref, do_ref, sent, kept, w_nat, total, grad = refs[count:]
    i = pl.program_id(0)
    rows = du_ref.shape[0]

    @pl.when(i == 0)
    def _():
        natural(w_nat, slice(None), weights, slice(None), tab, block)

    frame = lax.broadcasted_iota(jnp.int32, (rows, 1), 0) + i * rows
    g = jnp.where(frame < n_ref[0], cot_ref[...].astype(f32), 0.0)
    dmid = g + norm_back(mid_ref[...], gain_ref[1:2, :], du_ref[...])
    dmid_ref[...] = dmid
    low = dmid.astype(bf16)
    do_ref[...] = lax.dot_general(low, w_nat[...], NT, preferred_element_type=f32).astype(bf16)
    o = jnp.concatenate([ref[...] for ref in o_refs], axis=1)
    part = lax.dot_general(o, low, TN, preferred_element_type=f32)

    @pl.when(i == 0)
    def _():
        total[...] = part

    @pl.when(i > 0)
    def _():
        total[...] += part

    @pl.when(i == steps - 1)
    def _():
        grad[...] = total[...].astype(bf16)
        relative(sent, kept, slice(None), grad, slice(None), tab, block)


def middle_back(tab, frames, du, mid, cot, gains, o, pieces, block):
    length, width = mid.shape
    rows = 256
    steps = length // rows
    row = pl.BlockSpec((rows, width), lambda i, t, n: (i, 0))
    half = width // 2
    return pl.pallas_call(
        functools.partial(dmid_kernel, len(pieces), len(o), block, steps),
        grid_spec=pltpu.PrefetchScalarGridSpec(
            num_scalar_prefetch=2,
            grid=(steps,),
            in_specs=[row, row, row, full((8, width))]
            + [pl.BlockSpec((rows, v.shape[1]), lambda i, t, n: (i, 0)) for v in o]
            + [full(p.shape) for p in pieces],
            out_specs=[row, row, full((half, width)), full((half, width))],
            scratch_shapes=[
                pltpu.VMEM((width, width), bf16),
                pltpu.VMEM((width, width), f32),
                pltpu.VMEM((width, width), bf16),
            ],
        ),
        out_shape=[
            jax.ShapeDtypeStruct((length, width), f32),
            jax.ShapeDtypeStruct((length, width), bf16),
            jax.ShapeDtypeStruct((half, width), bf16),
            jax.ShapeDtypeStruct((half, width), bf16),
        ],
        compiler_params=params(),
        cost_estimate=cost(4 * length * width * width, 24 << 20),
        name="middle_back",
    )(tab, frames, du, mid, cot, gains, *o, *pieces)


def attend_back_kernel(rows_of, n_ref, q_ref, k_ref, v_ref, g_ref, lse_ref, d_ref, dk, dv):
    n = n_ref[0]
    length = q_ref.shape[0]
    scale = HEAD_DIM**-0.5
    lane = lax.broadcasted_iota(jnp.int32, (1, LANES), 1)
    masks = [(lane < HEAD_DIM).astype(bf16), (lane >= HEAD_DIM).astype(bf16)]
    dk[...] = jnp.zeros_like(dk)
    dv[...] = jnp.zeros_like(dv)
    for i in range(length // rows_of):
        rows = pl.ds(i * rows_of, rows_of)
        keys = (i + 1) * rows_of

        @pl.when(n > i * rows_of)
        def _():
            q = q_ref[rows, :] * bf16(scale)
            g = g_ref[rows, :]
            k, v = k_ref[0:keys, :], v_ref[0:keys, :]
            dq = None
            for h in range(2):
                q_h, g_h, k_h = q * masks[h], g * masks[h], k * masks[h]
                s = lax.dot_general(k, q_h, NT, preferred_element_type=f32)
                key = lax.broadcasted_iota(jnp.int32, (rows_of, rows_of), 0)
                query = lax.broadcasted_iota(jnp.int32, (rows_of, rows_of), 1)
                tail = jnp.where(key <= query, s[keys - rows_of :], -1e30)
                s = tail if i == 0 else jnp.concatenate([s[: keys - rows_of], tail], axis=0)
                p = jnp.exp(s - lse_ref[0, h : h + 1, rows])
                dp = lax.dot_general(v, g_h, NT, preferred_element_type=f32)
                delta = jnp.sum(p * dp, axis=0, keepdims=True)
                ds = (p * (dp - delta)).astype(bf16)
                dv[0:keys, :] += jnp.dot(p.astype(bf16), g_h, preferred_element_type=f32)
                dk[0:keys, :] += jnp.dot(ds, q_h, preferred_element_type=f32)
                part = lax.dot_general(ds, k_h, TN, preferred_element_type=f32)
                dq = part if dq is None else dq + part
            d_ref[0, rows, :] = (dq * scale).astype(bf16)

        @pl.when(n <= i * rows_of)
        def _():
            d_ref[0, rows, :] = jnp.zeros((rows_of, LANES), bf16)

    d_ref[1] = dk[...].astype(bf16)
    d_ref[2] = dv[...].astype(bf16)


def attend_back(frames, qkv, g, lse, at):
    length, pairs = qkv.shape[0], lse.shape[0]
    width = pairs * LANES
    every = qkv.shape[1] // 3 // LANES
    part = lambda c: pl.BlockSpec((length, LANES), lambda j, n: (0, j + at + c * every))
    return pl.pallas_call(
        functools.partial(attend_back_kernel, 256),
        grid_spec=pltpu.PrefetchScalarGridSpec(
            num_scalar_prefetch=1,
            grid=(pairs,),
            in_specs=[
                part(0),
                part(1),
                part(2),
                part(0),
                pl.BlockSpec((1, 2, length), lambda j, n: (j, 0, 0)),
            ],
            out_specs=pl.BlockSpec((3, length, LANES), lambda j, n: (0, 0, j)),
            scratch_shapes=[pltpu.VMEM((length, LANES), f32), pltpu.VMEM((length, LANES), f32)],
        ),
        out_shape=jax.ShapeDtypeStruct((3, length, width), bf16),
        compiler_params=params(),
        cost_estimate=cost(24 * length * length * width, 16 << 20, length * length * 16),
        name="attend_back",
    )(frames, qkv, qkv, qkv, g, lse)


def qkv_grad_kernel(block, tab, u_t_ref, d_ref, sent, kept, grad):
    total = jnp.dot(u_t_ref[...], d_ref[0], preferred_element_type=f32)
    grad[...] = total.astype(bf16)
    relative(sent, kept, slice(None), grad, slice(None), tab, block)


def qkv_grad(tab, u_t, d, block):
    width, length = u_t.shape
    wide = 512
    half = width // 2
    columns = d.shape[2]
    per = columns // wide
    out = pl.BlockSpec((half, wide), lambda j, t: (0, j))
    shape = jax.ShapeDtypeStruct((half, 3 * columns), bf16)
    return pl.pallas_call(
        functools.partial(qkv_grad_kernel, block),
        grid_spec=pltpu.PrefetchScalarGridSpec(
            num_scalar_prefetch=1,
            grid=(3 * per,),
            in_specs=[
                full((width, length), True),
                pl.BlockSpec((1, length, wide), lambda j, t: (j // per, 0, j % per)),
            ],
            out_specs=[out, out],
            scratch_shapes=[pltpu.VMEM((width, wide), bf16)],
        ),
        out_shape=[shape, shape],
        compiler_params=params(),
        cost_estimate=cost(6 * length * width * columns, 14 << 20),
        name="qkv_grad",
    )(tab, u_t, d)


def input_grad_kernel(count, groups, block, tab, dmid_ref, x_ref, gain_ref, *refs):
    d_refs, refs = refs[:groups], refs[groups:]
    weights = refs[:count]
    out_ref, w_nat = refs[count:]
    width = x_ref.shape[1]

    @pl.when(pl.program_id(0) == 0)
    def _():
        natural(w_nat, slice(None), weights, slice(None), tab, block)

    du = None
    for c in range(3):
        w = w_nat[:, c * width : (c + 1) * width]
        d = jnp.concatenate([ref[c] for ref in d_refs], axis=1)
        part = lax.dot_general(d, w, NT, preferred_element_type=f32)
        du = part if du is None else du + part
    out_ref[...] = dmid_ref[...] + norm_back(x_ref[...].astype(f32), gain_ref[0:1, :], du)


def input_grad(tab, d, dmid, x, gains, pieces, block):
    length, width = x.shape
    rows = 256
    row = pl.BlockSpec((rows, width), lambda i, t: (i, 0))
    return pl.pallas_call(
        functools.partial(input_grad_kernel, len(pieces), len(d), block),
        grid_spec=pltpu.PrefetchScalarGridSpec(
            num_scalar_prefetch=1,
            grid=(length // rows,),
            in_specs=[row, row, full((8, width))]
            + [pl.BlockSpec((3, rows, v.shape[2]), lambda i, t: (0, i, 0)) for v in d]
            + [pl.BlockSpec((p.shape[0], 3 * width), lambda i, t: (0, 0), pipeline_mode=pl.Buffered(1)) for p in pieces],
            out_specs=row,
            scratch_shapes=[pltpu.VMEM((width, 3 * width), bf16)],
        ),
        out_shape=jax.ShapeDtypeStruct((length, width), f32),
        compiler_params=params(),
        cost_estimate=cost(6 * length * width * width, 22 << 20),
        name="input_grad",
    )(tab, dmid, x, gains, *d, *pieces)


def adam_step(weight, first, second, gradient, clip_factor, step_rate, decay_rate, shadow):
    clipped = gradient * clip_factor
    first_new = BETA_ONE * first + (1.0 - BETA_ONE) * clipped
    second_new = BETA_TWO * second + (1.0 - BETA_TWO) * clipped * clipped
    first_hat = first_new / (1.0 - BETA_ONE**STEP)
    second_hat = second_new / (1.0 - BETA_TWO**STEP)
    weight_new = weight - step_rate * (
        first_hat / (jnp.sqrt(second_hat) + ADAM_EPS) + decay_rate * weight
    )
    shadow_new = SHADOW_KEEP * shadow + (1.0 - SHADOW_KEEP) * weight_new
    return (weight_new, first_new, second_new, shadow_new)


def body(plan, *args):
    inputs, cotangent, frames = args[:3]
    masters, firsts, seconds, shadows = args[3:8], args[8:13], args[13:18], args[18:23]
    w_qkv, w_out, w_up, w_down, norm_gains = masters
    block, ndev = plan.block, plan.ndev
    x = inputs[0]
    length = x.shape[0]
    own = D // ndev
    subs = FF // D
    per = subs // CHUNKS
    tab = lax.dynamic_index_in_dim(jnp.asarray(plan.tab), lax.axis_index("dp"), 0, keepdims=False)

    gain_cols = jnp.pad(norm_gains.astype(bf16).T, ((0, 0), (0, LANES - 2)))
    local_qkv = jnp.concatenate([w_qkv.astype(bf16), gain_cols], axis=1)
    up_low = w_up.astype(bf16).reshape(own, ndev, subs, own).transpose(2, 0, 1, 3).reshape(subs, own, D)
    down_low = w_down.astype(bf16).reshape(subs, own, D)
    local_mlp = [
        jnp.concatenate(
            [half for q in range(k * per, (k + 1) * per) for half in (up_low[q], down_low[q])], axis=1
        )
        for k in range(CHUNKS)
    ]
    flow = Flow()
    step = flow.step
    reach = lambda v: lax.all_gather(v, "fsdp", axis=0, tiled=True)
    flow.add("q", plan.gather(reach(local_qkv)))
    rest = reach(jnp.concatenate([w_out.astype(bf16)] + local_mlp, axis=1))
    flow.add("o", plan.gather(rest[:, :D]))
    size = 2 * per * D
    for k in range(CHUNKS):
        flow.add(f"m{k}", plan.gather(rest[:, D + k * size : D + (k + 1) * size]))

    x = step(x, ["q"])
    for _ in range(plan.bits - 1):
        x = step(x, ["q"])
    x = step(x, ["q", "o", "m0", "m1"])
    x = flow.until(x, ["q"])
    full_qkv = flow.done["q"]
    qkv, u_one, gains, u_one_t = project_qkv(tab, x, full_qkv, block)
    pairs = D // LANES // GROUPS
    qkv = step(qkv, ["o", "m0"])
    o0, lse0 = attend(frames, qkv, 0, pairs)
    o0, qkv = step((o0, qkv), ["o", "m0", "m1"])
    o1, lse1 = attend(frames, qkv, pairs, pairs)
    o, lse = [o0, o1], [lse0, lse1]
    o = step(o, ["o", "m0", "m1", "m2", "m3"])
    o = flow.until(o, ["o"])
    full_out = flow.done["o"]
    mid, u_two, u_two_t = middle(tab, o, x, gains, full_out, block)
    keep = (jnp.arange(length) < frames[0])[:, None]
    g_low = jnp.where(keep, cotangent[0], jnp.zeros((), bf16))
    held = [mid, None]
    plans = [["m1", "m2"], ["m1", "m2", "m3"], ["m2", "m3", "g0"], ["m3", "g0", "g1"]]
    u_two = step(u_two, ["m0", "m1", "m2"])
    for k in range(CHUNKS):
        u_two = flow.until(u_two, [f"m{k}"])
        out, du, sent, kept = feed_forward(
            tab, u_two, u_two_t, g_low, flow.done[f"m{k}"], held, block, k == 0, k == CHUNKS - 1
        )
        held = [out, du]
        flow.add(f"g{k}", plan.scatter(sent, kept))
        if k == 0:
            held = step(held, ["m1", "m2", "m3", "g0"])
        elif k == 1:
            held = step(held, ["m2", "m3", "g0", "g1"])
        elif k == 2:
            held = step(held, ["m3", "g0", "g1", "g2"])
        elif k == 3:
            held = step(held, ["g0", "g1", "g2", "g3"])
    out, du = held
    dmid, d_o, sent, kept = middle_back(
        tab, frames, du, mid, cotangent[0], gains, o, full_out, block
    )
    flow.add("go", plan.scatter(sent, kept))
    d_o = step(d_o, ["g1", "g2", "g3", "go"])
    d0 = attend_back(frames, qkv, d_o, lse[0], 0)
    d0 = step(d0, ["g2", "g3", "go"])
    sent, kept = qkv_grad(tab, u_one_t, d0, block)
    flow.add("gq0", plan.scatter(sent, kept))
    kept, qkv = step((kept, qkv), ["gq0", "g3", "go"])
    d1 = attend_back(frames, qkv, d_o, lse[1], pairs)
    d1 = step(d1, ["gq0", "go"])
    sent, kept = qkv_grad(tab, u_one_t, d1, block)
    flow.add("gq1", plan.scatter(sent, kept))
    kept, d = step((kept, [d0, d1]), ["gq0", "gq1"])
    grad_in = input_grad(tab, d, dmid, x, gains, full_qkv, block)
    grad_in = step(grad_in, ["gq0", "gq1"])
    grad_in = flow.until(grad_in, list(flow.live))
    own_rows = lambda n: lax.psum_scatter(flow.done[n], "fsdp", scatter_dimension=0, tiled=True)
    mlp_shards = [own_rows(f"g{k}") for k in range(CHUNKS)]
    out_shard = own_rows("go")
    parts = [own_rows("gq0"), own_rows("gq1")]
    wide = pairs * LANES
    qkv_shard = jnp.concatenate(
        [v[:, c * wide : (c + 1) * wide] for c in range(3) for v in parts], axis=1
    )

    ups, downs = [], []
    for k in range(CHUNKS):
        for i in range(per):
            at = 2 * i * D
            ups.append(mlp_shards[k][:, at : at + D])
            downs.append(mlp_shards[k][:, at + D : at + 2 * D])
    up_shard = (
        jnp.stack(ups).reshape(subs, own, ndev, own).transpose(1, 2, 0, 3).reshape(own, FF)
    )
    down_shard = jnp.concatenate(downs, axis=0)
    gain_low = norm_gains.astype(bf16).astype(f32)
    one = jnp.sum(w_qkv.astype(bf16).astype(f32) * qkv_shard, axis=1)
    two = jnp.sum(w_up.astype(bf16).astype(f32) * up_shard, axis=1)
    gain_shard = jnp.stack([one, two]) / gain_low
    shards = (qkv_shard, out_shard, up_shard, down_shard, gain_shard)
    local_sq = sum(jnp.sum(piece * piece) for piece in shards)
    everyone = lax.all_to_all(jnp.broadcast_to(local_sq, (ndev, 1, LANES)), AXES, 0, 0)
    grad_norm = jnp.sqrt(jnp.sum(everyone[:, 0, 0]))
    clip_factor = jnp.minimum(1.0, CLIP_NORM / grad_norm)
    rates = (0.6 / D**0.5, 0.6 / FANO**0.5, 0.6 / D**0.5, 0.6 / FF**0.5, 1.0)
    decays = (0.1, 0.1, 0.1, 0.1, 0.0)
    updated = [
        adam_step(
            masters[i], firsts[i], seconds[i], shards[i], clip_factor, rates[i], decays[i], shadows[i]
        )
        for i in range(5)
    ]
    return (
        out[None],
        grad_in[None],
        grad_norm,
        *(updated[i][part] for part in range(4) for i in range(5)),
    )


def solution(mesh):
    plan = Plan(mesh)
    split = P(AXES, None)
    lanes = P(None, AXES)
    weights = (split, split, split, split, lanes)
    return jax.shard_map(
        functools.partial(body, plan),
        mesh=mesh,
        in_specs=(P(AXES, None, None), P(AXES, None, None), P(AXES)) + weights * 4,
        out_specs=(P(AXES, None, None), P(AXES, None, None), P()) + weights * 4,
        check_vma=False,
    )
```

```python
import functools

import jax
import jax.numpy as jnp
import numpy as np
from jax import lax
from jax.experimental import pallas as pl
from jax.experimental.pallas import tpu as pltpu
from jax.sharding import PartitionSpec as P

D = 1024
HEAD_DIM = 64
FF = 4096
STEP = 7
FANO = 16

NORM_EPS = 1e-06
ADAM_EPS = 1e-08
BETA_ONE = 0.9
BETA_TWO = 0.95
SHADOW_KEEP = 0.8
CLIP_NORM = 1.0

AXES = ("dp", "fsdp")
GROUPS = 2
LANES = 128
VMEM = 62 << 20
f32 = jnp.float32
bf16 = jnp.bfloat16
NT = (((1,), (1,)), ((), ()))
TN = (((0,), (0,)), ((), ()))
GELU_A = 0.7978845608028654
GELU_B = 0.044715


def full(shape, single=False):
    rank = len(shape)
    mode = dict(pipeline_mode=pl.Buffered(1)) if single else {}
    return pl.BlockSpec(shape, lambda *_: (0,) * rank, **mode)


def params():
    return pltpu.CompilerParams(vmem_limit_bytes=VMEM)


def cost(flops, nbytes, trans=0):
    return pl.CostEstimate(flops=flops, bytes_accessed=nbytes, transcendentals=trans)


class Plan:
    def __init__(self, mesh):
        self.ndp, self.nfs = mesh.shape["dp"], mesh.shape["fsdp"]
        self.ndev = self.ndp * self.nfs
        self.bits = self.ndp.bit_length() - 1
        others = list(range(1, self.bits))
        half = len(others) // 2
        self.order = (others, others[half:] + others[:half])
        self.block = D // self.ndp
        tab = np.zeros((self.ndp, self.ndp), np.int32)
        for me in range(self.ndp):
            for rel in range(self.ndp):
                core = (me & 1) ^ (rel >> (self.bits - 1))
                nat = core
                for s, bit in enumerate(self.order[core]):
                    r = (rel >> (self.bits - 2 - s)) & 1
                    nat |= (((me >> bit) & 1) ^ r) << bit
                tab[me, rel] = nat
        self.tab = tab

    def pairs(self, flip):
        out = []
        for d in range(self.ndp):
            for f in range(self.nfs):
                out.append((d * self.nfs + f, flip(d) * self.nfs + f))
        return out

    def core_pairs(self):
        return self.pairs(lambda d: d ^ 1)

    def mix_pairs(self, s):
        return self.pairs(lambda d: d ^ (1 << self.order[d & 1][s]))

    def gather(self, mine):
        for s in reversed(range(self.bits - 1)):
            wide = s == 0
            (got,) = yield [mine], self.mix_pairs(s), None if wide else ("join", mine)
            mine = mine if wide else got
        held = [mine, got]
        return held + (yield held, self.core_pairs(), None)

    def scatter(self, sent, kept):
        pairs = self.core_pairs()
        for s in range(self.bits - 1):
            kept, sent = yield [sent], pairs, ("sum", [kept], [bf16, bf16])
            pairs = self.mix_pairs(s)
        (total,) = yield [sent], pairs, ("sum", [kept], [bf16])
        return total

    def scatter_direct(self, sent, kept):
        count = self.ndp // 2
        kept, *sent = yield [sent], self.core_pairs(), ("sum", [kept], [f32] + [bf16] * (count - 1))
        pairs = [None] + [
            self.pairs(lambda d: d ^ self.mask(d & 1, rel)) for rel in range(1, count)
        ]
        (total,) = yield sent, pairs[1:], ("sum", [kept], [f32])
        return total

    def mask(self, core, rel):
        bits = enumerate(self.order[core])
        return sum(((rel >> (self.bits - 2 - s)) & 1) << bit for s, bit in bits)

    def own_rows(self, total, direct=False):
        if not direct or self.nfs > 4:
            return lax.psum_scatter(total, "fsdp", scatter_dimension=0, tiled=True).astype(f32)
        me, rows = lax.axis_index("fsdp"), total.shape[0] // self.nfs
        block = lambda f: lax.dynamic_slice_in_dim(total, f * rows, rows, 0)
        sum_ = block(me)
        for flip in range(1, self.nfs):
            pairs = [(i, i // self.nfs * self.nfs + (i % self.nfs ^ flip)) for i in range(self.ndev)]
            sum_ = sum_ + lax.ppermute(block(me ^ flip), AXES, pairs)
        return sum_


def tie_kernel(count, jobs, *refs):
    sems = refs[-1]
    free = iter(range(sems.shape[0]))
    copy = lambda x, y: pltpu.make_async_copy(x, y, sems.at[next(free)])
    total = count + sum(job["inputs"] for job in jobs)
    made = sum(len(job["outputs"]) for job in jobs)
    inputs, outputs = list(refs[count:total]), list(refs[total + count : total + count + made])
    scratch = list(refs[total + count + made : -1])
    steps = []
    for job in jobs:
        ins = [inputs.pop(0) for _ in range(job["inputs"])]
        outs = [outputs.pop(0) for _ in job["outputs"]]
        if job["kind"] == "cut":
            at, wide = job["cut"]
            held = scratch.pop(0)
            steps.append(([copy(ins[0].at[:, pl.ds(at, wide)], held)], None, copy(held, outs[0])))
        elif job["kind"] == "join":
            held = scratch.pop(0)
            rows = ins[0].shape[0]
            loads = [copy(v, held.at[pl.ds(i * rows, rows)]) for i, v in enumerate(ins)]
            steps.append((loads, None, copy(held, outs[0])))
        else:
            rows = outs[0].shape[0]
            for i, out in reversed(list(enumerate(outs))):
                held = [scratch.pop(0) for _ in range(len(ins) + 1)]
                loads = [copy(v.at[pl.ds(i * rows, rows)], h) for v, h in zip(ins, held)]
                steps.append((loads, held, copy(held[-1], out)))
    for loads, _, _ in steps:
        for c in loads:
            c.start()
    for loads, held, save in steps:
        for c in loads:
            c.wait()
        if held:
            total = held[0][...].astype(f32)
            for h in held[1:-1]:
                total = total + h[...].astype(f32)
            held[-1][...] = total.astype(held[-1].dtype)
        save.start()
    for _, _, save in steps:
        save.wait()


def tie(same, work=()):
    leaves, form = jax.tree.flatten(same)
    place = pl.BlockSpec(memory_space=pl.ANY)
    count = len(leaves)
    jobs, inputs, made, scratch, copies = [], list(leaves), [], [], 1
    shape = lambda dims, kind: jax.ShapeDtypeStruct(dims, kind)
    for kind, *rest in work:
        if kind == "cut":
            v, at, wide = rest
            arrays, outs = [v], [shape((v.shape[0], wide), v.dtype)]
            scratch.append(outs[0])
            copies += 2
        elif kind == "join":
            arrays = rest
            outs = [shape((2 * rest[0].shape[0], rest[0].shape[1]), rest[0].dtype)]
            scratch.append(outs[0])
            copies += 3
        else:
            arrays, kinds = rest
            rows = arrays[0].shape[0] // len(kinds)
            outs = [shape((rows, arrays[0].shape[1]), k) for k in kinds]
            for out in reversed(outs):
                scratch += [shape(out.shape, v.dtype) for v in arrays] + [out]
            copies += (len(arrays) + 1) * len(outs)
        inputs += arrays
        made.append(outs)
        jobs.append(dict(kind=kind, inputs=len(arrays), outputs=outs, cut=tuple(rest[1:3]) if kind == "cut" else None))
    if not inputs:
        return same, []
    outputs = [shape(v.shape, v.dtype) for v in leaves] + [v for outs in made for v in outs]
    out = list(
        pl.pallas_call(
            functools.partial(tie_kernel, count, jobs),
            in_specs=[place] * len(inputs),
            out_specs=[place] * len(outputs),
            out_shape=outputs,
            scratch_shapes=[pltpu.VMEM(v.shape, v.dtype) for v in scratch]
            + [pltpu.SemaphoreType.DMA((copies,))],
            input_output_aliases={i: i for i in range(count)},
            compiler_params=params(),
            name="tie",
        )(*inputs)
    )
    same, out = jax.tree.unflatten(form, out[:count]), out[count:]
    return same, [[out.pop(0) for _ in outs] for outs in made]


class Flow:
    def __init__(self, plan):
        self.plan = plan
        self.live, self.flying, self.done, self.waiting = {}, {}, {}, {}

    def gather(self, name, array, at=None, wide=None):
        self.waiting[name] = (array, at, wide)

    def scatter(self, name, sent, kept, direct=False):
        way = self.plan.scatter_direct if direct else self.plan.scatter
        self.live[name] = way(sent, kept)

    def step(self, x, names):
        names = [n for n in names if n not in self.done]
        came = {n: self.flying.pop(n) for n in names if n in self.flying}
        start = {n: self.waiting.pop(n) for n in names if n in self.waiting}
        plain = {n: got for n, (got, merge) in came.items() if merge is None}
        whole = {n: v for n, (v, at, _) in start.items() if at is None}
        work = {}
        for n, (got, merge) in came.items():
            if merge and merge[0] == "join":
                work[n] = ("join", merge[1], *got)
            elif merge:
                work[n] = ("sum", merge[1] + got, merge[2])
        work |= {n: ("cut", *v) for n, v in start.items() if v[1] is not None}
        (x, plain, whole), made = tie((x, plain, whole), list(work.values()))
        made = dict(zip(work, made))
        for n in start:
            self.live[n] = self.plan.gather(whole[n] if n in whole else made[n][0])
        for n in names:
            value = None if n in start else plain.get(n, made.get(n))
            try:
                sent, pairs, merge = self.live[n].send(value)
                each = pairs if isinstance(pairs[0], list) else [pairs] * len(sent)
                self.flying[n] = ([lax.ppermute(v, AXES, p) for v, p in zip(sent, each)], merge)
            except StopIteration as stop:
                self.done[n] = stop.value
        return x

    def until(self, x, names):
        while any(n not in self.done for n in names):
            x = self.step(x, names)
        return x


def natural(dst, cols, pieces, src_cols, tab, block):
    j = 0
    for piece in pieces:
        for i in range(piece.shape[0] // block):
            row = pl.multiple_of(tab[j] * block, block)
            dst[pl.ds(row, block), cols] = piece[i * block : (i + 1) * block, src_cols]
            j += 1


def relative(sent, kept, cols, src, src_cols, tab, block):
    half = src.shape[0] // block // 2
    for j in range(2 * half):
        row = pl.multiple_of(tab[j] * block, block)
        out = kept if j < half else sent
        i = j % half
        out[i * block : (i + 1) * block, cols] = src[pl.ds(row, block), src_cols]


def qkv_kernel(count, block, first, tab, *refs):
    if first:
        x_ref, refs = refs[0], refs[1:]
        gains, weights = refs[:count], refs[count : 2 * count]
        qkv_ref, u_ref, gain_ref, u_t_ref, w_nat, g_nat = refs[2 * count :]

        @pl.when(pl.program_id(0) == 0)
        def _():
            natural(g_nat, slice(None), gains, slice(None), tab, block)
            rows = g_nat[...].astype(f32).T
            gain_ref[...] = rows[:8]
            x = x_ref[...].astype(f32)
            r = lax.rsqrt(jnp.mean(x * x, axis=1, keepdims=True) + NORM_EPS)
            u = (x * r * rows[0:1]).astype(bf16)
            u_ref[...] = u
            u_t_ref[...] = u.T

    else:
        u_ref, weights, (qkv_ref, w_nat) = refs[0], refs[1 : 1 + count], refs[1 + count :]
    natural(w_nat, slice(None), weights, slice(None), tab, block)
    qkv_ref[...] = jnp.dot(u_ref[...], w_nat[...], preferred_element_type=f32).astype(bf16)


def project_qkv(tab, x, pieces, block, columns, first):
    length, width = x.shape
    wide = 512
    last = columns // LANES
    col = pl.BlockSpec((length, wide), lambda j, t: (0, j))
    extra = first * [full((length, width)), full((8, width)), full((width, length))]
    shapes = first * [
        jax.ShapeDtypeStruct((length, width), bf16),
        jax.ShapeDtypeStruct((8, width), f32),
        jax.ShapeDtypeStruct((width, length), bf16),
    ]
    gains = first * [pl.BlockSpec((p.shape[0], LANES), lambda j, t: (0, last)) for p in pieces]
    return pl.pallas_call(
        functools.partial(qkv_kernel, len(pieces), block, first),
        grid_spec=pltpu.PrefetchScalarGridSpec(
            num_scalar_prefetch=1,
            grid=(columns // wide,),
            in_specs=[full((length, width), True)]
            + gains
            + [pl.BlockSpec((p.shape[0], wide), lambda j, t: (0, j)) for p in pieces],
            out_specs=[col] + extra,
            scratch_shapes=[pltpu.VMEM((width, wide), bf16)]
            + first * [pltpu.VMEM((width, LANES), bf16)],
        ),
        out_shape=[jax.ShapeDtypeStruct((length, columns), bf16)] + shapes,
        compiler_params=params(),
        cost_estimate=cost(2 * length * width * columns, 20 << 20),
        name="qkv",
    )(tab, x, *(first * pieces), *pieces)


def fold(v, op):
    v = v.reshape(v.shape[0] // 64, 64, v.shape[1])
    return op(op(v, axis=0), axis=0, keepdims=True)


def attend_kernel(rows_of, n_ref, q_ref, k_ref, v_ref, o_ref, lse_ref):
    n = n_ref[0]
    length = q_ref.shape[0]
    lane = lax.broadcasted_iota(jnp.int32, (1, LANES), 1)
    masks = [(lane < HEAD_DIM).astype(bf16), (lane >= HEAD_DIM).astype(bf16)]
    v_t = v_ref[...].T
    for i in range(length // rows_of):
        rows = pl.ds(i * rows_of, rows_of)
        keys = (i + 1) * rows_of

        def run(limited):
            q = q_ref[rows, :] * bf16(HEAD_DIM**-0.5)
            k = k_ref[0:keys, :]
            parts = []
            for h in range(2):
                s = lax.dot_general(k, q * masks[h], NT, preferred_element_type=f32)
                if limited:
                    key = lax.broadcasted_iota(jnp.int32, (keys, rows_of), 0)
                    query = lax.broadcasted_iota(jnp.int32, (keys, rows_of), 1) + i * rows_of
                    s = jnp.where((key <= query) & (key < n), s, -1e30)
                else:
                    key = lax.broadcasted_iota(jnp.int32, (rows_of, rows_of), 0)
                    query = lax.broadcasted_iota(jnp.int32, (rows_of, rows_of), 1)
                    tail = jnp.where(key <= query, s[keys - rows_of :], -1e30)
                    s = tail if i == 0 else jnp.concatenate([s[: keys - rows_of], tail], axis=0)
                peak = fold(s, jnp.max)
                e = jnp.exp(s - peak)
                total = fold(e, jnp.sum)
                p = (e * (1.0 / total)).astype(bf16)
                v_h = v_t[h * HEAD_DIM : (h + 1) * HEAD_DIM, 0:keys]
                parts.append(jnp.dot(v_h, p, preferred_element_type=f32))
                query = lax.broadcasted_iota(jnp.int32, (1, rows_of), 1) + i * rows_of
                lse_ref[0, h : h + 1, rows] = jnp.where(query < n, peak + jnp.log(total), 1e30)
            o_ref[rows, :] = jnp.concatenate(parts, axis=0).astype(bf16).T

        @pl.when(n >= keys)
        def _():
            run(False)

        @pl.when(n < keys)
        def _():
            run(True)


def attend(frames, qkv):
    length, width = qkv.shape[0], qkv.shape[1] // 3
    pairs = width // LANES
    part = lambda c: pl.BlockSpec((length, LANES), lambda j, n: (0, 3 * j + c))
    return pl.pallas_call(
        functools.partial(attend_kernel, 512),
        grid_spec=pltpu.PrefetchScalarGridSpec(
            num_scalar_prefetch=1,
            grid=(pairs,),
            in_specs=[part(0), part(1), part(2)],
            out_specs=[
                pl.BlockSpec((length, LANES), lambda j, n: (0, j)),
                pl.BlockSpec((1, 2, length), lambda j, n: (j, 0, 0)),
            ],
        ),
        out_shape=[
            jax.ShapeDtypeStruct((length, width), bf16),
            jax.ShapeDtypeStruct((pairs, 2, length), f32),
        ],
        compiler_params=params(),
        cost_estimate=cost(16 * length * length * width, 8 << 20, length * length * 16),
        name="attend",
    )(frames, qkv, qkv, qkv)


def mid_kernel(count, groups, block, tab, x_ref, gain_ref, *refs):
    o_refs, refs = refs[:groups], refs[groups:]
    weights = refs[:count]
    mid_ref, u_ref, u_t_ref, w_nat = refs[count:]

    @pl.when(pl.program_id(0) == 0)
    def _():
        natural(w_nat, slice(None), weights, slice(None), tab, block)

    o = jnp.concatenate([ref[...] for ref in o_refs], axis=1)
    mid = x_ref[...].astype(f32) + jnp.dot(o, w_nat[...], preferred_element_type=f32)
    r = lax.rsqrt(jnp.mean(mid * mid, axis=1, keepdims=True) + NORM_EPS)
    u = (mid * r * gain_ref[1:2, :]).astype(bf16)
    mid_ref[...] = mid
    u_ref[...] = u
    u_t_ref[...] = u.T


def middle(tab, o, x, gains, pieces, block):
    length, width = x.shape
    rows = 256
    row = pl.BlockSpec((rows, width), lambda i, t: (i, 0))
    return pl.pallas_call(
        functools.partial(mid_kernel, len(pieces), len(o), block),
        grid_spec=pltpu.PrefetchScalarGridSpec(
            num_scalar_prefetch=1,
            grid=(length // rows,),
            in_specs=[row, full((8, width))]
            + [pl.BlockSpec((rows, v.shape[1]), lambda i, t: (i, 0)) for v in o]
            + [full(p.shape) for p in pieces],
            out_specs=[row, row, pl.BlockSpec((width, rows), lambda i, t: (0, i))],
            scratch_shapes=[pltpu.VMEM((width, width), bf16)],
        ),
        out_shape=[
            jax.ShapeDtypeStruct((length, width), f32),
            jax.ShapeDtypeStruct((length, width), bf16),
            jax.ShapeDtypeStruct((width, length), bf16),
        ],
        compiler_params=params(),
        cost_estimate=cost(2 * length * width * width, 16 << 20),
        name="middle",
    )(tab, x, gains, *o, *pieces)


def gelu_both(z):
    sq = z * z
    t = jnp.tanh(z * (GELU_A + (GELU_A * GELU_B) * sq))
    half = 0.5 + 0.5 * t
    slope = half + (0.5 * z) * (1.0 - t * t) * (GELU_A + (3 * GELU_A * GELU_B) * sq)
    return z * half, slope


def mlp_kernel(count, block, sub, first, last, tab, *refs):
    u_hbm, u_t_hbm, g_hbm = refs[:3]
    pieces, refs = refs[3 : 3 + count], refs[3 + count :]
    held_out, refs = refs[0], refs[1:]
    if not first:
        held_du, refs = refs[0], refs[1:]
    out_hbm, du_hbm, sent, kept = refs[:4]
    u, u_t, g, up, down, out_acc, du_acc, a_s, dz_s, grad, low, sems = refs[4:]
    width = u.shape[1]
    wide = 512
    halves = width // wide
    blocks = width // block
    base = 2 * sub * width
    free = iter(range(sems.shape[0]))

    def copy(src, dst):
        return pltpu.make_async_copy(src, dst, sems.at[next(free)])

    def rows(at, columns, dst, dst_columns):
        out, j = [], 0
        for piece in pieces:
            for i in range(piece.shape[0] // block):
                row = pl.multiple_of(tab[j] * block, block)
                src = piece.at[pl.ds(i * block, block), pl.ds(at, columns)]
                out.append(copy(src, dst.at[pl.ds(row, block), dst_columns]))
                j += 1
        return out

    get_u = [copy(u_hbm, u)]
    get_up = [rows(base + f * wide, wide, up, pl.ds(f * wide, wide)) for f in range(halves)]
    get_g = [copy(g_hbm, g)]
    get_down = rows(base + width, width, down, pl.ds(0, width))
    get_acc = [copy(held_out, out_acc)] + ([] if first else [copy(held_du, du_acc)])
    get_t = [copy(u_t_hbm, u_t)]

    def start(copies):
        for c in copies:
            c.start()

    def wait(copies):
        for c in copies:
            c.wait()

    start(get_u + get_up[0] + get_g + get_down + get_t)
    for f in range(1, halves):
        start(get_up[f])
    start(get_acc)
    for f in range(halves):
        cols = slice(f * wide, (f + 1) * wide)
        wait((get_u if f == 0 else []) + get_up[f])
        z = jnp.dot(u[...], up[:, cols], preferred_element_type=f32)
        a, slope = gelu_both(z)
        if f == 0:
            wait(get_g + get_down)
        da = lax.dot_general(g[...], down[cols, :], NT, preferred_element_type=f32)
        a_s[:, cols] = a.astype(bf16)
        dz_s[:, cols] = (da * slope).astype(bf16)
        if f == 0:
            wait(get_t)
        grad[:, cols] = jnp.dot(u_t[...], dz_s[:, cols], preferred_element_type=f32).astype(bf16)
        turned = lax.dot_general(a_s[:, cols], g[...], TN, preferred_element_type=f32)
        grad[cols, width:] = turned.astype(bf16)
    saved = []
    for j in range(blocks):
        row = pl.multiple_of(tab[j] * block, block)
        out = kept if j < blocks // 2 else sent
        at = j % (blocks // 2) * block
        saved.append(copy(grad.at[pl.ds(row, block)], out.at[pl.ds(at, block)]))
    start(saved)
    wait(get_acc)
    half = u.shape[0] // 2
    for i in range(2):
        part = pl.ds(i * half, half)
        out = out_acc[part, :] + jnp.dot(a_s[part, :], down[...], preferred_element_type=f32)
        if last:
            low[part, :] = out.astype(bf16)
            saved.append(copy(low.at[part], out_hbm.at[part]))
        else:
            out_acc[part, :] = out
            saved.append(copy(out_acc.at[part], out_hbm.at[part]))
        saved[-1].start()
    for i in range(2):
        part = pl.ds(i * half, half)
        du = lax.dot_general(dz_s[part, :], up[...], NT, preferred_element_type=f32)
        du_acc[part, :] = du if first else du_acc[part, :] + du
        saved.append(copy(du_acc.at[part], du_hbm.at[part]))
        saved[-1].start()
    wait(saved)


def feed_forward(tab, u, u_t, g, pieces, sub, held, block, first, last):
    length, width = u.shape
    half = width // 2
    anywhere = pl.BlockSpec(memory_space=pl.ANY)
    held = held[:1] if first else held
    inputs = [u, u_t, g, *pieces, *held]
    alias = {}
    if not first:
        alias[len(inputs)] = 1
        if not last:
            alias[len(inputs) - 1] = 0
    acc = jax.ShapeDtypeStruct((length, width), f32)
    part = jax.ShapeDtypeStruct((half, 2 * width), bf16)
    blocks = width // block
    return pl.pallas_call(
        functools.partial(mlp_kernel, len(pieces), block, sub, first, last),
        grid_spec=pltpu.PrefetchScalarGridSpec(
            num_scalar_prefetch=1,
            grid=(1,),
            in_specs=[anywhere] * len(inputs),
            out_specs=[anywhere] * 4,
            scratch_shapes=[
                pltpu.VMEM((length, width), bf16),
                pltpu.VMEM((width, length), bf16),
                pltpu.VMEM((length, width), bf16),
                pltpu.VMEM((width, width), bf16),
                pltpu.VMEM((width, width), bf16),
                pltpu.VMEM((length, width), f32),
                pltpu.VMEM((length, width), f32),
                pltpu.VMEM((length, width), bf16),
                pltpu.VMEM((length, width), bf16),
                pltpu.VMEM((width, 2 * width), bf16),
                pltpu.VMEM((length, width) if last else (16, LANES), bf16),
                pltpu.SemaphoreType.DMA((4 * blocks + 12,)),
            ],
        ),
        out_shape=[jax.ShapeDtypeStruct((length, width), bf16) if last else acc, acc, part, part],
        input_output_aliases=alias,
        compiler_params=params(),
        cost_estimate=cost(12 * length * width * width, 24 << 20),
        name="feed_forward",
    )(tab, *inputs)


def norm_back(v, gain, du):
    r = lax.rsqrt(jnp.mean(v * v, axis=1, keepdims=True) + NORM_EPS)
    up = du * gain
    return r * up - v * (r * r * r * jnp.mean(up * v, axis=1, keepdims=True))


def dmid_kernel(count, groups, block, steps, tab, n_ref, du_ref, mid_ref, cot_ref, gain_ref, *refs):
    o_refs, refs = refs[:groups], refs[groups:]
    weights = refs[:count]
    dmid_ref, do_ref, sent, kept, w_nat, total, grad = refs[count:]
    i = pl.program_id(0)
    rows = du_ref.shape[0]

    @pl.when(i == 0)
    def _():
        natural(w_nat, slice(None), weights, slice(None), tab, block)

    frame = lax.broadcasted_iota(jnp.int32, (rows, 1), 0) + i * rows
    g = jnp.where(frame < n_ref[0], cot_ref[...].astype(f32), 0.0)
    dmid = g + norm_back(mid_ref[...], gain_ref[1:2, :], du_ref[...])
    dmid_ref[...] = dmid
    low = dmid.astype(bf16)
    do_ref[...] = lax.dot_general(low, w_nat[...], NT, preferred_element_type=f32).astype(bf16)
    o = jnp.concatenate([ref[...] for ref in o_refs], axis=1)
    part = lax.dot_general(o, low, TN, preferred_element_type=f32)

    @pl.when(i == 0)
    def _():
        total[...] = part

    @pl.when(i > 0)
    def _():
        total[...] += part

    @pl.when(i == steps - 1)
    def _():
        grad[...] = total[...].astype(bf16)
        relative(sent, kept, slice(None), grad, slice(None), tab, block)


def middle_back(tab, frames, du, mid, cot, gains, o, pieces, block):
    length, width = mid.shape
    rows = 256
    steps = length // rows
    row = pl.BlockSpec((rows, width), lambda i, t, n: (i, 0))
    half = width // 2
    return pl.pallas_call(
        functools.partial(dmid_kernel, len(pieces), len(o), block, steps),
        grid_spec=pltpu.PrefetchScalarGridSpec(
            num_scalar_prefetch=2,
            grid=(steps,),
            in_specs=[row, row, row, full((8, width))]
            + [pl.BlockSpec((rows, v.shape[1]), lambda i, t, n: (i, 0)) for v in o]
            + [full(p.shape) for p in pieces],
            out_specs=[row, row, full((half, width)), full((half, width))],
            scratch_shapes=[
                pltpu.VMEM((width, width), bf16),
                pltpu.VMEM((width, width), f32),
                pltpu.VMEM((width, width), bf16),
            ],
        ),
        out_shape=[
            jax.ShapeDtypeStruct((length, width), f32),
            jax.ShapeDtypeStruct((length, width), bf16),
            jax.ShapeDtypeStruct((half, width), bf16),
            jax.ShapeDtypeStruct((half, width), bf16),
        ],
        compiler_params=params(),
        cost_estimate=cost(4 * length * width * width, 24 << 20),
        name="middle_back",
    )(tab, frames, du, mid, cot, gains, *o, *pieces)


def attend_back_kernel(
    rows_of, block, n_ref, tab, q_ref, k_ref, v_ref, g_ref, lse_ref, u_t_ref, d_ref, sent, kept, dk, dv, d_s, grad
):
    n = n_ref[0]
    length = q_ref.shape[0]
    scale = HEAD_DIM**-0.5
    lane = lax.broadcasted_iota(jnp.int32, (1, LANES), 1)
    masks = [(lane < HEAD_DIM).astype(bf16), (lane >= HEAD_DIM).astype(bf16)]
    dk[...] = jnp.zeros_like(dk)
    dv[...] = jnp.zeros_like(dv)
    for i in range(length // rows_of):
        rows = pl.ds(i * rows_of, rows_of)
        keys = (i + 1) * rows_of

        @pl.when(n > i * rows_of)
        def _():
            q = q_ref[rows, :] * bf16(scale)
            g = g_ref[rows, :]
            k, v = k_ref[0:keys, :], v_ref[0:keys, :]
            dq = None
            for h in range(2):
                q_h, g_h, k_h = q * masks[h], g * masks[h], k * masks[h]
                s = lax.dot_general(k, q_h, NT, preferred_element_type=f32)
                key = lax.broadcasted_iota(jnp.int32, (rows_of, rows_of), 0)
                query = lax.broadcasted_iota(jnp.int32, (rows_of, rows_of), 1)
                tail = jnp.where(key <= query, s[keys - rows_of :], -1e30)
                s = tail if i == 0 else jnp.concatenate([s[: keys - rows_of], tail], axis=0)
                p = jnp.exp(s - lse_ref[0, h : h + 1, rows])
                dp = lax.dot_general(v, g_h, NT, preferred_element_type=f32)
                delta = fold(p * dp, jnp.sum)
                ds = (p * (dp - delta)).astype(bf16)
                dv[0:keys, :] += jnp.dot(p.astype(bf16), g_h, preferred_element_type=f32)
                dk[0:keys, :] += jnp.dot(ds, q_h, preferred_element_type=f32)
                part = lax.dot_general(ds, k_h, TN, preferred_element_type=f32)
                dq = part if dq is None else dq + part
            d_s[rows, 0:LANES] = (dq * scale).astype(bf16)

        @pl.when(n <= i * rows_of)
        def _():
            d_s[rows, 0:LANES] = jnp.zeros((rows_of, LANES), bf16)

    d_s[:, LANES : 2 * LANES] = dk[...].astype(bf16)
    d_s[:, 2 * LANES :] = dv[...].astype(bf16)
    d_ref[...] = d_s[...]
    grad[...] = jnp.dot(u_t_ref[...], d_s[...], preferred_element_type=f32)
    relative(sent, kept, slice(None), grad, slice(None), tab, block)


def attend_back(frames, tab, qkv, g, lse, u_t, first, at, pairs, block):
    length, width = qkv.shape[0], u_t.shape[0]
    wide = 3 * LANES
    part = lambda c: pl.BlockSpec((length, LANES), lambda j, n, t: (0, 3 * (j + at) + c))
    half = width // 2
    out = pl.BlockSpec((half, wide), lambda j, n, t: (0, j))
    shape = jax.ShapeDtypeStruct((half, pairs * wide), f32)
    return pl.pallas_call(
        functools.partial(attend_back_kernel, 256, block),
        grid_spec=pltpu.PrefetchScalarGridSpec(
            num_scalar_prefetch=2,
            grid=(pairs,),
            in_specs=[
                part(0),
                part(1),
                part(2),
                pl.BlockSpec((length, LANES), lambda j, n, t: (0, j + first)),
                pl.BlockSpec((1, 2, length), lambda j, n, t: (j + at, 0, 0)),
                full((width, length), True),
            ],
            out_specs=[pl.BlockSpec((length, wide), lambda j, n, t: (0, j)), out, out],
            scratch_shapes=[
                pltpu.VMEM((length, LANES), f32),
                pltpu.VMEM((length, LANES), f32),
                pltpu.VMEM((length, wide), bf16),
                pltpu.VMEM((width, wide), f32),
            ],
        ),
        out_shape=[jax.ShapeDtypeStruct((length, pairs * wide), bf16), shape, shape],
        compiler_params=params(),
        cost_estimate=cost(40 * length * length * pairs * LANES, 16 << 20, length * length * 2 * pairs),
        name="attend_back",
    )(frames, tab, qkv, qkv, qkv, g, lse, u_t)


def input_grad_kernel(groups, parts, block, tab, dmid_ref, x_ref, gain_ref, *refs):
    d_refs, refs = refs[:parts], refs[parts:]
    weights, out_ref, nats = refs[: -1 - groups], refs[-1 - groups], refs[-groups:]
    count = len(weights) // groups

    @pl.when(pl.program_id(0) == 0)
    def _():
        for i, nat in enumerate(nats):
            natural(nat, slice(None), weights[i * count : (i + 1) * count], slice(None), tab, block)

    du = None
    for i, nat in enumerate(nats):
        mine = d_refs[i * parts // groups : (i + 1) * parts // groups]
        d = jnp.concatenate([ref[...] for ref in mine], axis=1)
        part = lax.dot_general(d, nat[...], NT, preferred_element_type=f32)
        du = part if du is None else du + part
    out_ref[...] = dmid_ref[...] + norm_back(x_ref[...].astype(f32), gain_ref[0:1, :], du)


def input_grad(tab, d, dmid, x, gains, pieces, block, lo, hi):
    length, width = x.shape
    rows = 256
    groups = len(pieces)
    columns = 3 * width // groups
    row = lambda w: pl.BlockSpec((rows, w), lambda i, t: (i + lo, 0))
    weights = [
        pl.BlockSpec((p.shape[0], columns), lambda i, t: (0, 0), pipeline_mode=pl.Buffered(1))
        for group in pieces
        for p in group
    ]
    return pl.pallas_call(
        functools.partial(input_grad_kernel, groups, len(d), block),
        grid_spec=pltpu.PrefetchScalarGridSpec(
            num_scalar_prefetch=1,
            grid=(hi - lo,),
            in_specs=[row(width), row(width), full((8, width))] + [row(v.shape[1]) for v in d] + weights,
            out_specs=pl.BlockSpec((rows, width), lambda i, t: (i, 0)),
            scratch_shapes=[pltpu.VMEM((width, columns), bf16)] * groups,
        ),
        out_shape=jax.ShapeDtypeStruct(((hi - lo) * rows, width), f32),
        compiler_params=params(),
        cost_estimate=cost(6 * length * width * width * (hi - lo) // 4, 22 << 20),
        name="input_grad",
    )(tab, dmid, x, gains, *d, *[p for group in pieces for p in group])


def adam_step(weight, first, second, gradient, clip_factor, step_rate, decay_rate, shadow):
    clipped = gradient * clip_factor
    first_new = BETA_ONE * first + (1.0 - BETA_ONE) * clipped
    second_new = BETA_TWO * second + (1.0 - BETA_TWO) * clipped * clipped
    first_hat = first_new / (1.0 - BETA_ONE**STEP)
    second_hat = second_new / (1.0 - BETA_TWO**STEP)
    weight_new = weight - step_rate * (
        first_hat / (jnp.sqrt(second_hat) + ADAM_EPS) + decay_rate * weight
    )
    shadow_new = SHADOW_KEEP * shadow + (1.0 - SHADOW_KEEP) * weight_new
    return (weight_new, first_new, second_new, shadow_new)


def square(v):
    return jnp.sum(v * v)


def norm_kernel(parts, subs, *refs):
    grads, rest = refs[: parts + 1 + subs], refs[parts + 1 + subs :]
    weights, (gains, everyone, gain_grad) = rest[: parts + subs], rest[parts + subs :]
    rows, width = grads[parts].shape
    one = two = jnp.zeros((rows, 1), f32)
    total = square(grads[parts][...])
    for i in range(parts):
        grad = grads[i][...]
        total = total + square(grad)
        one = one + jnp.sum(weights[i][...].astype(f32) * grad, axis=1, keepdims=True)
    for i in range(subs):
        grad = grads[parts + 1 + i][...]
        total = total + square(grad)
        up = weights[parts + i][...].astype(f32) * grad[:, :width]
        two = two + jnp.sum(up, axis=1, keepdims=True)
    lane = lax.broadcasted_iota(jnp.int32, (rows, LANES), 1)
    both = jnp.where(lane == 0, one, two)
    both = both.T[0:2, :] / gains[...].astype(bf16).astype(f32)
    gain_grad[...] = both
    everyone[...] = jnp.broadcast_to(total + square(both), everyone.shape)


def square_sums(parts, out, mlp, weights, gains, ndev):
    place = pl.BlockSpec(memory_space=pltpu.VMEM)
    inputs = [*parts, out, *mlp, *weights, gains]
    return pl.pallas_call(
        functools.partial(norm_kernel, len(parts), len(mlp)),
        in_specs=[place] * len(inputs),
        out_specs=[place] * 2,
        out_shape=[
            jax.ShapeDtypeStruct((ndev, 1, LANES), f32),
            jax.ShapeDtypeStruct(gains.shape, f32),
        ],
        compiler_params=params(),
        name="square_sums",
    )(*inputs)


def adam_kernel(parts, subs, rates, decays, sums_ref, *refs):
    count = parts + 2 + subs
    grads, states, outs = refs[:count], refs[count : count + 20], refs[count + 20 :]
    norm = jnp.sqrt(jnp.sum(sums_ref[...], axis=0))
    outs[20][...] = norm
    clip = jnp.minimum(1.0, CLIP_NORM / norm[:, 0:1])

    def update(i, rows, cols, grad):
        w, m, v, s = [states[4 * i + k][rows, cols] for k in range(4)]
        new = adam_step(w, m, v, grad, clip, rates[i], decays[i], s)
        for k in range(4):
            outs[4 * i + k][rows, cols] = new[k]

    wide = D // LANES // parts
    every = slice(None)
    for c in range(3):
        for p in range(parts):
            for j in range(wide):
                at = c * D + (p * wide + j) * LANES
                src = (3 * j + c) * LANES
                update(0, every, slice(at, at + LANES), grads[p][:, src : src + LANES])
    update(1, every, every, grads[parts][...])
    mlp = grads[parts + 1 : parts + 1 + subs]
    own = mlp[0].shape[0]
    size = subs * own
    for at in range(0, FF, LANES):
        grad = jnp.concatenate(
            [
                mlp[q][:, dev * own : (dev + 1) * own]
                for dev in range(at // size, (at + LANES) // size)
                for q in range(subs)
            ],
            axis=1,
        )
        update(2, every, slice(at, at + LANES), grad)
    for q in range(subs):
        update(3, slice(q * own, (q + 1) * own), every, mlp[q][:, D:])
    update(4, every, every, grads[-1][...])


def adam(sums, parts, out, mlp, gain, states, rates, decays):
    place = pl.BlockSpec(memory_space=pltpu.VMEM)
    inputs = [sums, *parts, out, *mlp, gain, *[v for group in states for v in group]]
    outputs = [jax.ShapeDtypeStruct(v.shape, f32) for group in states for v in group]
    outputs.append(jax.ShapeDtypeStruct((1, LANES), f32))
    done = pl.pallas_call(
        functools.partial(adam_kernel, len(parts), len(mlp), rates, decays),
        in_specs=[place] * len(inputs),
        out_specs=[place] * len(outputs),
        out_shape=outputs,
        compiler_params=params(),
        name="adam",
    )(*inputs)
    return [done[4 * i : 4 * i + 4] for i in range(5)], done[-1][0, 0]


def body(plan, *args):
    inputs, cotangent, frames = args[:3]
    masters, firsts, seconds, shadows = args[3:8], args[8:13], args[13:18], args[18:23]
    w_qkv, w_out, w_up, w_down, norm_gains = masters
    block, ndev = plan.block, plan.ndev
    x = inputs[0]
    length = x.shape[0]
    own = D // ndev
    subs = FF // D
    tab = lax.dynamic_index_in_dim(jnp.asarray(plan.tab), lax.axis_index("dp"), 0, keepdims=False)

    wide = D // GROUPS
    pairs = wide // LANES
    columns = 3 * wide
    every = D // LANES
    qkv_low = w_qkv.astype(bf16).reshape(own, 3, every, LANES).transpose(0, 2, 1, 3).reshape(own, 3 * D)
    gain_cols = jnp.pad(norm_gains.astype(bf16).T, ((0, 0), (0, LANES - 2)))
    local_q0 = jnp.concatenate([qkv_low[:, :columns], gain_cols], axis=1)
    up_low = w_up.astype(bf16).reshape(own, ndev, subs, own).transpose(2, 0, 1, 3).reshape(subs, own, D)
    down_low = w_down.astype(bf16).reshape(subs, own, D)
    local_mlp = [v for q in range(subs) for v in (up_low[q], down_low[q])]
    early = jnp.concatenate([qkv_low[:, columns:], w_out.astype(bf16)] + local_mlp[:2], axis=1)
    late = jnp.concatenate(local_mlp[2:], axis=1)

    flow = Flow(plan)
    step = flow.step
    reach = lambda v: lax.all_gather(v, "fsdp", axis=0, tiled=True)
    early = reach(early)
    held_q0 = reach(local_q0)
    flow.gather("q0", held_q0)
    step(None, ["q0"])
    late = reach(late)
    flow.gather("q1", early, 0, columns)
    flow.gather("o", early, columns, D)
    flow.gather("m0", early, columns + D, 2 * D)
    for k in range(1, subs):
        flow.gather(f"m{k}", late, 2 * (k - 1) * D, 2 * D)
    step(None, ["q0"])
    step(None, ["q0"])
    flow.until(None, ["q0"])
    step(None, ["q1", "o", "m0"])
    qkv0, u_one, gains, u_one_t = project_qkv(tab, x, flow.done["q0"], block, columns, True)
    qkv0, u_one = step((qkv0, u_one), ["q1", "o"])
    o0, lse0 = attend(frames, qkv0)
    o0, u_one = step((o0, u_one), ["q1", "o", "m0", "m1"])
    u_one = flow.until(u_one, ["q1"])
    (qkv1,) = project_qkv(tab, u_one, flow.done["q1"], block, columns, False)
    qkv1 = step(qkv1, ["o", "m1", "m2"])
    o1, lse1 = attend(frames, qkv1)
    qkv, o, lse = [qkv0, qkv1], [o0, o1], [lse0, lse1]
    o = step(o, ["o", "m0", "m2"])
    o = flow.until(o, ["o"])
    full_out = flow.done["o"]
    mid, u_two, u_two_t = middle(tab, o, x, gains, full_out, block)
    keep = (jnp.arange(length) < frames[0])[:, None]
    g_low = jnp.where(keep, cotangent[0], jnp.zeros((), bf16))
    u_two = step(u_two, ["m0", "m1", "m3"])
    held = [mid, None]
    plans = [
        ["m1", "m2", "m3", "g0"],
        ["m2", "m3", "g0", "g1"],
        ["m3", "g0", "g1", "g2"],
        ["g0", "g1", "g2", "g3"],
    ]
    for k in range(subs):
        u_two = flow.until(u_two, [f"m{k}"])
        out, du, sent, kept = feed_forward(
            tab, u_two, u_two_t, g_low, flow.done[f"m{k}"], 0, held, block, k == 0, k == subs - 1
        )
        held = [out, du]
        flow.scatter(f"g{k}", sent, kept)
        held[1] = step(held[1], plans[k])
    out, du = held
    dmid, d_o, sent, kept = middle_back(
        tab, frames, du, mid, cotangent[0], gains, o, full_out, block
    )
    flow.scatter("go", sent, kept)
    d_o = step(d_o, ["g1", "g2", "g3", "go"])
    calls = 4
    per = every // calls
    d_qkv = []
    plans = [["g2", "g3", "go", "gq0"], ["g3", "go", "gq0", "gq1"], ["go", "gq0", "gq1", "gq2"]]
    for i in range(calls):
        group, at = divmod(i * per, pairs)
        d, sent, kept = attend_back(
            frames, tab, qkv[group], d_o, lse[group], u_one_t, i * per, at, per, block
        )
        d_qkv.append(d)
        flow.scatter(f"gq{i}", sent, kept, True)
        if i < calls - 1:
            d_o = step(d_o, plans[i])
    dmid = step(dmid, ["gq1", "gq2", "gq3"])
    blocks = length // 256
    held_q = [flow.done["q0"], flow.done["q1"]]
    top = input_grad(tab, d_qkv, dmid, x, gains, held_q, block, 0, blocks // 2)
    top, dmid = step((top, dmid), ["gq2", "gq3"])
    low = input_grad(tab, d_qkv, dmid, x, gains, held_q, block, blocks // 2, blocks)
    low = step(low, ["gq3"])
    flow.until(None, list(flow.live))
    grad_in = jnp.concatenate([top, low], axis=0)
    own_rows = lambda n, direct=False: plan.own_rows(flow.done[n], direct)
    mlp_shards = [own_rows(f"g{k}") for k in range(subs)]
    out_shard = own_rows("go")
    parts = [own_rows(f"gq{i}", i == calls - 1) for i in range(calls)]

    size = per * 3 * LANES
    weights = [qkv_low[:, i * size : (i + 1) * size] for i in range(calls)] + list(up_low)
    sums, gain_shard = square_sums(parts, out_shard, mlp_shards, weights, norm_gains, ndev)
    everyone = lax.all_to_all(sums, AXES, 0, 0)
    rates = (0.6 / D**0.5, 0.6 / FANO**0.5, 0.6 / D**0.5, 0.6 / FF**0.5, 1.0)
    decays = (0.1, 0.1, 0.1, 0.1, 0.0)
    states = [(masters[i], firsts[i], seconds[i], shadows[i]) for i in range(5)]
    updated, grad_norm = adam(
        everyone, parts, out_shard, mlp_shards, gain_shard, states, rates, decays
    )
    return (
        out[None],
        grad_in[None],
        grad_norm,
        *(updated[i][part] for part in range(4) for i in range(5)),
    )


def solution(mesh):
    plan = Plan(mesh)
    split = P(AXES, None)
    lanes = P(None, AXES)
    weights = (split, split, split, split, lanes)
    return jax.shard_map(
        functools.partial(body, plan),
        mesh=mesh,
        in_specs=(P(AXES, None, None), P(AXES, None, None), P(AXES)) + weights * 4,
        out_specs=(P(AXES, None, None), P(AXES, None, None), P()) + weights * 4,
        check_vma=False,
    )
```

```python
import functools

import jax
import jax.numpy as jnp
import numpy as np
from jax import lax
from jax.experimental import pallas as pl
from jax.experimental.pallas import tpu as pltpu
from jax.sharding import PartitionSpec as P

D = 1024
HEAD_DIM = 64
FF = 4096
STEP = 7
FANO = 16

NORM_EPS = 1e-06
ADAM_EPS = 1e-08
BETA_ONE = 0.9
BETA_TWO = 0.95
SHADOW_KEEP = 0.8
CLIP_NORM = 1.0

AXES = ("dp", "fsdp")
GROUPS = 2
LANES = 128
VMEM = 62 << 20
f32 = jnp.float32
bf16 = jnp.bfloat16
NT = (((1,), (1,)), ((), ()))
TN = (((0,), (0,)), ((), ()))
GELU_A = 0.7978845608028654
GELU_B = 0.044715


def full(shape, single=False):
    rank = len(shape)
    mode = dict(pipeline_mode=pl.Buffered(1)) if single else {}
    return pl.BlockSpec(shape, lambda *_: (0,) * rank, **mode)


def params():
    return pltpu.CompilerParams(vmem_limit_bytes=VMEM)


def cost(flops, nbytes, trans=0):
    return pl.CostEstimate(flops=flops, bytes_accessed=nbytes, transcendentals=trans)


class Plan:
    def __init__(self, mesh):
        self.ndp, self.nfs = mesh.shape["dp"], mesh.shape["fsdp"]
        self.ndev = self.ndp * self.nfs
        self.bits = self.ndp.bit_length() - 1
        others = list(range(1, self.bits))
        half = len(others) // 2
        self.order = (others, others[half:] + others[:half])
        self.block = D // self.ndp
        tab = np.zeros((self.ndp, self.ndp), np.int32)
        for me in range(self.ndp):
            for rel in range(self.ndp):
                core = (me & 1) ^ (rel >> (self.bits - 1))
                nat = core
                for s, bit in enumerate(self.order[core]):
                    r = (rel >> (self.bits - 2 - s)) & 1
                    nat |= (((me >> bit) & 1) ^ r) << bit
                tab[me, rel] = nat
        self.tab = tab

    def pairs(self, flip):
        out = []
        for d in range(self.ndp):
            for f in range(self.nfs):
                out.append((d * self.nfs + f, flip(d) * self.nfs + f))
        return out

    def core_pairs(self):
        return self.pairs(lambda d: d ^ 1)

    def mix_pairs(self, s):
        return self.pairs(lambda d: d ^ (1 << self.order[d & 1][s]))

    def gather(self, mine):
        for s in reversed(range(self.bits - 1)):
            wide = s == 0
            (got,) = yield [mine], self.mix_pairs(s), None if wide else ("join", mine)
            mine = mine if wide else got
        held = [mine, got]
        return held + (yield held, self.core_pairs(), None)

    def scatter(self, sent, kept):
        pairs = self.core_pairs()
        for s in range(self.bits - 1):
            kept, sent = yield [sent], pairs, ("sum", [kept], [bf16, bf16])
            pairs = self.mix_pairs(s)
        (total,) = yield [sent], pairs, ("sum", [kept], [f32])
        return total

    def scatter_direct(self, sent, kept):
        count = self.ndp // 2
        kept, *sent = yield [sent], self.core_pairs(), ("sum", [kept], [f32] + [bf16] * (count - 1))
        pairs = [None] + [
            self.pairs(lambda d: d ^ self.mask(d & 1, rel)) for rel in range(1, count)
        ]
        (total,) = yield sent, pairs[1:], ("sum", [kept], [f32])
        return total

    def mask(self, core, rel):
        bits = enumerate(self.order[core])
        return sum(((rel >> (self.bits - 2 - s)) & 1) << bit for s, bit in bits)

    def own_rows(self, total, direct=False):
        if not direct or self.nfs > 4:
            return lax.psum_scatter(total, "fsdp", scatter_dimension=0, tiled=True)
        me, rows = lax.axis_index("fsdp"), total.shape[0] // self.nfs
        block = lambda f: lax.dynamic_slice_in_dim(total, f * rows, rows, 0)
        sum_ = block(me)
        for flip in range(1, self.nfs):
            pairs = [(i, i // self.nfs * self.nfs + (i % self.nfs ^ flip)) for i in range(self.ndev)]
            sum_ = sum_ + lax.ppermute(block(me ^ flip), AXES, pairs)
        return sum_


def tie_kernel(count, jobs, *refs):
    sems = refs[-1]
    free = iter(range(sems.shape[0]))
    copy = lambda x, y: pltpu.make_async_copy(x, y, sems.at[next(free)])
    total = count + sum(job["inputs"] for job in jobs)
    made = sum(len(job["outputs"]) for job in jobs)
    inputs, outputs = list(refs[count:total]), list(refs[total + count : total + count + made])
    scratch = list(refs[total + count + made : -1])
    steps = []
    for job in jobs:
        ins = [inputs.pop(0) for _ in range(job["inputs"])]
        outs = [outputs.pop(0) for _ in job["outputs"]]
        if job["kind"] == "cut":
            at, wide = job["cut"]
            held = scratch.pop(0)
            steps.append(([copy(ins[0].at[:, pl.ds(at, wide)], held)], None, copy(held, outs[0])))
        elif job["kind"] == "join":
            held = scratch.pop(0)
            rows = ins[0].shape[0]
            loads = [copy(v, held.at[pl.ds(i * rows, rows)]) for i, v in enumerate(ins)]
            steps.append((loads, None, copy(held, outs[0])))
        else:
            rows = outs[0].shape[0]
            for i, out in reversed(list(enumerate(outs))):
                held = [scratch.pop(0) for _ in range(len(ins) + 1)]
                loads = [copy(v.at[pl.ds(i * rows, rows)], h) for v, h in zip(ins, held)]
                steps.append((loads, held, copy(held[-1], out)))
    for loads, _, _ in steps:
        for c in loads:
            c.start()
    for loads, held, save in steps:
        for c in loads:
            c.wait()
        if held:
            total = held[0][...].astype(f32)
            for h in held[1:-1]:
                total = total + h[...].astype(f32)
            held[-1][...] = total.astype(held[-1].dtype)
        save.start()
    for _, _, save in steps:
        save.wait()


def tie(same, work=()):
    leaves, form = jax.tree.flatten(same)
    place = pl.BlockSpec(memory_space=pl.ANY)
    count = len(leaves)
    jobs, inputs, made, scratch, copies = [], list(leaves), [], [], 1
    shape = lambda dims, kind: jax.ShapeDtypeStruct(dims, kind)
    for kind, *rest in work:
        if kind == "cut":
            v, at, wide = rest
            arrays, outs = [v], [shape((v.shape[0], wide), v.dtype)]
            scratch.append(outs[0])
            copies += 2
        elif kind == "join":
            arrays = rest
            outs = [shape((2 * rest[0].shape[0], rest[0].shape[1]), rest[0].dtype)]
            scratch.append(outs[0])
            copies += 3
        else:
            arrays, kinds = rest
            rows = arrays[0].shape[0] // len(kinds)
            outs = [shape((rows, arrays[0].shape[1]), k) for k in kinds]
            for out in reversed(outs):
                scratch += [shape(out.shape, v.dtype) for v in arrays] + [out]
            copies += (len(arrays) + 1) * len(outs)
        inputs += arrays
        made.append(outs)
        jobs.append(dict(kind=kind, inputs=len(arrays), outputs=outs, cut=tuple(rest[1:3]) if kind == "cut" else None))
    if not inputs:
        return same, []
    outputs = [shape(v.shape, v.dtype) for v in leaves] + [v for outs in made for v in outs]
    out = list(
        pl.pallas_call(
            functools.partial(tie_kernel, count, jobs),
            in_specs=[place] * len(inputs),
            out_specs=[place] * len(outputs),
            out_shape=outputs,
            scratch_shapes=[pltpu.VMEM(v.shape, v.dtype) for v in scratch]
            + [pltpu.SemaphoreType.DMA((copies,))],
            input_output_aliases={i: i for i in range(count)},
            compiler_params=params(),
            name="tie",
        )(*inputs)
    )
    same, out = jax.tree.unflatten(form, out[:count]), out[count:]
    return same, [[out.pop(0) for _ in outs] for outs in made]


class Flow:
    def __init__(self, plan):
        self.plan = plan
        self.live, self.flying, self.done, self.waiting, self.shards = {}, {}, {}, {}, {}

    def gather(self, name, array, at=None, wide=None):
        self.waiting[name] = (array, at, wide)

    def scatter(self, name, sent, kept, direct=False):
        way = self.plan.scatter_direct if direct else self.plan.scatter
        self.live[name] = way(sent, kept)

    def own_rows(self, name, total=None):
        self.shards[name] = self.plan.own_rows(self.done[name] if total is None else total)

    def step(self, x, names, pinned=()):
        names = [n for n in names if n not in self.done]
        came = {n: self.flying.pop(n) for n in names if n in self.flying}
        start = {n: self.waiting.pop(n) for n in names if n in self.waiting}
        plain = {n: got for n, (got, merge) in came.items() if merge is None}
        whole = {n: v for n, (v, at, _) in start.items() if at is None}
        work = {}
        for n, (got, merge) in came.items():
            if merge and merge[0] == "join":
                work[n] = ("join", merge[1], *got)
            elif merge:
                work[n] = ("sum", merge[1] + got, merge[2])
        work |= {n: ("cut", *v) for n, v in start.items() if v[1] is not None}
        held = {n: self.shards[n] for n in pinned}
        (x, plain, whole, held), made = tie((x, plain, whole, held), list(work.values()))
        self.shards |= held
        made = dict(zip(work, made))
        for n in start:
            self.live[n] = self.plan.gather(whole[n] if n in whole else made[n][0])
        for n in names:
            value = None if n in start else plain.get(n, made.get(n))
            try:
                sent, pairs, merge = self.live[n].send(value)
                each = pairs if isinstance(pairs[0], list) else [pairs] * len(sent)
                self.flying[n] = ([lax.ppermute(v, AXES, p) for v, p in zip(sent, each)], merge)
            except StopIteration as stop:
                self.done[n] = stop.value
        return x

    def until(self, x, names):
        while any(n not in self.done for n in names):
            x = self.step(x, names)
        return x


def natural(dst, cols, pieces, src_cols, tab, block):
    j = 0
    for piece in pieces:
        for i in range(piece.shape[0] // block):
            row = pl.multiple_of(tab[j] * block, block)
            dst[pl.ds(row, block), cols] = piece[i * block : (i + 1) * block, src_cols]
            j += 1


def relative(sent, kept, cols, src, src_cols, tab, block):
    half = src.shape[0] // block // 2
    for j in range(2 * half):
        row = pl.multiple_of(tab[j] * block, block)
        out = kept if j < half else sent
        i = j % half
        out[i * block : (i + 1) * block, cols] = src[pl.ds(row, block), src_cols]


def qkv_kernel(count, block, first, tab, *refs):
    if first:
        x_ref, refs = refs[0], refs[1:]
        gains, weights = refs[:count], refs[count : 2 * count]
        qkv_ref, u_ref, gain_ref, u_t_ref, w_nat, g_nat = refs[2 * count :]

        @pl.when(pl.program_id(0) == 0)
        def _():
            natural(g_nat, slice(None), gains, slice(None), tab, block)
            rows = g_nat[...].astype(f32).T
            gain_ref[...] = rows[:8]
            x = x_ref[...].astype(f32)
            r = lax.rsqrt(jnp.mean(x * x, axis=1, keepdims=True) + NORM_EPS)
            u = (x * r * rows[0:1]).astype(bf16)
            u_ref[...] = u
            u_t_ref[...] = u.T

    else:
        u_ref, weights, (qkv_ref, w_nat) = refs[0], refs[1 : 1 + count], refs[1 + count :]
    natural(w_nat, slice(None), weights, slice(None), tab, block)
    qkv_ref[...] = jnp.dot(u_ref[...], w_nat[...], preferred_element_type=f32).astype(bf16)


def project_qkv(tab, x, pieces, block, columns, first):
    length, width = x.shape
    wide = 512
    last = columns // LANES
    col = pl.BlockSpec((length, wide), lambda j, t: (0, j))
    extra = first * [full((length, width)), full((8, width)), full((width, length))]
    shapes = first * [
        jax.ShapeDtypeStruct((length, width), bf16),
        jax.ShapeDtypeStruct((8, width), f32),
        jax.ShapeDtypeStruct((width, length), bf16),
    ]
    gains = first * [pl.BlockSpec((p.shape[0], LANES), lambda j, t: (0, last)) for p in pieces]
    return pl.pallas_call(
        functools.partial(qkv_kernel, len(pieces), block, first),
        grid_spec=pltpu.PrefetchScalarGridSpec(
            num_scalar_prefetch=1,
            grid=(columns // wide,),
            in_specs=[full((length, width), True)]
            + gains
            + [pl.BlockSpec((p.shape[0], wide), lambda j, t: (0, j)) for p in pieces],
            out_specs=[col] + extra,
            scratch_shapes=[pltpu.VMEM((width, wide), bf16)]
            + first * [pltpu.VMEM((width, LANES), bf16)],
        ),
        out_shape=[jax.ShapeDtypeStruct((length, columns), bf16)] + shapes,
        compiler_params=params(),
        cost_estimate=cost(2 * length * width * columns, 20 << 20),
        name="qkv",
    )(tab, x, *(first * pieces), *pieces)


def fold(v, op):
    v = v.reshape(v.shape[0] // 64, 64, v.shape[1])
    return op(op(v, axis=0), axis=0, keepdims=True)


def attend_kernel(rows_of, n_ref, q_ref, k_ref, v_ref, o_ref, lse_ref):
    n = n_ref[0]
    length = q_ref.shape[0]
    lane = lax.broadcasted_iota(jnp.int32, (1, LANES), 1)
    masks = [(lane < HEAD_DIM).astype(bf16), (lane >= HEAD_DIM).astype(bf16)]
    v_t = v_ref[...].T
    for i in range(length // rows_of):
        rows = pl.ds(i * rows_of, rows_of)
        keys = (i + 1) * rows_of

        def run(limited):
            q = q_ref[rows, :] * bf16(HEAD_DIM**-0.5)
            k = k_ref[0:keys, :]
            parts = []
            for h in range(2):
                s = lax.dot_general(k, q * masks[h], NT, preferred_element_type=f32)
                if limited:
                    key = lax.broadcasted_iota(jnp.int32, (keys, rows_of), 0)
                    query = lax.broadcasted_iota(jnp.int32, (keys, rows_of), 1) + i * rows_of
                    s = jnp.where((key <= query) & (key < n), s, -1e30)
                else:
                    key = lax.broadcasted_iota(jnp.int32, (rows_of, rows_of), 0)
                    query = lax.broadcasted_iota(jnp.int32, (rows_of, rows_of), 1)
                    tail = jnp.where(key <= query, s[keys - rows_of :], -1e30)
                    s = tail if i == 0 else jnp.concatenate([s[: keys - rows_of], tail], axis=0)
                peak = fold(s, jnp.max)
                e = jnp.exp(s - peak)
                total = fold(e, jnp.sum)
                p = (e * (1.0 / total)).astype(bf16)
                v_h = v_t[h * HEAD_DIM : (h + 1) * HEAD_DIM, 0:keys]
                parts.append(jnp.dot(v_h, p, preferred_element_type=f32))
                query = lax.broadcasted_iota(jnp.int32, (1, rows_of), 1) + i * rows_of
                lse_ref[0, h : h + 1, rows] = jnp.where(query < n, peak + jnp.log(total), 1e30)
            o_ref[rows, :] = jnp.concatenate(parts, axis=0).astype(bf16).T

        @pl.when(n >= keys)
        def _():
            run(False)

        @pl.when(n < keys)
        def _():
            run(True)


def attend(frames, qkv):
    length, width = qkv.shape[0], qkv.shape[1] // 3
    pairs = width // LANES
    part = lambda c: pl.BlockSpec((length, LANES), lambda j, n: (0, 3 * j + c))
    return pl.pallas_call(
        functools.partial(attend_kernel, 512),
        grid_spec=pltpu.PrefetchScalarGridSpec(
            num_scalar_prefetch=1,
            grid=(pairs,),
            in_specs=[part(0), part(1), part(2)],
            out_specs=[
                pl.BlockSpec((length, LANES), lambda j, n: (0, j)),
                pl.BlockSpec((1, 2, length), lambda j, n: (j, 0, 0)),
            ],
        ),
        out_shape=[
            jax.ShapeDtypeStruct((length, width), bf16),
            jax.ShapeDtypeStruct((pairs, 2, length), f32),
        ],
        compiler_params=params(),
        cost_estimate=cost(16 * length * length * width, 8 << 20, length * length * 16),
        name="attend",
    )(frames, qkv, qkv, qkv)


def mid_kernel(count, groups, block, tab, x_ref, gain_ref, *refs):
    o_refs, refs = refs[:groups], refs[groups:]
    weights = refs[:count]
    mid_ref, u_ref, u_t_ref, w_nat = refs[count:]

    @pl.when(pl.program_id(0) == 0)
    def _():
        natural(w_nat, slice(None), weights, slice(None), tab, block)

    o = jnp.concatenate([ref[...] for ref in o_refs], axis=1)
    mid = x_ref[...].astype(f32) + jnp.dot(o, w_nat[...], preferred_element_type=f32)
    r = lax.rsqrt(jnp.mean(mid * mid, axis=1, keepdims=True) + NORM_EPS)
    u = (mid * r * gain_ref[1:2, :]).astype(bf16)
    mid_ref[...] = mid
    u_ref[...] = u
    u_t_ref[...] = u.T


def middle(tab, o, x, gains, pieces, block):
    length, width = x.shape
    rows = 256
    row = pl.BlockSpec((rows, width), lambda i, t: (i, 0))
    return pl.pallas_call(
        functools.partial(mid_kernel, len(pieces), len(o), block),
        grid_spec=pltpu.PrefetchScalarGridSpec(
            num_scalar_prefetch=1,
            grid=(length // rows,),
            in_specs=[row, full((8, width))]
            + [pl.BlockSpec((rows, v.shape[1]), lambda i, t: (i, 0)) for v in o]
            + [full(p.shape) for p in pieces],
            out_specs=[row, row, pl.BlockSpec((width, rows), lambda i, t: (0, i))],
            scratch_shapes=[pltpu.VMEM((width, width), bf16)],
        ),
        out_shape=[
            jax.ShapeDtypeStruct((length, width), f32),
            jax.ShapeDtypeStruct((length, width), bf16),
            jax.ShapeDtypeStruct((width, length), bf16),
        ],
        compiler_params=params(),
        cost_estimate=cost(2 * length * width * width, 16 << 20),
        name="middle",
    )(tab, x, gains, *o, *pieces)


def gelu_both(z):
    sq = z * z
    t = jnp.tanh(z * (GELU_A + (GELU_A * GELU_B) * sq))
    half = 0.5 + 0.5 * t
    slope = half + (0.5 * z) * (1.0 - t * t) * (GELU_A + (3 * GELU_A * GELU_B) * sq)
    return z * half, slope


def norm_back(v, gain, du):
    r = lax.rsqrt(jnp.mean(v * v, axis=1, keepdims=True) + NORM_EPS)
    up = du * gain
    return r * up - v * (r * r * r * jnp.mean(up * v, axis=1, keepdims=True))


def mlp_kernel(counts, block, first, last, outs, tab, *refs):
    refs = list(refs)
    take = lambda n: [refs.pop(0) for _ in range(n)]
    u_hbm, u_t_hbm, g_hbm = take(3)
    pieces = [take(count) for count in counts]
    (held_out,) = take(1)
    held_du = None if first else take(1)[0]
    if last:
        mid_hbm, gain_hbm = take(2)
        o_hbm, w_hbm = take(outs[0]), take(outs[1])
    (out_hbm,) = take(1)
    if last:
        dmid_hbm, do_hbm, out_sent, out_kept = take(4)
    else:
        (du_hbm,) = take(1)
    sent, kept = take(2)
    u, u_t, g, up_s, down_s, out_acc, du_acc, a_s, dz_s, grad, low, gain, sems = refs
    length, width = u.shape
    wide = 512
    halves = width // wide
    blocks = width // block
    subs = len(counts)
    free = iter(range(sems.shape[0]))

    def copy(src, dst):
        return pltpu.make_async_copy(src, dst, sems.at[next(free)])

    def rows(held, at, columns, dst, dst_columns):
        out, j = [], 0
        for piece in held:
            for i in range(piece.shape[0] // block):
                row = pl.multiple_of(tab[j] * block, block)
                src = piece.at[pl.ds(i * block, block), pl.ds(at, columns)]
                out.append(copy(src, dst.at[pl.ds(row, block), dst_columns]))
                j += 1
        return out

    def back(columns, sent_to, kept_to, at):
        out = []
        for j in range(blocks):
            row = pl.multiple_of(tab[j] * block, block)
            to = kept_to if j < blocks // 2 else sent_to
            dst = to.at[pl.ds(j % (blocks // 2) * block, block), pl.ds(at, columns)]
            out.append(copy(grad.at[pl.ds(row, block), pl.ds(0, columns)], dst))
        return out

    def start(copies):
        for c in copies:
            c.start()

    def wait(copies):
        for c in copies:
            c.wait()

    get_u, get_g, get_t = [copy(u_hbm, u)], [copy(g_hbm, g)], [copy(u_t_hbm, u_t)]
    get_up = [
        [rows(pieces[i], f * wide, wide, up_s.at[i], pl.ds(f * wide, wide)) for f in range(halves)]
        for i in range(subs)
    ]
    get_down = [rows(pieces[i], width, width, down_s.at[i], pl.ds(0, width)) for i in range(subs)]
    get_acc = [copy(held_out, out_acc)] + ([] if first else [copy(held_du, du_acc)])
    start(get_u + get_up[0][0] + get_g + get_down[0] + get_t)
    for f in range(1, halves):
        start(get_up[0][f])
    start(get_acc)
    for i in range(1, subs):
        start(sum(get_up[i], []) + get_down[i])
    waiting, saved = [], []
    half = length // 2
    for i in range(subs):
        up, down = up_s.at[i], down_s.at[i]
        final = i == subs - 1
        for f in range(halves):
            cols = slice(f * wide, (f + 1) * wide)
            wait((get_u if i + f == 0 else []) + get_up[i][f])
            z = jnp.dot(u[...], up[:, cols], preferred_element_type=f32)
            a, slope = gelu_both(z)
            if f == 0:
                wait((get_g if i == 0 else []) + get_down[i])
            da = lax.dot_general(g[...], down[cols, :], NT, preferred_element_type=f32)
            a_s[:, cols] = a.astype(bf16)
            dz_s[:, cols] = (da * slope).astype(bf16)
            if f == 0:
                wait((get_t if i == 0 else []) + waiting)
            part = jnp.dot(u_t[...], dz_s[:, cols], preferred_element_type=f32)
            grad[:, cols] = part.astype(bf16)
            turned = lax.dot_general(a_s[:, cols], g[...], TN, preferred_element_type=f32)
            grad[cols, width:] = turned.astype(bf16)
        waiting = back(2 * width, sent, kept, 2 * i * width)
        start(waiting)
        if i == 0:
            wait(get_acc)
        for r in range(2):
            part = pl.ds(r * half, half)
            out = out_acc[part, :] + jnp.dot(a_s[part, :], down[...], preferred_element_type=f32)
            if last and final:
                low[part, :] = out.astype(bf16)
                saved.append(copy(low.at[part], out_hbm.at[part]))
                saved[-1].start()
            else:
                out_acc[part, :] = out
                if final:
                    saved.append(copy(out_acc.at[part], out_hbm.at[part]))
                    saved[-1].start()
        if last and final:
            get_w = rows(w_hbm, 0, width, down, pl.ds(0, width)) + [copy(gain_hbm, gain)]
            start(get_w)
            get_mid = [copy(mid_hbm, out_acc)]
            at = 0
            for o in o_hbm:
                get_mid.append(copy(o, a_s.at[:, pl.ds(at, o.shape[1])]))
                at += o.shape[1]
            start(get_mid)
        for r in range(2):
            part = pl.ds(r * half, half)
            du = lax.dot_general(dz_s[part, :], up[...], NT, preferred_element_type=f32)
            du_acc[part, :] = du if first and i == 0 else du_acc[part, :] + du
            if final and not last:
                saved.append(copy(du_acc.at[part], du_hbm.at[part]))
                saved[-1].start()
    if last:
        wait(get_w + get_mid)
        size = 256
        for r in range(length // size):
            part = pl.ds(r * size, size)
            dmid = g[part, :].astype(f32) + norm_back(out_acc[part, :], gain[1:2, :], du_acc[part, :])
            du_acc[part, :] = dmid
            u[part, :] = dmid.astype(bf16)
            saved.append(copy(du_acc.at[part], dmid_hbm.at[part]))
            saved[-1].start()
            do = lax.dot_general(u[part, :], down_s[subs - 1], NT, preferred_element_type=f32)
            dz_s[part, :] = do.astype(bf16)
            saved.append(copy(dz_s.at[part], do_hbm.at[part]))
            saved[-1].start()
        wait(waiting)
        turned = lax.dot_general(a_s[...], u[...], TN, preferred_element_type=f32)
        grad[:, 0:width] = turned.astype(bf16)
        waiting = back(width, out_sent, out_kept, 0)
        start(waiting)
    wait(waiting + saved)


def feed_forward(tab, u, u_t, g, pieces, held, block, first, last=None):
    length, width = u.shape
    half = width // 2
    anywhere = pl.BlockSpec(memory_space=pl.ANY)
    held = held[:1] if first else held
    inputs = [u, u_t, g, *[p for group in pieces for p in group], *held]
    acc = jax.ShapeDtypeStruct((length, width), f32)
    low = jax.ShapeDtypeStruct((length, width), bf16)
    shard = lambda w: jax.ShapeDtypeStruct((half, w), bf16)
    alias, outs = {}, (0, 0)
    if last:
        mid, gains, o, w_out = last
        inputs += [mid, gains, *o, *w_out]
        outputs = [low, acc, low, shard(width), shard(width)]
        outs = (len(o), len(w_out))
    else:
        outputs = [acc, acc]
    outputs += [shard(2 * width * len(pieces))] * 2
    blocks = width // block
    subs = len(pieces)
    return pl.pallas_call(
        functools.partial(mlp_kernel, [len(p) for p in pieces], block, first, last is not None, outs),
        grid_spec=pltpu.PrefetchScalarGridSpec(
            num_scalar_prefetch=1,
            grid=(1,),
            in_specs=[anywhere] * len(inputs),
            out_specs=[anywhere] * len(outputs),
            scratch_shapes=[
                pltpu.VMEM((length, width), bf16),
                pltpu.VMEM((width, length), bf16),
                pltpu.VMEM((length, width), bf16),
                pltpu.VMEM((subs, width, width), bf16),
                pltpu.VMEM((subs, width, width), bf16),
                pltpu.VMEM((length, width), f32),
                pltpu.VMEM((length, width), f32),
                pltpu.VMEM((length, width), bf16),
                pltpu.VMEM((length, width), bf16),
                pltpu.VMEM((width, 2 * width), bf16),
                pltpu.VMEM((length, width) if last else (16, LANES), bf16),
                pltpu.VMEM((8, width), f32),
                pltpu.SemaphoreType.DMA(((4 * subs + 2) * blocks + 32,)),
            ],
        ),
        out_shape=outputs,
        input_output_aliases=alias,
        compiler_params=params(),
        cost_estimate=cost((12 * subs + 4 * outs[0]) * length * width * width, 48 << 20),
        name="feed_forward",
    )(tab, *inputs)


def attend_back_kernel(
    rows_of, block, n_ref, tab, q_ref, k_ref, v_ref, g_ref, lse_ref, u_t_ref, d_ref, sent, kept, dk, dv, d_s, grad
):
    n = n_ref[0]
    length = q_ref.shape[0]
    scale = HEAD_DIM**-0.5
    lane = lax.broadcasted_iota(jnp.int32, (1, LANES), 1)
    masks = [(lane < HEAD_DIM).astype(bf16), (lane >= HEAD_DIM).astype(bf16)]
    dk[...] = jnp.zeros_like(dk)
    dv[...] = jnp.zeros_like(dv)
    for i in range(length // rows_of):
        rows = pl.ds(i * rows_of, rows_of)
        keys = (i + 1) * rows_of

        @pl.when(n > i * rows_of)
        def _():
            q = q_ref[rows, :] * bf16(scale)
            g = g_ref[rows, :]
            k, v = k_ref[0:keys, :], v_ref[0:keys, :]
            dq = None
            for h in range(2):
                q_h, g_h, k_h = q * masks[h], g * masks[h], k * masks[h]
                s = lax.dot_general(k, q_h, NT, preferred_element_type=f32)
                key = lax.broadcasted_iota(jnp.int32, (rows_of, rows_of), 0)
                query = lax.broadcasted_iota(jnp.int32, (rows_of, rows_of), 1)
                tail = jnp.where(key <= query, s[keys - rows_of :], -1e30)
                s = tail if i == 0 else jnp.concatenate([s[: keys - rows_of], tail], axis=0)
                p = jnp.exp(s - lse_ref[0, h : h + 1, rows])
                dp = lax.dot_general(v, g_h, NT, preferred_element_type=f32)
                delta = fold(p * dp, jnp.sum)
                ds = (p * (dp - delta)).astype(bf16)
                dv[0:keys, :] += jnp.dot(p.astype(bf16), g_h, preferred_element_type=f32)
                dk[0:keys, :] += jnp.dot(ds, q_h, preferred_element_type=f32)
                part = lax.dot_general(ds, k_h, TN, preferred_element_type=f32)
                dq = part if dq is None else dq + part
            d_s[rows, 0:LANES] = (dq * scale).astype(bf16)

        @pl.when(n <= i * rows_of)
        def _():
            d_s[rows, 0:LANES] = jnp.zeros((rows_of, LANES), bf16)

    d_s[:, LANES : 2 * LANES] = dk[...].astype(bf16)
    d_s[:, 2 * LANES :] = dv[...].astype(bf16)
    d_ref[...] = d_s[...]
    grad[...] = jnp.dot(u_t_ref[...], d_s[...], preferred_element_type=f32)
    relative(sent, kept, slice(None), grad, slice(None), tab, block)


def attend_back(frames, tab, qkv, g, lse, u_t, first, at, pairs, block):
    length, width = qkv.shape[0], u_t.shape[0]
    wide = 3 * LANES
    part = lambda c: pl.BlockSpec((length, LANES), lambda j, n, t: (0, 3 * (j + at) + c))
    half = width // 2
    out = pl.BlockSpec((half, wide), lambda j, n, t: (0, j))
    shape = jax.ShapeDtypeStruct((half, pairs * wide), f32)
    return pl.pallas_call(
        functools.partial(attend_back_kernel, 256, block),
        grid_spec=pltpu.PrefetchScalarGridSpec(
            num_scalar_prefetch=2,
            grid=(pairs,),
            in_specs=[
                part(0),
                part(1),
                part(2),
                pl.BlockSpec((length, LANES), lambda j, n, t: (0, j + first)),
                pl.BlockSpec((1, 2, length), lambda j, n, t: (j + at, 0, 0)),
                full((width, length), True),
            ],
            out_specs=[pl.BlockSpec((length, wide), lambda j, n, t: (0, j)), out, out],
            scratch_shapes=[
                pltpu.VMEM((length, LANES), f32),
                pltpu.VMEM((length, LANES), f32),
                pltpu.VMEM((length, wide), bf16),
                pltpu.VMEM((width, wide), f32),
            ],
        ),
        out_shape=[jax.ShapeDtypeStruct((length, pairs * wide), bf16), shape, shape],
        compiler_params=params(),
        cost_estimate=cost(40 * length * length * pairs * LANES, 16 << 20, length * length * 2 * pairs),
        name="attend_back",
    )(frames, tab, qkv, qkv, qkv, g, lse, u_t)


def input_grad_kernel(groups, parts, more, block, tab, dmid_ref, x_ref, gain_ref, *refs):
    refs = refs[more:]
    d_refs, refs = refs[:parts], refs[parts:]
    weights, out_ref, nats = refs[: -1 - groups], refs[-1 - groups], refs[-groups:]
    count = len(weights) // groups

    @pl.when(pl.program_id(0) == 0)
    def _():
        for i, nat in enumerate(nats):
            natural(nat, slice(None), weights[i * count : (i + 1) * count], slice(None), tab, block)

    du = None
    for i, nat in enumerate(nats):
        mine = d_refs[i * parts // groups : (i + 1) * parts // groups]
        d = jnp.concatenate([ref[...] for ref in mine], axis=1)
        part = lax.dot_general(d, nat[...], NT, preferred_element_type=f32)
        du = part if du is None else du + part
    out_ref[...] = dmid_ref[...] + norm_back(x_ref[...].astype(f32), gain_ref[0:1, :], du)


def input_grad(tab, d, dmid, x, gains, pieces, block, lo, hi, done=()):
    length, width = x.shape
    rows = 256
    groups = len(pieces)
    columns = 3 * width // groups
    row = lambda w: pl.BlockSpec((rows, w), lambda i, t: (i + lo, 0))
    weights = [
        pl.BlockSpec((p.shape[0], columns), lambda i, t: (0, 0), pipeline_mode=pl.Buffered(1))
        for group in pieces
        for p in group
    ]
    return pl.pallas_call(
        functools.partial(input_grad_kernel, groups, len(d), len(done), block),
        grid_spec=pltpu.PrefetchScalarGridSpec(
            num_scalar_prefetch=1,
            grid=(hi - lo,),
            in_specs=[row(width), row(width), full((8, width))]
            + [pl.BlockSpec(memory_space=pl.ANY)] * len(done)
            + [row(v.shape[1]) for v in d]
            + weights,
            out_specs=row(width),
            scratch_shapes=[pltpu.VMEM((width, columns), bf16)] * groups,
        ),
        out_shape=jax.ShapeDtypeStruct((length, width), f32),
        input_output_aliases={4: 0} if done else {},
        compiler_params=params(),
        cost_estimate=cost(6 * length * width * width * (hi - lo) // 4, 22 << 20),
        name="input_grad",
    )(tab, dmid, x, gains, *done, *d, *[p for group in pieces for p in group])


def adam_step(weight, first, second, gradient, clip_factor, step_rate, decay_rate, shadow):
    clipped = gradient * clip_factor
    first_new = BETA_ONE * first + (1.0 - BETA_ONE) * clipped
    second_new = BETA_TWO * second + (1.0 - BETA_TWO) * clipped * clipped
    first_hat = first_new / (1.0 - BETA_ONE**STEP)
    second_hat = second_new / (1.0 - BETA_TWO**STEP)
    weight_new = weight - step_rate * (
        first_hat / (jnp.sqrt(second_hat) + ADAM_EPS) + decay_rate * weight
    )
    shadow_new = SHADOW_KEEP * shadow + (1.0 - SHADOW_KEEP) * weight_new
    return (weight_new, first_new, second_new, shadow_new)


def square(v):
    return jnp.sum(v * v)


def view(refs, views, i, lo=0, hi=None):
    array, at, width = views[i]
    return refs[array][:, at + lo : at + (width if hi is None else hi)].astype(f32)


def norm_kernel(arrays, views, parts, *refs):
    grads, rest = refs[:arrays], refs[arrays:]
    weights, (gains, everyone, gain_grad) = rest[:-3], rest[-3:]
    rows, width = gains.shape[1], D
    one = two = jnp.zeros((rows, 1), f32)
    total = square(view(grads, views, parts))
    for i in range(parts):
        grad = view(grads, views, i)
        total = total + square(grad)
        one = one + jnp.sum(weights[i][...].astype(f32) * grad, axis=1, keepdims=True)
    for i in range(len(views) - parts - 1):
        grad = view(grads, views, parts + 1 + i)
        total = total + square(grad)
        up = weights[parts + i][...].astype(f32) * grad[:, :width]
        two = two + jnp.sum(up, axis=1, keepdims=True)
    lane = lax.broadcasted_iota(jnp.int32, (rows, LANES), 1)
    both = jnp.where(lane == 0, one, two)
    both = both.T[0:2, :] / gains[...].astype(bf16).astype(f32)
    gain_grad[...] = both
    everyone[...] = jnp.broadcast_to(total + square(both), everyone.shape)


def square_sums(arrays, views, parts, weights, gains, ndev):
    place = pl.BlockSpec(memory_space=pltpu.VMEM)
    inputs = [*arrays, *weights, gains]
    return pl.pallas_call(
        functools.partial(norm_kernel, len(arrays), views, parts),
        in_specs=[place] * len(inputs),
        out_specs=[place] * 2,
        out_shape=[
            jax.ShapeDtypeStruct((ndev, 1, LANES), f32),
            jax.ShapeDtypeStruct(gains.shape, f32),
        ],
        compiler_params=params(),
        name="square_sums",
    )(*inputs)


def adam_kernel(arrays, views, parts, rates, decays, sums_ref, *refs):
    grads, gain_grad, refs = refs[:arrays], refs[arrays], refs[arrays + 1 :]
    states, outs = refs[:20], refs[20:]
    norm = jnp.sqrt(jnp.sum(sums_ref[...], axis=0))
    outs[20][...] = norm
    clip = jnp.minimum(1.0, CLIP_NORM / norm[:, 0:1])

    def update(i, rows, cols, grad):
        w, m, v, s = [states[4 * i + k][rows, cols] for k in range(4)]
        new = adam_step(w, m, v, grad, clip, rates[i], decays[i], s)
        for k in range(4):
            outs[4 * i + k][rows, cols] = new[k]

    every = slice(None)
    col = 0
    for p in range(parts):
        for j in range(views[p][2] // (3 * LANES)):
            for c in range(3):
                at = c * D + col * LANES
                src = (3 * j + c) * LANES
                update(0, every, slice(at, at + LANES), view(grads, views, p, src, src + LANES))
            col += 1
    update(1, every, every, view(grads, views, parts))
    own = states[0].shape[0]
    subs = FF // D
    size = subs * own
    for at in range(0, FF, LANES):
        pieces = [
            view(grads, views, parts + 1 + q, dev * own, (dev + 1) * own)
            for dev in range(at // size, (at + LANES) // size)
            for q in range(subs)
        ]
        update(2, every, slice(at, at + LANES), jnp.concatenate(pieces, axis=1))
    for q in range(subs):
        grad = view(grads, views, parts + 1 + q, D, 2 * D)
        update(3, slice(q * own, (q + 1) * own), every, grad)
    update(4, every, every, gain_grad[...])


def adam(sums, arrays, views, parts, gain, states, rates, decays):
    place = pl.BlockSpec(memory_space=pltpu.VMEM)
    inputs = [sums, *arrays, gain, *[v for group in states for v in group]]
    outputs = [jax.ShapeDtypeStruct(v.shape, f32) for group in states for v in group]
    outputs.append(jax.ShapeDtypeStruct((1, LANES), f32))
    done = pl.pallas_call(
        functools.partial(adam_kernel, len(arrays), views, parts, rates, decays),
        in_specs=[place] * len(inputs),
        out_specs=[place] * len(outputs),
        out_shape=outputs,
        compiler_params=params(),
        name="adam",
    )(*inputs)
    return [done[4 * i : 4 * i + 4] for i in range(5)], done[-1][0, 0]


def body(plan, *args):
    inputs, cotangent, frames = args[:3]
    masters, firsts, seconds, shadows = args[3:8], args[8:13], args[13:18], args[18:23]
    w_qkv, w_out, w_up, w_down, norm_gains = masters
    block, ndev = plan.block, plan.ndev
    x = inputs[0]
    length = x.shape[0]
    own = D // ndev
    subs = FF // D
    tab = lax.dynamic_index_in_dim(jnp.asarray(plan.tab), lax.axis_index("dp"), 0, keepdims=False)

    wide = D // GROUPS
    pairs = wide // LANES
    columns = 3 * wide
    every = D // LANES
    qkv_low = w_qkv.astype(bf16).reshape(own, 3, every, LANES).transpose(0, 2, 1, 3).reshape(own, 3 * D)
    gain_cols = jnp.pad(norm_gains.astype(bf16).T, ((0, 0), (0, LANES - 2)))
    local_q0 = jnp.concatenate([qkv_low[:, :columns], gain_cols], axis=1)
    up_low = w_up.astype(bf16).reshape(own, ndev, subs, own).transpose(2, 0, 1, 3).reshape(subs, own, D)
    down_low = w_down.astype(bf16).reshape(subs, own, D)
    local_mlp = [v for q in range(subs) for v in (up_low[q], down_low[q])]
    early = jnp.concatenate([qkv_low[:, columns:], w_out.astype(bf16)] + local_mlp[:2], axis=1)
    late = jnp.concatenate(local_mlp[2:], axis=1)
    keep = (jnp.arange(length) < frames[0])[:, None]
    g_low = jnp.where(keep, cotangent[0], jnp.zeros((), bf16))

    flow = Flow(plan)
    step = flow.step
    reach = lambda v: lax.all_gather(v, "fsdp", axis=0, tiled=True)
    early = reach(early)
    flow.gather("q0", reach(local_q0))
    step(None, ["q0"])
    late = reach(late)
    flow.gather("q1", early, 0, columns)
    flow.gather("o", early, columns, D)
    flow.gather("m0", early, columns + D, 2 * D)
    for k in range(1, subs):
        flow.gather(f"m{k}", late, 2 * (k - 1) * D, 2 * D)
    g_low = step(g_low, ["q0"])
    step(None, ["q0"])
    flow.until(None, ["q0"])
    step(None, ["q1", "o", "m0"])
    qkv0, u_one, gains, u_one_t = project_qkv(tab, x, flow.done["q0"], block, columns, True)
    qkv0, u_one = step((qkv0, u_one), ["q1", "o"])
    o0, lse0 = attend(frames, qkv0)
    o0, u_one = step((o0, u_one), ["q1", "o", "m0", "m1"])
    u_one = flow.until(u_one, ["q1"])
    (qkv1,) = project_qkv(tab, u_one, flow.done["q1"], block, columns, False)
    qkv1 = step(qkv1, ["o", "m1", "m2"])
    o1, lse1 = attend(frames, qkv1)
    qkv, o, lse = [qkv0, qkv1], [o0, o1], [lse0, lse1]
    o = step(o, ["o", "m0", "m2"])
    o = flow.until(o, ["o"])
    full_out = flow.done["o"]
    mid, u_two, u_two_t = middle(tab, o, x, gains, full_out, block)
    u_two = step(u_two, ["m0", "m1", "m3"])
    held = [mid, None]
    plans = [["m1", "m2", "m3", "g0"], ["m2", "m3", "g0", "g1"], ["m3", "g0", "g1", "g2"]]
    for k in range(subs):
        u_two = flow.until(u_two, [f"m{k}"])
        last = (mid, gains, o, full_out) if k == subs - 1 else None
        out, held_du, *more, sent, kept = feed_forward(
            tab, u_two, u_two_t, g_low, [flow.done[f"m{k}"]], held, block, k == 0, last
        )
        flow.scatter(f"g{k}", sent, kept)
        if last:
            dmid, (d_o, out_sent, out_kept) = held_du, more
            flow.scatter("go", out_sent, out_kept)
        else:
            held = [out, step(held_du, plans[k])]
    d_o = step(d_o, ["g0", "g1", "g2", "g3", "go"])
    d_o = flow.until(d_o, ["g0"])
    flow.own_rows("g0")
    calls = 4
    per = every // calls
    d_qkv = []
    plans = [
        ["g1", "g2", "g3", "go", "gq0"],
        ["g2", "g3", "go", "gq0", "gq1"],
        ["g3", "go", "gq0", "gq1", "gq2"],
    ]
    for i in range(calls):
        group, at = divmod(i * per, pairs)
        d, sent, kept = attend_back(
            frames, tab, qkv[group], d_o, lse[group], u_one_t, i * per, at, per, block
        )
        d_qkv.append(d)
        flow.scatter(f"gq{i}", sent, kept, True)
        if i < calls - 1:
            d_o = step(d_o, plans[i], [f"g{i - 1}"] if i > 0 else [])
        if i < 2:
            d_o = flow.until(d_o, [f"g{i + 1}"])
            flow.own_rows(f"g{i + 1}")
        elif i == 2:
            some = ["g3", "go", "gq0"]
            d_o = flow.until(d_o, some)
            flow.own_rows("joined", jnp.concatenate([flow.done[n] for n in some], axis=1))
    dmid = step(dmid, ["gq1", "gq2", "gq3"], ["g2"])
    dmid = flow.until(dmid, ["gq1"])
    flow.own_rows("gq1")
    blocks = length // 256
    held_q = [flow.done["q0"], flow.done["q1"]]
    top = input_grad(tab, d_qkv, dmid, x, gains, held_q, block, 0, blocks // 2)
    top, dmid = step((top, dmid), ["gq2", "gq3"])
    grad_in = input_grad(tab, d_qkv, dmid, x, gains, held_q, block, blocks // 2, blocks, (top,))
    grad_in = step(grad_in, ["gq3"], ["joined"])
    flow.until(None, list(flow.live))
    size = per * 3 * LANES
    late_parts = [plan.own_rows(flow.done[f"gq{i}"], True) for i in range(2, calls)]
    arrays = [flow.shards[n] for n in ("joined", "gq1", "g0", "g1", "g2")] + late_parts
    views = [(0, 3 * D, size), (1, 0, size)] + [(5 + i, 0, size) for i in range(calls - 2)]
    views += [(0, 2 * D, D)] + [(2 + k, 0, 2 * D) for k in range(subs - 1)] + [(0, 0, 2 * D)]
    weights = [qkv_low[:, i * size : (i + 1) * size] for i in range(calls)] + list(up_low)
    sums, gain_shard = square_sums(arrays, views, calls, weights, norm_gains, ndev)
    everyone = lax.all_to_all(sums, AXES, 0, 0)
    rates = (0.6 / D**0.5, 0.6 / FANO**0.5, 0.6 / D**0.5, 0.6 / FF**0.5, 1.0)
    decays = (0.1, 0.1, 0.1, 0.1, 0.0)
    states = [(masters[i], firsts[i], seconds[i], shadows[i]) for i in range(5)]
    updated, grad_norm = adam(
        everyone, arrays, views, calls, gain_shard, states, rates, decays
    )
    return (
        out[None],
        grad_in[None],
        grad_norm,
        *(updated[i][part] for part in range(4) for i in range(5)),
    )


def solution(mesh):
    plan = Plan(mesh)
    split = P(AXES, None)
    lanes = P(None, AXES)
    weights = (split, split, split, split, lanes)
    return jax.shard_map(
        functools.partial(body, plan),
        mesh=mesh,
        in_specs=(P(AXES, None, None), P(AXES, None, None), P(AXES)) + weights * 4,
        out_specs=(P(AXES, None, None), P(AXES, None, None), P()) + weights * 4,
        check_vma=False,
    )
```

```python
import functools

import jax
import jax.numpy as jnp
import numpy as np
from jax import lax
from jax.experimental import pallas as pl
from jax.experimental.pallas import tpu as pltpu
from jax.sharding import PartitionSpec as P

D = 1024
HEAD_DIM = 64
FF = 4096
STEP = 7
FANO = 16

NORM_EPS = 1e-06
ADAM_EPS = 1e-08
BETA_ONE = 0.9
BETA_TWO = 0.95
SHADOW_KEEP = 0.8
CLIP_NORM = 1.0

AXES = ("dp", "fsdp")
GROUPS = 2
LANES = 128
VMEM = (64 << 20) - (256 << 10)
f32 = jnp.float32
bf16 = jnp.bfloat16
NT = (((1,), (1,)), ((), ()))
TN = (((0,), (0,)), ((), ()))
GELU_A = 0.7978845608028654
GELU_B = 0.044715


def full(shape, single=False):
    rank = len(shape)
    mode = dict(pipeline_mode=pl.Buffered(1)) if single else {}
    return pl.BlockSpec(shape, lambda *_: (0,) * rank, **mode)


def params():
    return pltpu.CompilerParams(vmem_limit_bytes=VMEM)


def cost(flops, nbytes, trans=0):
    return pl.CostEstimate(flops=flops, bytes_accessed=nbytes, transcendentals=trans)


class Plan:
    def __init__(self, mesh):
        self.ndp, self.nfs = mesh.shape["dp"], mesh.shape["fsdp"]
        self.ndev = self.ndp * self.nfs
        self.bits = self.ndp.bit_length() - 1
        others = list(range(1, self.bits))
        half = len(others) // 2
        self.order = (others, others[half:] + others[:half])
        self.block = D // self.ndp
        tab = np.zeros((self.ndp, self.ndp), np.int32)
        for me in range(self.ndp):
            for rel in range(self.ndp):
                core = (me & 1) ^ (rel >> (self.bits - 1))
                nat = core
                for s, bit in enumerate(self.order[core]):
                    r = (rel >> (self.bits - 2 - s)) & 1
                    nat |= (((me >> bit) & 1) ^ r) << bit
                tab[me, rel] = nat
        self.tab = tab

    def pairs(self, flip):
        out = []
        for d in range(self.ndp):
            for f in range(self.nfs):
                out.append((d * self.nfs + f, flip(d) * self.nfs + f))
        return out

    def core_pairs(self):
        return self.pairs(lambda d: d ^ 1)

    def mix_pairs(self, s):
        return self.pairs(lambda d: d ^ (1 << self.order[d & 1][s]))

    def gather(self, mine):
        for s in reversed(range(self.bits - 1)):
            wide = s == 0
            (got,) = yield [mine], self.mix_pairs(s), None if wide else ("join", mine)
            mine = mine if wide else got
        held = [mine, got]
        return held + (yield held, self.core_pairs(), None)

    def scatter(self, sent, kept):
        pairs = self.core_pairs()
        for s in range(self.bits - 1):
            kept, sent = yield [sent], pairs, ("sum", [kept], [bf16, bf16])
            pairs = self.mix_pairs(s)
        (total,) = yield [sent], pairs, ("sum", [kept], [f32])
        return total

    def scatter_direct(self, sent, kept):
        count = self.ndp // 2
        kept, *sent = yield [sent], self.core_pairs(), ("sum", [kept], [f32] + [bf16] * (count - 1))
        pairs = [None] + [
            self.pairs(lambda d: d ^ self.mask(d & 1, rel)) for rel in range(1, count)
        ]
        (total,) = yield sent, pairs[1:], ("sum", [kept], [f32])
        return total

    def mask(self, core, rel):
        bits = enumerate(self.order[core])
        return sum(((rel >> (self.bits - 2 - s)) & 1) << bit for s, bit in bits)

    def own_rows(self, total, direct=False):
        if not direct or self.nfs > 4:
            return lax.psum_scatter(total, "fsdp", scatter_dimension=0, tiled=True)
        me, rows = lax.axis_index("fsdp"), total.shape[0] // self.nfs
        block = lambda f: lax.dynamic_slice_in_dim(total, f * rows, rows, 0)
        sum_ = block(me)
        for flip in range(1, self.nfs):
            pairs = [(i, i // self.nfs * self.nfs + (i % self.nfs ^ flip)) for i in range(self.ndev)]
            sum_ = sum_ + lax.ppermute(block(me ^ flip), AXES, pairs)
        return sum_


def tie_kernel(count, jobs, *refs):
    sems = refs[-1]
    free = iter(range(sems.shape[0]))
    copy = lambda x, y: pltpu.make_async_copy(x, y, sems.at[next(free)])
    total = count + sum(job["inputs"] for job in jobs)
    made = sum(len(job["outputs"]) for job in jobs)
    inputs, outputs = list(refs[count:total]), list(refs[total + count : total + count + made])
    scratch = list(refs[total + count + made : -1])
    steps = []
    for job in jobs:
        ins = [inputs.pop(0) for _ in range(job["inputs"])]
        outs = [outputs.pop(0) for _ in job["outputs"]]
        if job["kind"] == "cut":
            at, wide = job["cut"]
            held = scratch.pop(0)
            steps.append(([copy(ins[0].at[:, pl.ds(at, wide)], held)], None, copy(held, outs[0])))
        elif job["kind"] == "join":
            held = scratch.pop(0)
            rows = ins[0].shape[0]
            loads = [copy(v, held.at[pl.ds(i * rows, rows)]) for i, v in enumerate(ins)]
            steps.append((loads, None, copy(held, outs[0])))
        else:
            rows = outs[0].shape[0]
            for i, out in reversed(list(enumerate(outs))):
                held = [scratch.pop(0) for _ in range(len(ins) + 1)]
                loads = [copy(v.at[pl.ds(i * rows, rows)], h) for v, h in zip(ins, held)]
                steps.append((loads, held, copy(held[-1], out)))
    for loads, _, _ in steps:
        for c in loads:
            c.start()
    for loads, held, save in steps:
        for c in loads:
            c.wait()
        if held:
            total = held[0][...].astype(f32)
            for h in held[1:-1]:
                total = total + h[...].astype(f32)
            held[-1][...] = total.astype(held[-1].dtype)
        save.start()
    for _, _, save in steps:
        save.wait()


def tie(same, work=()):
    leaves, form = jax.tree.flatten(same)
    place = pl.BlockSpec(memory_space=pl.ANY)
    count = len(leaves)
    jobs, inputs, made, scratch, copies = [], list(leaves), [], [], 1
    shape = lambda dims, kind: jax.ShapeDtypeStruct(dims, kind)
    for kind, *rest in work:
        if kind == "cut":
            v, at, wide = rest
            arrays, outs = [v], [shape((v.shape[0], wide), v.dtype)]
            scratch.append(outs[0])
            copies += 2
        elif kind == "join":
            arrays = rest
            outs = [shape((2 * rest[0].shape[0], rest[0].shape[1]), rest[0].dtype)]
            scratch.append(outs[0])
            copies += 3
        else:
            arrays, kinds = rest
            rows = arrays[0].shape[0] // len(kinds)
            outs = [shape((rows, arrays[0].shape[1]), k) for k in kinds]
            for out in reversed(outs):
                scratch += [shape(out.shape, v.dtype) for v in arrays] + [out]
            copies += (len(arrays) + 1) * len(outs)
        inputs += arrays
        made.append(outs)
        jobs.append(dict(kind=kind, inputs=len(arrays), outputs=outs, cut=tuple(rest[1:3]) if kind == "cut" else None))
    if not inputs:
        return same, []
    outputs = [shape(v.shape, v.dtype) for v in leaves] + [v for outs in made for v in outs]
    out = list(
        pl.pallas_call(
            functools.partial(tie_kernel, count, jobs),
            in_specs=[place] * len(inputs),
            out_specs=[place] * len(outputs),
            out_shape=outputs,
            scratch_shapes=[pltpu.VMEM(v.shape, v.dtype) for v in scratch]
            + [pltpu.SemaphoreType.DMA((copies,))],
            input_output_aliases={i: i for i in range(count)},
            compiler_params=params(),
            name="tie",
        )(*inputs)
    )
    same, out = jax.tree.unflatten(form, out[:count]), out[count:]
    return same, [[out.pop(0) for _ in outs] for outs in made]


class Flow:
    def __init__(self, plan):
        self.plan = plan
        self.live, self.flying, self.done, self.waiting, self.shards = {}, {}, {}, {}, {}

    def gather(self, name, array, at=None, wide=None):
        self.waiting[name] = (array, at, wide)

    def scatter(self, name, sent, kept, direct=False):
        way = self.plan.scatter_direct if direct else self.plan.scatter
        self.live[name] = way(sent, kept)

    def own_rows(self, name, total=None):
        self.shards[name] = self.plan.own_rows(self.done[name] if total is None else total)

    def step(self, x, names, pinned=()):
        names = [n for n in names if n not in self.done]
        came = {n: self.flying.pop(n) for n in names if n in self.flying}
        start = {n: self.waiting.pop(n) for n in names if n in self.waiting}
        plain = {n: got for n, (got, merge) in came.items() if merge is None}
        whole = {n: v for n, (v, at, _) in start.items() if at is None}
        work = {}
        for n, (got, merge) in came.items():
            if merge and merge[0] == "join":
                work[n] = ("join", merge[1], *got)
            elif merge:
                work[n] = ("sum", merge[1] + got, merge[2])
        work |= {n: ("cut", *v) for n, v in start.items() if v[1] is not None}
        held = {n: self.shards[n] for n in pinned}
        (x, plain, whole, held), made = tie((x, plain, whole, held), list(work.values()))
        self.shards |= held
        made = dict(zip(work, made))
        for n in start:
            self.live[n] = self.plan.gather(whole[n] if n in whole else made[n][0])
        for n in names:
            value = None if n in start else plain.get(n, made.get(n))
            try:
                sent, pairs, merge = self.live[n].send(value)
                each = pairs if isinstance(pairs[0], list) else [pairs] * len(sent)
                self.flying[n] = ([lax.ppermute(v, AXES, p) for v, p in zip(sent, each)], merge)
            except StopIteration as stop:
                self.done[n] = stop.value
        return x

    def until(self, x, names):
        while any(n not in self.done for n in names):
            x = self.step(x, names)
        return x


def natural(dst, cols, pieces, src_cols, tab, block):
    j = 0
    for piece in pieces:
        for i in range(piece.shape[0] // block):
            row = pl.multiple_of(tab[j] * block, block)
            dst[pl.ds(row, block), cols] = piece[i * block : (i + 1) * block, src_cols]
            j += 1


def relative(sent, kept, cols, src, src_cols, tab, block):
    half = src.shape[0] // block // 2
    for j in range(2 * half):
        row = pl.multiple_of(tab[j] * block, block)
        out = kept if j < half else sent
        i = j % half
        out[i * block : (i + 1) * block, cols] = src[pl.ds(row, block), src_cols]


def qkv_kernel(count, block, first, tab, *refs):
    if first:
        x_ref, refs = refs[0], refs[1:]
        gains, weights = refs[:count], refs[count : 2 * count]
        qkv_ref, u_ref, gain_ref, u_t_ref, w_nat, g_nat = refs[2 * count :]

        @pl.when(pl.program_id(0) == 0)
        def _():
            natural(g_nat, slice(None), gains, slice(None), tab, block)
            rows = g_nat[...].astype(f32).T
            gain_ref[...] = rows[:8]
            x = x_ref[...].astype(f32)
            r = lax.rsqrt(jnp.mean(x * x, axis=1, keepdims=True) + NORM_EPS)
            u = (x * r * rows[0:1]).astype(bf16)
            u_ref[...] = u
            u_t_ref[...] = u.T

    else:
        u_ref, weights, (qkv_ref, w_nat) = refs[0], refs[1 : 1 + count], refs[1 + count :]
    natural(w_nat, slice(None), weights, slice(None), tab, block)
    qkv_ref[...] = jnp.dot(u_ref[...], w_nat[...], preferred_element_type=f32).astype(bf16)


def project_qkv(tab, x, pieces, block, columns, first):
    length, width = x.shape
    wide = 512
    last = columns // LANES
    col = pl.BlockSpec((length, wide), lambda j, t: (0, j))
    extra = first * [full((length, width)), full((8, width)), full((width, length))]
    shapes = first * [
        jax.ShapeDtypeStruct((length, width), bf16),
        jax.ShapeDtypeStruct((8, width), f32),
        jax.ShapeDtypeStruct((width, length), bf16),
    ]
    gains = first * [pl.BlockSpec((p.shape[0], LANES), lambda j, t: (0, last)) for p in pieces]
    return pl.pallas_call(
        functools.partial(qkv_kernel, len(pieces), block, first),
        grid_spec=pltpu.PrefetchScalarGridSpec(
            num_scalar_prefetch=1,
            grid=(columns // wide,),
            in_specs=[full((length, width), True)]
            + gains
            + [pl.BlockSpec((p.shape[0], wide), lambda j, t: (0, j)) for p in pieces],
            out_specs=[col] + extra,
            scratch_shapes=[pltpu.VMEM((width, wide), bf16)]
            + first * [pltpu.VMEM((width, LANES), bf16)],
        ),
        out_shape=[jax.ShapeDtypeStruct((length, columns), bf16)] + shapes,
        compiler_params=params(),
        cost_estimate=cost(2 * length * width * columns, 20 << 20),
        name="qkv",
    )(tab, x, *(first * pieces), *pieces)


def fold(v, op):
    v = v.reshape(v.shape[0] // 64, 64, v.shape[1])
    return op(op(v, axis=0), axis=0, keepdims=True)


def attend_kernel(rows_of, n_ref, q_ref, k_ref, v_ref, o_ref, lse_ref):
    n = n_ref[0]
    length = q_ref.shape[0]
    lane = lax.broadcasted_iota(jnp.int32, (1, LANES), 1)
    masks = [(lane < HEAD_DIM).astype(bf16), (lane >= HEAD_DIM).astype(bf16)]
    v_t = v_ref[...].T
    for i in range(length // rows_of):
        rows = pl.ds(i * rows_of, rows_of)
        keys = (i + 1) * rows_of

        def run(limited):
            q = q_ref[rows, :] * bf16(HEAD_DIM**-0.5)
            k = k_ref[0:keys, :]
            parts = []
            for h in range(2):
                s = lax.dot_general(k, q * masks[h], NT, preferred_element_type=f32)
                if limited:
                    key = lax.broadcasted_iota(jnp.int32, (keys, rows_of), 0)
                    query = lax.broadcasted_iota(jnp.int32, (keys, rows_of), 1) + i * rows_of
                    s = jnp.where((key <= query) & (key < n), s, -1e30)
                else:
                    key = lax.broadcasted_iota(jnp.int32, (rows_of, rows_of), 0)
                    query = lax.broadcasted_iota(jnp.int32, (rows_of, rows_of), 1)
                    tail = jnp.where(key <= query, s[keys - rows_of :], -1e30)
                    s = tail if i == 0 else jnp.concatenate([s[: keys - rows_of], tail], axis=0)
                peak = fold(s, jnp.max)
                e = jnp.exp(s - peak)
                total = fold(e, jnp.sum)
                p = (e * (1.0 / total)).astype(bf16)
                v_h = v_t[h * HEAD_DIM : (h + 1) * HEAD_DIM, 0:keys]
                parts.append(jnp.dot(v_h, p, preferred_element_type=f32))
                query = lax.broadcasted_iota(jnp.int32, (1, rows_of), 1) + i * rows_of
                lse_ref[0, h : h + 1, rows] = jnp.where(query < n, peak + jnp.log(total), 1e30)
            o_ref[rows, :] = jnp.concatenate(parts, axis=0).astype(bf16).T

        @pl.when(n >= keys)
        def _():
            run(False)

        @pl.when(n < keys)
        def _():
            run(True)


def attend(frames, qkv):
    length, width = qkv.shape[0], qkv.shape[1] // 3
    pairs = width // LANES
    part = lambda c: pl.BlockSpec((length, LANES), lambda j, n: (0, 3 * j + c))
    return pl.pallas_call(
        functools.partial(attend_kernel, 512),
        grid_spec=pltpu.PrefetchScalarGridSpec(
            num_scalar_prefetch=1,
            grid=(pairs,),
            in_specs=[part(0), part(1), part(2)],
            out_specs=[
                pl.BlockSpec((length, LANES), lambda j, n: (0, j)),
                pl.BlockSpec((1, 2, length), lambda j, n: (j, 0, 0)),
            ],
        ),
        out_shape=[
            jax.ShapeDtypeStruct((length, width), bf16),
            jax.ShapeDtypeStruct((pairs, 2, length), f32),
        ],
        compiler_params=params(),
        cost_estimate=cost(16 * length * length * width, 8 << 20, length * length * 16),
        name="attend",
    )(frames, qkv, qkv, qkv)


def mid_kernel(count, groups, block, tab, x_ref, gain_ref, *refs):
    o_refs, refs = refs[:groups], refs[groups:]
    weights = refs[:count]
    mid_ref, u_ref, u_t_ref, w_nat = refs[count:]

    @pl.when(pl.program_id(0) == 0)
    def _():
        natural(w_nat, slice(None), weights, slice(None), tab, block)

    o = jnp.concatenate([ref[...] for ref in o_refs], axis=1)
    mid = x_ref[...].astype(f32) + jnp.dot(o, w_nat[...], preferred_element_type=f32)
    r = lax.rsqrt(jnp.mean(mid * mid, axis=1, keepdims=True) + NORM_EPS)
    u = (mid * r * gain_ref[1:2, :]).astype(bf16)
    mid_ref[...] = mid
    u_ref[...] = u
    u_t_ref[...] = u.T


def middle(tab, o, x, gains, pieces, block):
    length, width = x.shape
    rows = 256
    row = pl.BlockSpec((rows, width), lambda i, t: (i, 0))
    return pl.pallas_call(
        functools.partial(mid_kernel, len(pieces), len(o), block),
        grid_spec=pltpu.PrefetchScalarGridSpec(
            num_scalar_prefetch=1,
            grid=(length // rows,),
            in_specs=[row, full((8, width))]
            + [pl.BlockSpec((rows, v.shape[1]), lambda i, t: (i, 0)) for v in o]
            + [full(p.shape) for p in pieces],
            out_specs=[row, row, pl.BlockSpec((width, rows), lambda i, t: (0, i))],
            scratch_shapes=[pltpu.VMEM((width, width), bf16)],
        ),
        out_shape=[
            jax.ShapeDtypeStruct((length, width), f32),
            jax.ShapeDtypeStruct((length, width), bf16),
            jax.ShapeDtypeStruct((width, length), bf16),
        ],
        compiler_params=params(),
        cost_estimate=cost(2 * length * width * width, 16 << 20),
        name="middle",
    )(tab, x, gains, *o, *pieces)


def gelu_both(z):
    sq = z * z
    t = jnp.tanh(z * (GELU_A + (GELU_A * GELU_B) * sq))
    half = 0.5 + 0.5 * t
    slope = half + (0.5 * z) * (1.0 - t * t) * (GELU_A + (3 * GELU_A * GELU_B) * sq)
    return z * half, slope


def norm_back(v, gain, du):
    r = lax.rsqrt(jnp.mean(v * v, axis=1, keepdims=True) + NORM_EPS)
    up = du * gain
    return r * up - v * (r * r * r * jnp.mean(up * v, axis=1, keepdims=True))


def mlp_kernel(counts, block, first, last, outs, tab, *refs):
    refs = list(refs)
    take = lambda n: [refs.pop(0) for _ in range(n)]
    u_hbm, u_t_hbm, g_hbm = take(3)
    pieces = [take(count) for count in counts]
    (held_out,) = take(1)
    held_du = None if first else take(1)[0]
    if last:
        mid_hbm, gain_hbm = take(2)
        o_hbm, w_hbm = take(outs[0]), take(outs[1])
    (out_hbm,) = take(1)
    if last:
        dmid_hbm, do_hbm = take(2)
    else:
        (du_hbm,) = take(1)
    sent, kept = take(2)
    u, u_t, g, up_s, down_s, out_acc, du_acc, a_s, dz_s, grad, low, gain, sems = refs
    length, width = u.shape
    wide = 512
    halves = width // wide
    blocks = width // block
    subs = len(counts)
    free = iter(range(sems.shape[0]))

    def copy(src, dst):
        return pltpu.make_async_copy(src, dst, sems.at[next(free)])

    def rows(held, at, columns, dst, dst_columns):
        out, j = [], 0
        for piece in held:
            for i in range(piece.shape[0] // block):
                row = pl.multiple_of(tab[j] * block, block)
                src = piece.at[pl.ds(i * block, block), pl.ds(at, columns)]
                out.append(copy(src, dst.at[pl.ds(row, block), dst_columns]))
                j += 1
        return out

    def back(columns, sent_to, kept_to, at):
        out = []
        for j in range(blocks):
            row = pl.multiple_of(tab[j] * block, block)
            to = kept_to if j < blocks // 2 else sent_to
            dst = to.at[pl.ds(j % (blocks // 2) * block, block), pl.ds(at, columns)]
            out.append(copy(grad.at[pl.ds(row, block), pl.ds(0, columns)], dst))
        return out

    def start(copies):
        for c in copies:
            c.start()

    def wait(copies):
        for c in copies:
            c.wait()

    get_u, get_g, get_t = [copy(u_hbm, u)], [copy(g_hbm, g)], [copy(u_t_hbm, u_t)]
    get_up = [
        [rows(pieces[i], f * wide, wide, up_s.at[i], pl.ds(f * wide, wide)) for f in range(halves)]
        for i in range(subs)
    ]
    get_down = [rows(pieces[i], width, width, down_s.at[i], pl.ds(0, width)) for i in range(subs)]
    get_acc = [copy(held_out, out_acc)] + ([] if first else [copy(held_du, du_acc)])
    start(get_u + get_up[0][0] + get_g + get_down[0] + get_t)
    for f in range(1, halves):
        start(get_up[0][f])
    start(get_acc)
    for i in range(1, subs):
        start(sum(get_up[i], []) + get_down[i])
    waiting, saved = [], []
    half = length // 2
    for i in range(subs):
        up, down = up_s.at[i], down_s.at[i]
        final = i == subs - 1
        for f in range(halves):
            cols = slice(f * wide, (f + 1) * wide)
            wait((get_u if i + f == 0 else []) + get_up[i][f])
            z = jnp.dot(u[...], up[:, cols], preferred_element_type=f32)
            a, slope = gelu_both(z)
            if f == 0:
                wait((get_g if i == 0 else []) + get_down[i])
            da = lax.dot_general(g[...], down[cols, :], NT, preferred_element_type=f32)
            a_s[:, cols] = a.astype(bf16)
            dz_s[:, cols] = (da * slope).astype(bf16)
            if f == 0:
                wait((get_t if i == 0 else []) + waiting)
            part = jnp.dot(u_t[...], dz_s[:, cols], preferred_element_type=f32)
            grad[:, cols] = part.astype(bf16)
            turned = lax.dot_general(a_s[:, cols], g[...], TN, preferred_element_type=f32)
            grad[cols, width:] = turned.astype(bf16)
        waiting = back(2 * width, sent, kept, 2 * i * width)
        start(waiting)
        if i == 0:
            wait(get_acc)
        for r in range(2):
            part = pl.ds(r * half, half)
            out = out_acc[part, :] + jnp.dot(a_s[part, :], down[...], preferred_element_type=f32)
            if last and final:
                low[part, :] = out.astype(bf16)
                saved.append(copy(low.at[part], out_hbm.at[part]))
                saved[-1].start()
            else:
                out_acc[part, :] = out
                if final:
                    saved.append(copy(out_acc.at[part], out_hbm.at[part]))
                    saved[-1].start()
        if last and final:
            get_w = rows(w_hbm, 0, width, down, pl.ds(0, width)) + [copy(gain_hbm, gain)]
            start(get_w)
            get_mid = [copy(mid_hbm, out_acc)]
            at = 0
            for o in o_hbm:
                get_mid.append(copy(o, a_s.at[:, pl.ds(at, o.shape[1])]))
                at += o.shape[1]
            start(get_mid)
        for r in range(2):
            part = pl.ds(r * half, half)
            du = lax.dot_general(dz_s[part, :], up[...], NT, preferred_element_type=f32)
            du_acc[part, :] = du if first and i == 0 else du_acc[part, :] + du
            if final and not last:
                saved.append(copy(du_acc.at[part], du_hbm.at[part]))
                saved[-1].start()
    if last:
        wait(get_w + get_mid)
        size = 256
        for r in range(length // size):
            part = pl.ds(r * size, size)
            dmid = g[part, :].astype(f32) + norm_back(out_acc[part, :], gain[1:2, :], du_acc[part, :])
            du_acc[part, :] = dmid
            u[part, :] = dmid.astype(bf16)
            saved.append(copy(du_acc.at[part], dmid_hbm.at[part]))
            saved[-1].start()
            do = lax.dot_general(u[part, :], down_s[subs - 1], NT, preferred_element_type=f32)
            dz_s[part, :] = do.astype(bf16)
            saved.append(copy(dz_s.at[part], do_hbm.at[part]))
            saved[-1].start()
        wait(waiting)
        turned = lax.dot_general(a_s[...], u[...], TN, preferred_element_type=f32)
        grad[:, 0:width] = turned.astype(bf16)
        waiting = back(width, sent, kept, 2 * subs * width)
        start(waiting)
    wait(waiting + saved)


def feed_forward(tab, u, u_t, g, pieces, held, block, first, last=None):
    length, width = u.shape
    half = width // 2
    anywhere = pl.BlockSpec(memory_space=pl.ANY)
    held = held[:1] if first else held
    inputs = [u, u_t, g, *[p for group in pieces for p in group], *held]
    acc = jax.ShapeDtypeStruct((length, width), f32)
    low = jax.ShapeDtypeStruct((length, width), bf16)
    shard = lambda w: jax.ShapeDtypeStruct((half, w), bf16)
    alias, outs = {}, (0, 0)
    if last:
        mid, gains, o, w_out = last
        inputs += [mid, gains, *o, *w_out]
        outputs = [low, acc, low]
        outs = (len(o), len(w_out))
    else:
        outputs = [acc, acc]
    outputs += [shard(2 * width * len(pieces) + (width if last else 0))] * 2
    blocks = width // block
    subs = len(pieces)
    return pl.pallas_call(
        functools.partial(mlp_kernel, [len(p) for p in pieces], block, first, last is not None, outs),
        grid_spec=pltpu.PrefetchScalarGridSpec(
            num_scalar_prefetch=1,
            grid=(1,),
            in_specs=[anywhere] * len(inputs),
            out_specs=[anywhere] * len(outputs),
            scratch_shapes=[
                pltpu.VMEM((length, width), bf16),
                pltpu.VMEM((width, length), bf16),
                pltpu.VMEM((length, width), bf16),
                pltpu.VMEM((subs, width, width), bf16),
                pltpu.VMEM((subs, width, width), bf16),
                pltpu.VMEM((length, width), f32),
                pltpu.VMEM((length, width), f32),
                pltpu.VMEM((length, width), bf16),
                pltpu.VMEM((length, width), bf16),
                pltpu.VMEM((width, 2 * width), bf16),
                pltpu.VMEM((length, width) if last else (16, LANES), bf16),
                pltpu.VMEM((8, width), f32),
                pltpu.SemaphoreType.DMA(((4 * subs + 2) * blocks + 32,)),
            ],
        ),
        out_shape=outputs,
        input_output_aliases=alias,
        compiler_params=params(),
        cost_estimate=cost((12 * subs + 4 * outs[0]) * length * width * width, 48 << 20),
        name="feed_forward",
    )(tab, *inputs)


def attend_back_kernel(
    rows_of, block, n_ref, tab, q_ref, k_ref, v_ref, g_ref, lse_ref, u_t_ref, d_ref, sent, kept, dk, dv, d_s, grad
):
    n = n_ref[0]
    length = q_ref.shape[0]
    scale = HEAD_DIM**-0.5
    lane = lax.broadcasted_iota(jnp.int32, (1, LANES), 1)
    masks = [(lane < HEAD_DIM).astype(bf16), (lane >= HEAD_DIM).astype(bf16)]
    dk[...] = jnp.zeros_like(dk)
    dv[...] = jnp.zeros_like(dv)
    for i in range(length // rows_of):
        rows = pl.ds(i * rows_of, rows_of)
        keys = (i + 1) * rows_of

        @pl.when(n > i * rows_of)
        def _():
            q = q_ref[rows, :] * bf16(scale)
            g = g_ref[rows, :]
            k, v = k_ref[0:keys, :], v_ref[0:keys, :]
            dq = None
            for h in range(2):
                q_h, g_h, k_h = q * masks[h], g * masks[h], k * masks[h]
                s = lax.dot_general(k, q_h, NT, preferred_element_type=f32)
                key = lax.broadcasted_iota(jnp.int32, (rows_of, rows_of), 0)
                query = lax.broadcasted_iota(jnp.int32, (rows_of, rows_of), 1)
                tail = jnp.where(key <= query, s[keys - rows_of :], -1e30)
                s = tail if i == 0 else jnp.concatenate([s[: keys - rows_of], tail], axis=0)
                p = jnp.exp(s - lse_ref[0, h : h + 1, rows])
                dp = lax.dot_general(v, g_h, NT, preferred_element_type=f32)
                delta = fold(p * dp, jnp.sum)
                ds = (p * (dp - delta)).astype(bf16)
                dv[0:keys, :] += jnp.dot(p.astype(bf16), g_h, preferred_element_type=f32)
                dk[0:keys, :] += jnp.dot(ds, q_h, preferred_element_type=f32)
                part = lax.dot_general(ds, k_h, TN, preferred_element_type=f32)
                dq = part if dq is None else dq + part
            d_s[rows, 0:LANES] = (dq * scale).astype(bf16)

        @pl.when(n <= i * rows_of)
        def _():
            d_s[rows, 0:LANES] = jnp.zeros((rows_of, LANES), bf16)

    d_s[:, LANES : 2 * LANES] = dk[...].astype(bf16)
    d_s[:, 2 * LANES :] = dv[...].astype(bf16)
    d_ref[...] = d_s[...]
    grad[...] = jnp.dot(u_t_ref[...], d_s[...], preferred_element_type=f32)
    relative(sent, kept, slice(None), grad, slice(None), tab, block)


def attend_back(frames, tab, qkv, g, lse, u_t, first, at, pairs, block):
    length, width = qkv.shape[0], u_t.shape[0]
    wide = 3 * LANES
    part = lambda c: pl.BlockSpec((length, LANES), lambda j, n, t: (0, 3 * (j + at) + c))
    half = width // 2
    out = pl.BlockSpec((half, wide), lambda j, n, t: (0, j))
    shape = jax.ShapeDtypeStruct((half, pairs * wide), f32)
    return pl.pallas_call(
        functools.partial(attend_back_kernel, 256, block),
        grid_spec=pltpu.PrefetchScalarGridSpec(
            num_scalar_prefetch=2,
            grid=(pairs,),
            in_specs=[
                part(0),
                part(1),
                part(2),
                pl.BlockSpec((length, LANES), lambda j, n, t: (0, j + first)),
                pl.BlockSpec((1, 2, length), lambda j, n, t: (j + at, 0, 0)),
                full((width, length), True),
            ],
            out_specs=[pl.BlockSpec((length, wide), lambda j, n, t: (0, j)), out, out],
            scratch_shapes=[
                pltpu.VMEM((length, LANES), f32),
                pltpu.VMEM((length, LANES), f32),
                pltpu.VMEM((length, wide), bf16),
                pltpu.VMEM((width, wide), f32),
            ],
        ),
        out_shape=[jax.ShapeDtypeStruct((length, pairs * wide), bf16), shape, shape],
        compiler_params=params(),
        cost_estimate=cost(40 * length * length * pairs * LANES, 16 << 20, length * length * 2 * pairs),
        name="attend_back",
    )(frames, tab, qkv, qkv, qkv, g, lse, u_t)


def input_grad_kernel(groups, parts, more, block, tab, dmid_ref, x_ref, gain_ref, *refs):
    refs = refs[more:]
    d_refs, refs = refs[:parts], refs[parts:]
    weights, out_ref, nats = refs[: -1 - groups], refs[-1 - groups], refs[-groups:]
    count = len(weights) // groups

    @pl.when(pl.program_id(0) == 0)
    def _():
        for i, nat in enumerate(nats):
            natural(nat, slice(None), weights[i * count : (i + 1) * count], slice(None), tab, block)

    du = None
    for i, nat in enumerate(nats):
        mine = d_refs[i * parts // groups : (i + 1) * parts // groups]
        d = jnp.concatenate([ref[...] for ref in mine], axis=1)
        part = lax.dot_general(d, nat[...], NT, preferred_element_type=f32)
        du = part if du is None else du + part
    out_ref[...] = dmid_ref[...] + norm_back(x_ref[...].astype(f32), gain_ref[0:1, :], du)


def input_grad(tab, d, dmid, x, gains, pieces, block, lo, hi, done=()):
    length, width = x.shape
    rows = 256
    groups = len(pieces)
    columns = 3 * width // groups
    row = lambda w: pl.BlockSpec((rows, w), lambda i, t: (i + lo, 0))
    weights = [
        pl.BlockSpec((p.shape[0], columns), lambda i, t: (0, 0), pipeline_mode=pl.Buffered(1))
        for group in pieces
        for p in group
    ]
    return pl.pallas_call(
        functools.partial(input_grad_kernel, groups, len(d), len(done), block),
        grid_spec=pltpu.PrefetchScalarGridSpec(
            num_scalar_prefetch=1,
            grid=(hi - lo,),
            in_specs=[row(width), row(width), full((8, width))]
            + [pl.BlockSpec(memory_space=pl.ANY)] * len(done)
            + [row(v.shape[1]) for v in d]
            + weights,
            out_specs=row(width),
            scratch_shapes=[pltpu.VMEM((width, columns), bf16)] * groups,
        ),
        out_shape=jax.ShapeDtypeStruct((length, width), f32),
        input_output_aliases={4: 0} if done else {},
        compiler_params=params(),
        cost_estimate=cost(6 * length * width * width * (hi - lo) // 4, 22 << 20),
        name="input_grad",
    )(tab, dmid, x, gains, *done, *d, *[p for group in pieces for p in group])


def adam_step(weight, first, second, gradient, clip_factor, step_rate, decay_rate, shadow):
    clipped = gradient * clip_factor
    first_new = BETA_ONE * first + (1.0 - BETA_ONE) * clipped
    second_new = BETA_TWO * second + (1.0 - BETA_TWO) * clipped * clipped
    first_hat = first_new / (1.0 - BETA_ONE**STEP)
    second_hat = second_new / (1.0 - BETA_TWO**STEP)
    weight_new = weight - step_rate * (
        first_hat / (jnp.sqrt(second_hat) + ADAM_EPS) + decay_rate * weight
    )
    shadow_new = SHADOW_KEEP * shadow + (1.0 - SHADOW_KEEP) * weight_new
    return (weight_new, first_new, second_new, shadow_new)


def square(v):
    return jnp.sum(v * v)


def view(refs, views, i, lo=0, hi=None):
    array, at, width = views[i]
    return refs[array][:, at + lo : at + (width if hi is None else hi)].astype(f32)


def norm_kernel(arrays, views, parts, *refs):
    grads, rest = refs[:arrays], refs[arrays:]
    weights, (gains, everyone, gain_grad) = rest[:-3], rest[-3:]
    rows, width = gains.shape[1], D
    one = two = jnp.zeros((rows, 1), f32)
    total = square(view(grads, views, parts))
    for i in range(parts):
        grad = view(grads, views, i)
        total = total + square(grad)
        one = one + jnp.sum(weights[i][...].astype(f32) * grad, axis=1, keepdims=True)
    for i in range(len(views) - parts - 1):
        grad = view(grads, views, parts + 1 + i)
        total = total + square(grad)
        up = weights[parts + i][...].astype(f32) * grad[:, :width]
        two = two + jnp.sum(up, axis=1, keepdims=True)
    lane = lax.broadcasted_iota(jnp.int32, (rows, LANES), 1)
    both = jnp.where(lane == 0, one, two)
    both = both.T[0:2, :] / gains[...].astype(bf16).astype(f32)
    gain_grad[...] = both
    everyone[...] = jnp.broadcast_to(total + square(both), everyone.shape)


def square_sums(arrays, views, parts, weights, gains, ndev):
    place = pl.BlockSpec(memory_space=pltpu.VMEM)
    inputs = [*arrays, *weights, gains]
    return pl.pallas_call(
        functools.partial(norm_kernel, len(arrays), views, parts),
        in_specs=[place] * len(inputs),
        out_specs=[place] * 2,
        out_shape=[
            jax.ShapeDtypeStruct((ndev, 1, LANES), f32),
            jax.ShapeDtypeStruct(gains.shape, f32),
        ],
        compiler_params=params(),
        name="square_sums",
    )(*inputs)


def adam_kernel(arrays, views, parts, rates, decays, sums_ref, *refs):
    grads, gain_grad, refs = refs[:arrays], refs[arrays], refs[arrays + 1 :]
    states, outs = refs[:20], refs[20:]
    norm = jnp.sqrt(jnp.sum(sums_ref[...], axis=0))
    outs[20][...] = norm
    clip = jnp.minimum(1.0, CLIP_NORM / norm[:, 0:1])

    def update(i, rows, cols, grad):
        w, m, v, s = [states[4 * i + k][rows, cols] for k in range(4)]
        new = adam_step(w, m, v, grad, clip, rates[i], decays[i], s)
        for k in range(4):
            outs[4 * i + k][rows, cols] = new[k]

    every = slice(None)
    col = 0
    for p in range(parts):
        for j in range(views[p][2] // (3 * LANES)):
            for c in range(3):
                at = c * D + col * LANES
                src = (3 * j + c) * LANES
                update(0, every, slice(at, at + LANES), view(grads, views, p, src, src + LANES))
            col += 1
    update(1, every, every, view(grads, views, parts))
    own = states[0].shape[0]
    subs = FF // D
    size = subs * own
    for at in range(0, FF, LANES):
        pieces = [
            view(grads, views, parts + 1 + q, dev * own, (dev + 1) * own)
            for dev in range(at // size, (at + LANES) // size)
            for q in range(subs)
        ]
        update(2, every, slice(at, at + LANES), jnp.concatenate(pieces, axis=1))
    for q in range(subs):
        grad = view(grads, views, parts + 1 + q, D, 2 * D)
        update(3, slice(q * own, (q + 1) * own), every, grad)
    update(4, every, every, gain_grad[...])


def adam(sums, arrays, views, parts, gain, states, rates, decays):
    place = pl.BlockSpec(memory_space=pltpu.VMEM)
    inputs = [sums, *arrays, gain, *[v for group in states for v in group]]
    outputs = [jax.ShapeDtypeStruct(v.shape, f32) for group in states for v in group]
    outputs.append(jax.ShapeDtypeStruct((1, LANES), f32))
    done = pl.pallas_call(
        functools.partial(adam_kernel, len(arrays), views, parts, rates, decays),
        in_specs=[place] * len(inputs),
        out_specs=[place] * len(outputs),
        out_shape=outputs,
        compiler_params=params(),
        name="adam",
    )(*inputs)
    return [done[4 * i : 4 * i + 4] for i in range(5)], done[-1][0, 0]


def body(plan, *args):
    inputs, cotangent, frames = args[:3]
    masters, firsts, seconds, shadows = args[3:8], args[8:13], args[13:18], args[18:23]
    w_qkv, w_out, w_up, w_down, norm_gains = masters
    block, ndev = plan.block, plan.ndev
    x = inputs[0]
    length = x.shape[0]
    own = D // ndev
    subs = FF // D
    tab = lax.dynamic_index_in_dim(jnp.asarray(plan.tab), lax.axis_index("dp"), 0, keepdims=False)

    wide = D // GROUPS
    pairs = wide // LANES
    columns = 3 * wide
    every = D // LANES
    qkv_low = w_qkv.astype(bf16).reshape(own, 3, every, LANES).transpose(0, 2, 1, 3).reshape(own, 3 * D)
    gain_cols = jnp.pad(norm_gains.astype(bf16).T, ((0, 0), (0, LANES - 2)))
    local_q0 = jnp.concatenate([qkv_low[:, :columns], gain_cols], axis=1)
    up_low = w_up.astype(bf16).reshape(own, ndev, subs, own).transpose(2, 0, 1, 3).reshape(subs, own, D)
    down_low = w_down.astype(bf16).reshape(subs, own, D)
    local_mlp = [v for q in range(subs) for v in (up_low[q], down_low[q])]
    early = jnp.concatenate([qkv_low[:, columns:], w_out.astype(bf16)] + local_mlp[:2], axis=1)
    late = jnp.concatenate(local_mlp[2:], axis=1)
    keep = (jnp.arange(length) < frames[0])[:, None]
    g_low = jnp.where(keep, cotangent[0], jnp.zeros((), bf16))

    flow = Flow(plan)
    step = flow.step
    reach = lambda v: lax.all_gather(v, "fsdp", axis=0, tiled=True)
    early = reach(early)
    flow.gather("q0", reach(local_q0))
    step(None, ["q0"])
    late = reach(late)
    flow.gather("q1", early, 0, columns)
    flow.gather("o", early, columns, D)
    flow.gather("m0", early, columns + D, 2 * D)
    for k in range(1, subs):
        flow.gather(f"m{k}", late, 2 * (k - 1) * D, 2 * D)
    g_low = step(g_low, ["q0"])
    step(None, ["q0"])
    flow.until(None, ["q0"])
    step(None, ["q1", "o", "m0"])
    qkv0, u_one, gains, u_one_t = project_qkv(tab, x, flow.done["q0"], block, columns, True)
    qkv0, u_one = step((qkv0, u_one), ["q1", "o"])
    o0, lse0 = attend(frames, qkv0)
    o0, u_one = step((o0, u_one), ["q1", "o", "m0", "m1"])
    u_one = flow.until(u_one, ["q1"])
    (qkv1,) = project_qkv(tab, u_one, flow.done["q1"], block, columns, False)
    qkv1 = step(qkv1, ["o", "m1", "m2"])
    o1, lse1 = attend(frames, qkv1)
    qkv, o, lse = [qkv0, qkv1], [o0, o1], [lse0, lse1]
    o = step(o, ["o", "m0", "m2"])
    o = flow.until(o, ["o"])
    full_out = flow.done["o"]
    mid, u_two, u_two_t = middle(tab, o, x, gains, full_out, block)
    u_two = step(u_two, ["m0", "m1", "m3"])
    held = [mid, None]
    plans = [["m1", "m2", "m3", "g0"], ["m2", "m3", "g0", "g1"], ["m3", "g0", "g1", "g2"]]
    for k in range(subs):
        u_two = flow.until(u_two, [f"m{k}"])
        last = (mid, gains, o, full_out) if k == subs - 1 else None
        out, held_du, *more, sent, kept = feed_forward(
            tab, u_two, u_two_t, g_low, [flow.done[f"m{k}"]], held, block, k == 0, last
        )
        flow.scatter(f"g{k}", sent, kept)
        if last:
            dmid, (d_o,) = held_du, more
        else:
            held = [out, step(held_du, plans[k])]
    d_o = step(d_o, ["g0", "g1", "g2", "g3"])
    d_o = flow.until(d_o, ["g0"])
    flow.own_rows("g0")
    calls = 4
    per = every // calls
    d_qkv = []
    plans = [
        ["g1", "g2", "g3", "gq0"],
        ["g2", "g3", "gq0", "gq1"],
        ["g3", "gq0", "gq1", "gq2"],
    ]
    for i in range(calls):
        group, at = divmod(i * per, pairs)
        d, sent, kept = attend_back(
            frames, tab, qkv[group], d_o, lse[group], u_one_t, i * per, at, per, block
        )
        d_qkv.append(d)
        flow.scatter(f"gq{i}", sent, kept, True)
        if i < calls - 1:
            d_o = step(d_o, plans[i], [f"g{i - 1}"] if i > 0 else [])
        if i < 2:
            d_o = flow.until(d_o, [f"g{i + 1}"])
            flow.own_rows(f"g{i + 1}")
        elif i == 2:
            some = ["g3", "gq0"]
            d_o = flow.until(d_o, some)
            flow.own_rows("joined", jnp.concatenate([flow.done[n] for n in some], axis=1))
    dmid = step(dmid, ["gq1", "gq2", "gq3"], ["g2"])
    dmid = flow.until(dmid, ["gq1"])
    flow.own_rows("gq1")
    blocks = length // 256
    held_q = [flow.done["q0"], flow.done["q1"]]
    top = input_grad(tab, d_qkv, dmid, x, gains, held_q, block, 0, blocks // 2)
    top, dmid = step((top, dmid), ["gq2", "gq3"])
    grad_in = input_grad(tab, d_qkv, dmid, x, gains, held_q, block, blocks // 2, blocks, (top,))
    grad_in = step(grad_in, ["gq3"], ["joined"])
    flow.until(None, list(flow.live))
    size = per * 3 * LANES
    late_parts = [plan.own_rows(flow.done[f"gq{i}"], True) for i in range(2, calls)]
    arrays = [flow.shards[n] for n in ("joined", "gq1", "g0", "g1", "g2")] + late_parts
    views = [(0, 3 * D, size), (1, 0, size)] + [(5 + i, 0, size) for i in range(calls - 2)]
    views += [(0, 2 * D, D)] + [(2 + k, 0, 2 * D) for k in range(subs - 1)] + [(0, 0, 2 * D)]
    weights = [qkv_low[:, i * size : (i + 1) * size] for i in range(calls)] + list(up_low)
    sums, gain_shard = square_sums(arrays, views, calls, weights, norm_gains, ndev)
    everyone = lax.all_to_all(sums, AXES, 0, 0)
    rates = (0.6 / D**0.5, 0.6 / FANO**0.5, 0.6 / D**0.5, 0.6 / FF**0.5, 1.0)
    decays = (0.1, 0.1, 0.1, 0.1, 0.0)
    states = [(masters[i], firsts[i], seconds[i], shadows[i]) for i in range(5)]
    updated, grad_norm = adam(
        everyone, arrays, views, calls, gain_shard, states, rates, decays
    )
    return (
        out[None],
        grad_in[None],
        grad_norm,
        *(updated[i][part] for part in range(4) for i in range(5)),
    )


def solution(mesh):
    plan = Plan(mesh)
    split = P(AXES, None)
    lanes = P(None, AXES)
    weights = (split, split, split, split, lanes)
    return jax.shard_map(
        functools.partial(body, plan),
        mesh=mesh,
        in_specs=(P(AXES, None, None), P(AXES, None, None), P(AXES)) + weights * 4,
        out_specs=(P(AXES, None, None), P(AXES, None, None), P()) + weights * 4,
        check_vma=False,
    )
```

```python
import functools

import jax
import jax.numpy as jnp
import numpy as np
from jax import lax
from jax.experimental import pallas as pl
from jax.experimental.pallas import tpu as pltpu
from jax.sharding import PartitionSpec as P

D = 1024
HEAD_DIM = 64
FF = 4096
STEP = 7
FANO = 16

NORM_EPS = 1e-06
ADAM_EPS = 1e-08
BETA_ONE = 0.9
BETA_TWO = 0.95
SHADOW_KEEP = 0.8
CLIP_NORM = 1.0

AXES = ("dp", "fsdp")
GROUPS = 2
LANES = 128
VMEM = (64 << 20) - (256 << 10)
f32 = jnp.float32
bf16 = jnp.bfloat16
NT = (((1,), (1,)), ((), ()))
TN = (((0,), (0,)), ((), ()))
GELU_A = 0.7978845608028654
GELU_B = 0.044715


def full(shape, single=False):
    rank = len(shape)
    mode = dict(pipeline_mode=pl.Buffered(1)) if single else {}
    return pl.BlockSpec(shape, lambda *_: (0,) * rank, **mode)


def params():
    return pltpu.CompilerParams(vmem_limit_bytes=VMEM)


def cost(flops, nbytes, trans=0):
    return pl.CostEstimate(flops=flops, bytes_accessed=nbytes, transcendentals=trans)


class Plan:
    def __init__(self, mesh):
        self.ndp, self.nfs = mesh.shape["dp"], mesh.shape["fsdp"]
        self.ndev = self.ndp * self.nfs
        self.bits = self.ndp.bit_length() - 1
        others = list(range(1, self.bits))
        half = len(others) // 2
        self.order = (others, others[half:] + others[:half])
        self.block = D // self.ndp
        tab = np.zeros((self.ndp, self.ndp), np.int32)
        for me in range(self.ndp):
            for rel in range(self.ndp):
                core = (me & 1) ^ (rel >> (self.bits - 1))
                nat = core
                for s, bit in enumerate(self.order[core]):
                    r = (rel >> (self.bits - 2 - s)) & 1
                    nat |= (((me >> bit) & 1) ^ r) << bit
                tab[me, rel] = nat
        self.tab = tab

    def pairs(self, flip):
        out = []
        for d in range(self.ndp):
            for f in range(self.nfs):
                out.append((d * self.nfs + f, flip(d) * self.nfs + f))
        return out

    def core_pairs(self):
        return self.pairs(lambda d: d ^ 1)

    def mix_pairs(self, s):
        return self.pairs(lambda d: d ^ (1 << self.order[d & 1][s]))

    def gather(self, mine):
        for s in reversed(range(self.bits - 1)):
            wide = s == 0
            (got,) = yield [mine], self.mix_pairs(s), None if wide else ("join", mine)
            mine = mine if wide else got
        held = [mine, got]
        return held + (yield held, self.core_pairs(), None)

    def scatter(self, sent, kept, kind=f32):
        pairs = self.core_pairs()
        for s in range(self.bits - 1):
            kept, sent = yield [sent], pairs, ("sum", [kept], [bf16, bf16])
            pairs = self.mix_pairs(s)
        (total,) = yield [sent], pairs, ("sum", [kept], [kind])
        return total

    def scatter_direct(self, sent, kept):
        count = self.ndp // 2
        kept, *sent = yield [sent], self.core_pairs(), ("sum", [kept], [f32] + [bf16] * (count - 1))
        pairs = [None] + [
            self.pairs(lambda d: d ^ self.mask(d & 1, rel)) for rel in range(1, count)
        ]
        (total,) = yield sent, pairs[1:], ("sum", [kept], [f32])
        return total

    def mask(self, core, rel):
        bits = enumerate(self.order[core])
        return sum(((rel >> (self.bits - 2 - s)) & 1) << bit for s, bit in bits)

    def own_rows(self, total, direct=False):
        if not direct or self.nfs > 4:
            return lax.psum_scatter(total, "fsdp", scatter_dimension=0, tiled=True)
        me, rows = lax.axis_index("fsdp"), total.shape[0] // self.nfs
        block = lambda f: lax.dynamic_slice_in_dim(total, f * rows, rows, 0)
        sum_ = block(me)
        for flip in range(1, self.nfs):
            pairs = [(i, i // self.nfs * self.nfs + (i % self.nfs ^ flip)) for i in range(self.ndev)]
            sum_ = sum_ + lax.ppermute(block(me ^ flip), AXES, pairs)
        return sum_


def tie_kernel(count, jobs, *refs):
    sems = refs[-1]
    free = iter(range(sems.shape[0]))
    copy = lambda x, y: pltpu.make_async_copy(x, y, sems.at[next(free)])
    total = count + sum(job["inputs"] for job in jobs)
    made = sum(len(job["outputs"]) for job in jobs)
    inputs, outputs = list(refs[count:total]), list(refs[total + count : total + count + made])
    scratch = list(refs[total + count + made : -1])
    steps = []
    for job in jobs:
        ins = [inputs.pop(0) for _ in range(job["inputs"])]
        outs = [outputs.pop(0) for _ in job["outputs"]]
        if job["kind"] == "cut":
            at, wide = job["cut"]
            held = scratch.pop(0)
            steps.append(([copy(ins[0].at[:, pl.ds(at, wide)], held)], None, copy(held, outs[0])))
        elif job["kind"] == "join":
            held = scratch.pop(0)
            rows = ins[0].shape[0]
            loads = [copy(v, held.at[pl.ds(i * rows, rows)]) for i, v in enumerate(ins)]
            steps.append((loads, None, copy(held, outs[0])))
        else:
            rows = outs[0].shape[0]
            for i, out in reversed(list(enumerate(outs))):
                held = [scratch.pop(0) for _ in range(len(ins) + 1)]
                loads = [copy(v.at[pl.ds(i * rows, rows)], h) for v, h in zip(ins, held)]
                steps.append((loads, held, copy(held[-1], out)))
    for loads, _, _ in steps:
        for c in loads:
            c.start()
    for loads, held, save in steps:
        for c in loads:
            c.wait()
        if held:
            total = held[0][...].astype(f32)
            for h in held[1:-1]:
                total = total + h[...].astype(f32)
            held[-1][...] = total.astype(held[-1].dtype)
        save.start()
    for _, _, save in steps:
        save.wait()


def tie(same, work=()):
    leaves, form = jax.tree.flatten(same)
    place = pl.BlockSpec(memory_space=pl.ANY)
    count = len(leaves)
    jobs, inputs, made, scratch, copies = [], list(leaves), [], [], 1
    shape = lambda dims, kind: jax.ShapeDtypeStruct(dims, kind)
    for kind, *rest in work:
        if kind == "cut":
            v, at, wide = rest
            arrays, outs = [v], [shape((v.shape[0], wide), v.dtype)]
            scratch.append(outs[0])
            copies += 2
        elif kind == "join":
            arrays = rest
            outs = [shape((2 * rest[0].shape[0], rest[0].shape[1]), rest[0].dtype)]
            scratch.append(outs[0])
            copies += 3
        else:
            arrays, kinds = rest
            rows = arrays[0].shape[0] // len(kinds)
            outs = [shape((rows, arrays[0].shape[1]), k) for k in kinds]
            for out in reversed(outs):
                scratch += [shape(out.shape, v.dtype) for v in arrays] + [out]
            copies += (len(arrays) + 1) * len(outs)
        inputs += arrays
        made.append(outs)
        jobs.append(dict(kind=kind, inputs=len(arrays), outputs=outs, cut=tuple(rest[1:3]) if kind == "cut" else None))
    if not inputs:
        return same, []
    outputs = [shape(v.shape, v.dtype) for v in leaves] + [v for outs in made for v in outs]
    out = list(
        pl.pallas_call(
            functools.partial(tie_kernel, count, jobs),
            in_specs=[place] * len(inputs),
            out_specs=[place] * len(outputs),
            out_shape=outputs,
            scratch_shapes=[pltpu.VMEM(v.shape, v.dtype) for v in scratch]
            + [pltpu.SemaphoreType.DMA((copies,))],
            input_output_aliases={i: i for i in range(count)},
            compiler_params=params(),
            name="tie",
        )(*inputs)
    )
    same, out = jax.tree.unflatten(form, out[:count]), out[count:]
    return same, [[out.pop(0) for _ in outs] for outs in made]


class Flow:
    def __init__(self, plan):
        self.plan = plan
        self.live, self.flying, self.done, self.waiting, self.shards = {}, {}, {}, {}, {}

    def gather(self, name, array, at=None, wide=None):
        self.waiting[name] = (array, at, wide)

    def scatter(self, name, sent, kept, direct=False, kind=f32):
        way = self.plan.scatter_direct
        self.live[name] = way(sent, kept) if direct else self.plan.scatter(sent, kept, kind)

    def own_rows(self, name):
        self.shards[name] = self.plan.own_rows(self.done[name])

    def step(self, x, names, pinned=()):
        names = [n for n in names if n not in self.done]
        came = {n: self.flying.pop(n) for n in names if n in self.flying}
        start = {n: self.waiting.pop(n) for n in names if n in self.waiting}
        plain = {n: got for n, (got, merge) in came.items() if merge is None}
        whole = {n: v for n, (v, at, _) in start.items() if at is None}
        work = {}
        for n, (got, merge) in came.items():
            if merge and merge[0] == "join":
                work[n] = ("join", merge[1], *got)
            elif merge:
                work[n] = ("sum", merge[1] + got, merge[2])
        work |= {n: ("cut", *v) for n, v in start.items() if v[1] is not None}
        held = {n: self.shards[n] for n in pinned}
        (x, plain, whole, held), made = tie((x, plain, whole, held), list(work.values()))
        self.shards |= held
        made = dict(zip(work, made))
        for n in start:
            self.live[n] = self.plan.gather(whole[n] if n in whole else made[n][0])
        for n in names:
            value = None if n in start else plain.get(n, made.get(n))
            try:
                sent, pairs, merge = self.live[n].send(value)
                each = pairs if isinstance(pairs[0], list) else [pairs] * len(sent)
                self.flying[n] = ([lax.ppermute(v, AXES, p) for v, p in zip(sent, each)], merge)
            except StopIteration as stop:
                self.done[n] = stop.value
        return x

    def until(self, x, names):
        while any(n not in self.done for n in names):
            x = self.step(x, names)
        return x


def natural(dst, cols, pieces, src_cols, tab, block):
    j = 0
    for piece in pieces:
        for i in range(piece.shape[0] // block):
            row = pl.multiple_of(tab[j] * block, block)
            dst[pl.ds(row, block), cols] = piece[i * block : (i + 1) * block, src_cols]
            j += 1


def relative(sent, kept, cols, src, src_cols, tab, block):
    half = src.shape[0] // block // 2
    for j in range(2 * half):
        row = pl.multiple_of(tab[j] * block, block)
        out = kept if j < half else sent
        i = j % half
        out[i * block : (i + 1) * block, cols] = src[pl.ds(row, block), src_cols]


def qkv_kernel(count, block, first, tab, *refs):
    if first:
        x_ref, refs = refs[0], refs[1:]
        gains, weights = refs[:count], refs[count : 2 * count]
        qkv_ref, u_ref, gain_ref, u_t_ref, w_nat, g_nat = refs[2 * count :]

        @pl.when(pl.program_id(0) == 0)
        def _():
            natural(g_nat, slice(None), gains, slice(None), tab, block)
            rows = g_nat[...].astype(f32).T
            gain_ref[...] = rows[:8]
            x = x_ref[...].astype(f32)
            r = lax.rsqrt(jnp.mean(x * x, axis=1, keepdims=True) + NORM_EPS)
            u = (x * r * rows[0:1]).astype(bf16)
            u_ref[...] = u
            u_t_ref[...] = u.T

    else:
        u_ref, weights, (qkv_ref, w_nat) = refs[0], refs[1 : 1 + count], refs[1 + count :]
    natural(w_nat, slice(None), weights, slice(None), tab, block)
    qkv_ref[...] = jnp.dot(u_ref[...], w_nat[...], preferred_element_type=f32).astype(bf16)


def project_qkv(tab, x, pieces, block, columns, first):
    length, width = x.shape
    wide = 512
    last = columns // LANES
    col = pl.BlockSpec((length, wide), lambda j, t: (0, j))
    extra = first * [full((length, width)), full((8, width)), full((width, length))]
    shapes = first * [
        jax.ShapeDtypeStruct((length, width), bf16),
        jax.ShapeDtypeStruct((8, width), f32),
        jax.ShapeDtypeStruct((width, length), bf16),
    ]
    gains = first * [pl.BlockSpec((p.shape[0], LANES), lambda j, t: (0, last)) for p in pieces]
    return pl.pallas_call(
        functools.partial(qkv_kernel, len(pieces), block, first),
        grid_spec=pltpu.PrefetchScalarGridSpec(
            num_scalar_prefetch=1,
            grid=(columns // wide,),
            in_specs=[full((length, width), True)]
            + gains
            + [pl.BlockSpec((p.shape[0], wide), lambda j, t: (0, j)) for p in pieces],
            out_specs=[col] + extra,
            scratch_shapes=[pltpu.VMEM((width, wide), bf16)]
            + first * [pltpu.VMEM((width, LANES), bf16)],
        ),
        out_shape=[jax.ShapeDtypeStruct((length, columns), bf16)] + shapes,
        compiler_params=params(),
        cost_estimate=cost(2 * length * width * columns, 20 << 20),
        name="qkv",
    )(tab, x, *(first * pieces), *pieces)


def fold(v, op):
    v = v.reshape(v.shape[0] // 64, 64, v.shape[1])
    return op(op(v, axis=0), axis=0, keepdims=True)


def attend_kernel(rows_of, n_ref, q_ref, k_ref, v_ref, o_ref, lse_ref):
    n = n_ref[0]
    length = q_ref.shape[0]
    lane = lax.broadcasted_iota(jnp.int32, (1, LANES), 1)
    masks = [(lane < HEAD_DIM).astype(bf16), (lane >= HEAD_DIM).astype(bf16)]
    v_t = v_ref[...].T
    for i in range(length // rows_of):
        rows = pl.ds(i * rows_of, rows_of)
        keys = (i + 1) * rows_of

        def run(limited):
            q = q_ref[rows, :] * bf16(HEAD_DIM**-0.5)
            k = k_ref[0:keys, :]
            parts = []
            for h in range(2):
                s = lax.dot_general(k, q * masks[h], NT, preferred_element_type=f32)
                if limited:
                    key = lax.broadcasted_iota(jnp.int32, (keys, rows_of), 0)
                    query = lax.broadcasted_iota(jnp.int32, (keys, rows_of), 1) + i * rows_of
                    s = jnp.where((key <= query) & (key < n), s, -1e30)
                else:
                    key = lax.broadcasted_iota(jnp.int32, (rows_of, rows_of), 0)
                    query = lax.broadcasted_iota(jnp.int32, (rows_of, rows_of), 1)
                    tail = jnp.where(key <= query, s[keys - rows_of :], -1e30)
                    s = tail if i == 0 else jnp.concatenate([s[: keys - rows_of], tail], axis=0)
                peak = fold(s, jnp.max)
                e = jnp.exp(s - peak)
                total = fold(e, jnp.sum)
                p = (e * (1.0 / total)).astype(bf16)
                v_h = v_t[h * HEAD_DIM : (h + 1) * HEAD_DIM, 0:keys]
                parts.append(jnp.dot(v_h, p, preferred_element_type=f32))
                query = lax.broadcasted_iota(jnp.int32, (1, rows_of), 1) + i * rows_of
                lse_ref[0, h : h + 1, rows] = jnp.where(query < n, peak + jnp.log(total), 1e30)
            o_ref[rows, :] = jnp.concatenate(parts, axis=0).astype(bf16).T

        @pl.when(n >= keys)
        def _():
            run(False)

        @pl.when(n < keys)
        def _():
            run(True)


def attend(frames, qkv):
    length, width = qkv.shape[0], qkv.shape[1] // 3
    pairs = width // LANES
    part = lambda c: pl.BlockSpec((length, LANES), lambda j, n: (0, 3 * j + c))
    return pl.pallas_call(
        functools.partial(attend_kernel, 512),
        grid_spec=pltpu.PrefetchScalarGridSpec(
            num_scalar_prefetch=1,
            grid=(pairs,),
            in_specs=[part(0), part(1), part(2)],
            out_specs=[
                pl.BlockSpec((length, LANES), lambda j, n: (0, j)),
                pl.BlockSpec((1, 2, length), lambda j, n: (j, 0, 0)),
            ],
        ),
        out_shape=[
            jax.ShapeDtypeStruct((length, width), bf16),
            jax.ShapeDtypeStruct((pairs, 2, length), f32),
        ],
        compiler_params=params(),
        cost_estimate=cost(16 * length * length * width, 8 << 20, length * length * 16),
        name="attend",
    )(frames, qkv, qkv, qkv)


def mid_kernel(count, groups, block, tab, x_ref, gain_ref, *refs):
    o_refs, refs = refs[:groups], refs[groups:]
    weights = refs[:count]
    mid_ref, u_ref, u_t_ref, w_nat = refs[count:]

    @pl.when(pl.program_id(0) == 0)
    def _():
        natural(w_nat, slice(None), weights, slice(None), tab, block)

    o = jnp.concatenate([ref[...] for ref in o_refs], axis=1)
    mid = x_ref[...].astype(f32) + jnp.dot(o, w_nat[...], preferred_element_type=f32)
    r = lax.rsqrt(jnp.mean(mid * mid, axis=1, keepdims=True) + NORM_EPS)
    u = (mid * r * gain_ref[1:2, :]).astype(bf16)
    mid_ref[...] = mid
    u_ref[...] = u
    u_t_ref[...] = u.T


def middle(tab, o, x, gains, pieces, block):
    length, width = x.shape
    rows = 256
    row = pl.BlockSpec((rows, width), lambda i, t: (i, 0))
    return pl.pallas_call(
        functools.partial(mid_kernel, len(pieces), len(o), block),
        grid_spec=pltpu.PrefetchScalarGridSpec(
            num_scalar_prefetch=1,
            grid=(length // rows,),
            in_specs=[row, full((8, width))]
            + [pl.BlockSpec((rows, v.shape[1]), lambda i, t: (i, 0)) for v in o]
            + [full(p.shape) for p in pieces],
            out_specs=[row, row, pl.BlockSpec((width, rows), lambda i, t: (0, i))],
            scratch_shapes=[pltpu.VMEM((width, width), bf16)],
        ),
        out_shape=[
            jax.ShapeDtypeStruct((length, width), f32),
            jax.ShapeDtypeStruct((length, width), bf16),
            jax.ShapeDtypeStruct((width, length), bf16),
        ],
        compiler_params=params(),
        cost_estimate=cost(2 * length * width * width, 16 << 20),
        name="middle",
    )(tab, x, gains, *o, *pieces)


def gelu_both(z):
    sq = z * z
    t = jnp.tanh(z * (GELU_A + (GELU_A * GELU_B) * sq))
    half = 0.5 + 0.5 * t
    slope = half + (0.5 * z) * (1.0 - t * t) * (GELU_A + (3 * GELU_A * GELU_B) * sq)
    return z * half, slope


def norm_back(v, gain, du):
    r = lax.rsqrt(jnp.mean(v * v, axis=1, keepdims=True) + NORM_EPS)
    up = du * gain
    return r * up - v * (r * r * r * jnp.mean(up * v, axis=1, keepdims=True))


def mlp_kernel(counts, block, first, last, outs, tab, *refs):
    refs = list(refs)
    take = lambda n: [refs.pop(0) for _ in range(n)]
    u_hbm, u_t_hbm, g_hbm = take(3)
    pieces = [take(count) for count in counts]
    (held_out,) = take(1)
    held_du = None if first else take(1)[0]
    if last:
        mid_hbm, gain_hbm = take(2)
        o_hbm, w_hbm = take(outs[0]), take(outs[1])
    (out_hbm,) = take(1)
    if last:
        dmid_hbm, do_hbm = take(2)
    else:
        (du_hbm,) = take(1)
    sent, kept = take(2)
    u, u_t, g, up_s, down_s, out_acc, du_acc, a_s, dz_s, grad, low, gain, sems = refs
    length, width = u.shape
    wide = 512
    halves = width // wide
    blocks = width // block
    subs = len(counts)
    free = iter(range(sems.shape[0]))

    def copy(src, dst):
        return pltpu.make_async_copy(src, dst, sems.at[next(free)])

    def rows(held, at, columns, dst, dst_columns):
        out, j = [], 0
        for piece in held:
            for i in range(piece.shape[0] // block):
                row = pl.multiple_of(tab[j] * block, block)
                src = piece.at[pl.ds(i * block, block), pl.ds(at, columns)]
                out.append(copy(src, dst.at[pl.ds(row, block), dst_columns]))
                j += 1
        return out

    def back(columns, sent_to, kept_to, at):
        out = []
        for j in range(blocks):
            row = pl.multiple_of(tab[j] * block, block)
            to = kept_to if j < blocks // 2 else sent_to
            dst = to.at[pl.ds(j % (blocks // 2) * block, block), pl.ds(at, columns)]
            out.append(copy(grad.at[pl.ds(row, block), pl.ds(0, columns)], dst))
        return out

    def start(copies):
        for c in copies:
            c.start()

    def wait(copies):
        for c in copies:
            c.wait()

    get_u, get_g, get_t = [copy(u_hbm, u)], [copy(g_hbm, g)], [copy(u_t_hbm, u_t)]
    get_up = [
        [rows(pieces[i], f * wide, wide, up_s.at[i], pl.ds(f * wide, wide)) for f in range(halves)]
        for i in range(subs)
    ]
    get_down = [rows(pieces[i], width, width, down_s.at[i], pl.ds(0, width)) for i in range(subs)]
    get_acc = [copy(held_out, out_acc)] + ([] if first else [copy(held_du, du_acc)])
    start(get_u + get_up[0][0] + get_g + get_down[0] + get_t)
    for f in range(1, halves):
        start(get_up[0][f])
    start(get_acc)
    for i in range(1, subs):
        start(sum(get_up[i], []) + get_down[i])
    waiting, saved = [], []
    half = length // 2
    for i in range(subs):
        up, down = up_s.at[i], down_s.at[i]
        final = i == subs - 1
        for f in range(halves):
            cols = slice(f * wide, (f + 1) * wide)
            wait((get_u if i + f == 0 else []) + get_up[i][f])
            z = jnp.dot(u[...], up[:, cols], preferred_element_type=f32)
            a, slope = gelu_both(z)
            if f == 0:
                wait((get_g if i == 0 else []) + get_down[i])
            da = lax.dot_general(g[...], down[cols, :], NT, preferred_element_type=f32)
            a_s[:, cols] = a.astype(bf16)
            dz_s[:, cols] = (da * slope).astype(bf16)
            if f == 0:
                wait((get_t if i == 0 else []) + waiting)
            part = jnp.dot(u_t[...], dz_s[:, cols], preferred_element_type=f32)
            grad[:, cols] = part.astype(bf16)
            turned = lax.dot_general(a_s[:, cols], g[...], TN, preferred_element_type=f32)
            grad[cols, width:] = turned.astype(bf16)
        waiting = back(2 * width, sent, kept, 2 * i * width)
        start(waiting)
        if i == 0:
            wait(get_acc)
        for r in range(2):
            part = pl.ds(r * half, half)
            out = out_acc[part, :] + jnp.dot(a_s[part, :], down[...], preferred_element_type=f32)
            if last and final:
                low[part, :] = out.astype(bf16)
                saved.append(copy(low.at[part], out_hbm.at[part]))
                saved[-1].start()
            else:
                out_acc[part, :] = out
                if final:
                    saved.append(copy(out_acc.at[part], out_hbm.at[part]))
                    saved[-1].start()
        if last and final:
            get_w = rows(w_hbm, 0, width, down, pl.ds(0, width)) + [copy(gain_hbm, gain)]
            start(get_w)
            get_mid = [copy(mid_hbm, out_acc)]
            at = 0
            for o in o_hbm:
                get_mid.append(copy(o, a_s.at[:, pl.ds(at, o.shape[1])]))
                at += o.shape[1]
            start(get_mid)
        for r in range(2):
            part = pl.ds(r * half, half)
            du = lax.dot_general(dz_s[part, :], up[...], NT, preferred_element_type=f32)
            du_acc[part, :] = du if first and i == 0 else du_acc[part, :] + du
            if final and not last:
                saved.append(copy(du_acc.at[part], du_hbm.at[part]))
                saved[-1].start()
    if last:
        wait(get_w + get_mid)
        size = 256
        for r in range(length // size):
            part = pl.ds(r * size, size)
            dmid = g[part, :].astype(f32) + norm_back(out_acc[part, :], gain[1:2, :], du_acc[part, :])
            du_acc[part, :] = dmid
            u[part, :] = dmid.astype(bf16)
            saved.append(copy(du_acc.at[part], dmid_hbm.at[part]))
            saved[-1].start()
            do = lax.dot_general(u[part, :], down_s[subs - 1], NT, preferred_element_type=f32)
            dz_s[part, :] = do.astype(bf16)
            saved.append(copy(dz_s.at[part], do_hbm.at[part]))
            saved[-1].start()
        wait(waiting)
        turned = lax.dot_general(a_s[...], u[...], TN, preferred_element_type=f32)
        grad[:, 0:width] = turned.astype(bf16)
        waiting = back(width, sent, kept, 2 * subs * width)
        start(waiting)
    wait(waiting + saved)


def feed_forward(tab, u, u_t, g, pieces, held, block, first, last=None):
    length, width = u.shape
    half = width // 2
    anywhere = pl.BlockSpec(memory_space=pl.ANY)
    held = held[:1] if first else held
    inputs = [u, u_t, g, *[p for group in pieces for p in group], *held]
    acc = jax.ShapeDtypeStruct((length, width), f32)
    low = jax.ShapeDtypeStruct((length, width), bf16)
    shard = lambda w: jax.ShapeDtypeStruct((half, w), bf16)
    alias, outs = {}, (0, 0)
    if last:
        mid, gains, o, w_out = last
        inputs += [mid, gains, *o, *w_out]
        outputs = [low, acc, low]
        outs = (len(o), len(w_out))
    else:
        outputs = [acc, acc]
    outputs += [shard(2 * width * len(pieces) + (width if last else 0))] * 2
    blocks = width // block
    subs = len(pieces)
    return pl.pallas_call(
        functools.partial(mlp_kernel, [len(p) for p in pieces], block, first, last is not None, outs),
        grid_spec=pltpu.PrefetchScalarGridSpec(
            num_scalar_prefetch=1,
            grid=(1,),
            in_specs=[anywhere] * len(inputs),
            out_specs=[anywhere] * len(outputs),
            scratch_shapes=[
                pltpu.VMEM((length, width), bf16),
                pltpu.VMEM((width, length), bf16),
                pltpu.VMEM((length, width), bf16),
                pltpu.VMEM((subs, width, width), bf16),
                pltpu.VMEM((subs, width, width), bf16),
                pltpu.VMEM((length, width), f32),
                pltpu.VMEM((length, width), f32),
                pltpu.VMEM((length, width), bf16),
                pltpu.VMEM((length, width), bf16),
                pltpu.VMEM((width, 2 * width), bf16),
                pltpu.VMEM((length, width) if last else (16, LANES), bf16),
                pltpu.VMEM((8, width), f32),
                pltpu.SemaphoreType.DMA(((4 * subs + 2) * blocks + 32,)),
            ],
        ),
        out_shape=outputs,
        input_output_aliases=alias,
        compiler_params=params(),
        cost_estimate=cost((12 * subs + 4 * outs[0]) * length * width * width, 48 << 20),
        name="feed_forward",
    )(tab, *inputs)


def attend_back_kernel(
    rows_of, block, n_ref, tab, q_ref, k_ref, v_ref, g_ref, lse_ref, u_t_ref, d_ref, sent, kept, dk, dv, d_s, grad
):
    n = n_ref[0]
    length = q_ref.shape[0]
    scale = HEAD_DIM**-0.5
    lane = lax.broadcasted_iota(jnp.int32, (1, LANES), 1)
    masks = [(lane < HEAD_DIM).astype(bf16), (lane >= HEAD_DIM).astype(bf16)]
    dk[...] = jnp.zeros_like(dk)
    dv[...] = jnp.zeros_like(dv)
    for i in range(length // rows_of):
        rows = pl.ds(i * rows_of, rows_of)
        keys = (i + 1) * rows_of

        @pl.when(n > i * rows_of)
        def _():
            q = q_ref[rows, :] * bf16(scale)
            g = g_ref[rows, :]
            k, v = k_ref[0:keys, :], v_ref[0:keys, :]
            dq = None
            for h in range(2):
                q_h, g_h, k_h = q * masks[h], g * masks[h], k * masks[h]
                s = lax.dot_general(k, q_h, NT, preferred_element_type=f32)
                key = lax.broadcasted_iota(jnp.int32, (rows_of, rows_of), 0)
                query = lax.broadcasted_iota(jnp.int32, (rows_of, rows_of), 1)
                tail = jnp.where(key <= query, s[keys - rows_of :], -1e30)
                s = tail if i == 0 else jnp.concatenate([s[: keys - rows_of], tail], axis=0)
                p = jnp.exp(s - lse_ref[0, h : h + 1, rows])
                dp = lax.dot_general(v, g_h, NT, preferred_element_type=f32)
                delta = fold(p * dp, jnp.sum)
                ds = (p * (dp - delta)).astype(bf16)
                dv[0:keys, :] += jnp.dot(p.astype(bf16), g_h, preferred_element_type=f32)
                dk[0:keys, :] += jnp.dot(ds, q_h, preferred_element_type=f32)
                part = lax.dot_general(ds, k_h, TN, preferred_element_type=f32)
                dq = part if dq is None else dq + part
            d_s[rows, 0:LANES] = (dq * scale).astype(bf16)

        @pl.when(n <= i * rows_of)
        def _():
            d_s[rows, 0:LANES] = jnp.zeros((rows_of, LANES), bf16)

    d_s[:, LANES : 2 * LANES] = dk[...].astype(bf16)
    d_s[:, 2 * LANES :] = dv[...].astype(bf16)
    d_ref[...] = d_s[...]
    grad[...] = jnp.dot(u_t_ref[...], d_s[...], preferred_element_type=f32)
    relative(sent, kept, slice(None), grad, slice(None), tab, block)


def attend_back(frames, tab, qkv, g, lse, u_t, first, at, pairs, block):
    length, width = qkv.shape[0], u_t.shape[0]
    wide = 3 * LANES
    part = lambda c: pl.BlockSpec((length, LANES), lambda j, n, t: (0, 3 * (j + at) + c))
    half = width // 2
    out = pl.BlockSpec((half, wide), lambda j, n, t: (0, j))
    shape = jax.ShapeDtypeStruct((half, pairs * wide), f32)
    return pl.pallas_call(
        functools.partial(attend_back_kernel, 256, block),
        grid_spec=pltpu.PrefetchScalarGridSpec(
            num_scalar_prefetch=2,
            grid=(pairs,),
            in_specs=[
                part(0),
                part(1),
                part(2),
                pl.BlockSpec((length, LANES), lambda j, n, t: (0, j + first)),
                pl.BlockSpec((1, 2, length), lambda j, n, t: (j + at, 0, 0)),
                full((width, length), True),
            ],
            out_specs=[pl.BlockSpec((length, wide), lambda j, n, t: (0, j)), out, out],
            scratch_shapes=[
                pltpu.VMEM((length, LANES), f32),
                pltpu.VMEM((length, LANES), f32),
                pltpu.VMEM((length, wide), bf16),
                pltpu.VMEM((width, wide), f32),
            ],
        ),
        out_shape=[jax.ShapeDtypeStruct((length, pairs * wide), bf16), shape, shape],
        compiler_params=params(),
        cost_estimate=cost(40 * length * length * pairs * LANES, 16 << 20, length * length * 2 * pairs),
        name="attend_back",
    )(frames, tab, qkv, qkv, qkv, g, lse, u_t)


def input_grad_kernel(groups, parts, more, block, tab, dmid_ref, x_ref, gain_ref, *refs):
    refs = refs[more:]
    d_refs, refs = refs[:parts], refs[parts:]
    weights, out_ref, nats = refs[: -1 - groups], refs[-1 - groups], refs[-groups:]
    count = len(weights) // groups

    @pl.when(pl.program_id(0) == 0)
    def _():
        for i, nat in enumerate(nats):
            natural(nat, slice(None), weights[i * count : (i + 1) * count], slice(None), tab, block)

    du = None
    d_refs = list(d_refs)
    for nat in nats:
        mine = []
        while sum(v.shape[1] for v in mine) < nat.shape[1]:
            mine.append(d_refs.pop(0)[...])
        d = mine[0] if len(mine) == 1 else jnp.concatenate(mine, axis=1)
        part = lax.dot_general(d, nat[...], NT, preferred_element_type=f32)
        du = part if du is None else du + part
    out_ref[...] = dmid_ref[...] + norm_back(x_ref[...].astype(f32), gain_ref[0:1, :], du)


def input_grad(tab, d, dmid, x, gains, pieces, block, lo, hi, done=()):
    length, width = x.shape
    rows = 256
    groups = len(pieces)
    columns = 3 * width // groups
    row = lambda w: pl.BlockSpec((rows, w), lambda i, t: (i + lo, 0))
    weights = [
        pl.BlockSpec((p.shape[0], columns), lambda i, t: (0, 0), pipeline_mode=pl.Buffered(1))
        for group in pieces
        for p in group
    ]
    return pl.pallas_call(
        functools.partial(input_grad_kernel, groups, len(d), len(done), block),
        grid_spec=pltpu.PrefetchScalarGridSpec(
            num_scalar_prefetch=1,
            grid=(hi - lo,),
            in_specs=[row(width), row(width), full((8, width))]
            + [pl.BlockSpec(memory_space=pl.ANY)] * len(done)
            + [row(v.shape[1]) for v in d]
            + weights,
            out_specs=row(width),
            scratch_shapes=[pltpu.VMEM((width, columns), bf16)] * groups,
        ),
        out_shape=jax.ShapeDtypeStruct((length, width), f32),
        input_output_aliases={4: 0} if done else {},
        compiler_params=params(),
        cost_estimate=cost(6 * length * width * width * (hi - lo) // 4, 22 << 20),
        name="input_grad",
    )(tab, dmid, x, gains, *done, *d, *[p for group in pieces for p in group])


def adam_step(weight, first, second, gradient, clip_factor, step_rate, decay_rate, shadow):
    clipped = gradient * clip_factor
    first_new = BETA_ONE * first + (1.0 - BETA_ONE) * clipped
    second_new = BETA_TWO * second + (1.0 - BETA_TWO) * clipped * clipped
    first_hat = first_new / (1.0 - BETA_ONE**STEP)
    second_hat = second_new / (1.0 - BETA_TWO**STEP)
    weight_new = weight - step_rate * (
        first_hat / (jnp.sqrt(second_hat) + ADAM_EPS) + decay_rate * weight
    )
    shadow_new = SHADOW_KEEP * shadow + (1.0 - SHADOW_KEEP) * weight_new
    return (weight_new, first_new, second_new, shadow_new)


def square(v):
    return jnp.sum(v * v)


def view(refs, views, i, lo=0, hi=None):
    array, at, width = views[i]
    return refs[array][:, at + lo : at + (width if hi is None else hi)].astype(f32)


def norm_kernel(arrays, views, parts, *refs):
    grads, rest = refs[:arrays], refs[arrays:]
    weights, (gains, everyone, gain_grad) = rest[:-3], rest[-3:]
    rows, width = gains.shape[1], D
    one = two = jnp.zeros((rows, 1), f32)
    total = square(view(grads, views, parts))
    for i in range(parts):
        grad = view(grads, views, i)
        total = total + square(grad)
        one = one + jnp.sum(weights[i][...].astype(f32) * grad, axis=1, keepdims=True)
    for i in range(len(views) - parts - 1):
        grad = view(grads, views, parts + 1 + i)
        total = total + square(grad)
        up = weights[parts + i][...].astype(f32) * grad[:, :width]
        two = two + jnp.sum(up, axis=1, keepdims=True)
    lane = lax.broadcasted_iota(jnp.int32, (rows, LANES), 1)
    both = jnp.where(lane == 0, one, two)
    both = both.T[0:2, :] / gains[...].astype(bf16).astype(f32)
    gain_grad[...] = both
    everyone[...] = jnp.broadcast_to(total + square(both), everyone.shape)


def square_sums(arrays, views, parts, weights, gains, ndev):
    place = pl.BlockSpec(memory_space=pltpu.VMEM)
    inputs = [*arrays, *weights, gains]
    return pl.pallas_call(
        functools.partial(norm_kernel, len(arrays), views, parts),
        in_specs=[place] * len(inputs),
        out_specs=[place] * 2,
        out_shape=[
            jax.ShapeDtypeStruct((ndev, 1, LANES), f32),
            jax.ShapeDtypeStruct(gains.shape, f32),
        ],
        compiler_params=params(),
        name="square_sums",
    )(*inputs)


def adam_kernel(arrays, views, parts, rates, decays, sums_ref, *refs):
    grads, gain_grad, refs = refs[:arrays], refs[arrays], refs[arrays + 1 :]
    states, outs = refs[:20], refs[20:]
    norm = jnp.sqrt(jnp.sum(sums_ref[...], axis=0))
    outs[20][...] = norm
    clip = jnp.minimum(1.0, CLIP_NORM / norm[:, 0:1])

    def update(i, rows, cols, grad):
        w, m, v, s = [states[4 * i + k][rows, cols] for k in range(4)]
        new = adam_step(w, m, v, grad, clip, rates[i], decays[i], s)
        for k in range(4):
            outs[4 * i + k][rows, cols] = new[k]

    every = slice(None)
    col = 0
    for p in range(parts):
        for j in range(views[p][2] // (3 * LANES)):
            for c in range(3):
                at = c * D + col * LANES
                src = (3 * j + c) * LANES
                update(0, every, slice(at, at + LANES), view(grads, views, p, src, src + LANES))
            col += 1
    update(1, every, every, view(grads, views, parts))
    own = states[0].shape[0]
    subs = FF // D
    size = subs * own
    for at in range(0, FF, LANES):
        pieces = [
            view(grads, views, parts + 1 + q, dev * own, (dev + 1) * own)
            for dev in range(at // size, (at + LANES) // size)
            for q in range(subs)
        ]
        update(2, every, slice(at, at + LANES), jnp.concatenate(pieces, axis=1))
    for q in range(subs):
        grad = view(grads, views, parts + 1 + q, D, 2 * D)
        update(3, slice(q * own, (q + 1) * own), every, grad)
    update(4, every, every, gain_grad[...])


def adam(sums, arrays, views, parts, gain, states, rates, decays):
    place = pl.BlockSpec(memory_space=pltpu.VMEM)
    inputs = [sums, *arrays, gain, *[v for group in states for v in group]]
    outputs = [jax.ShapeDtypeStruct(v.shape, f32) for group in states for v in group]
    outputs.append(jax.ShapeDtypeStruct((1, LANES), f32))
    done = pl.pallas_call(
        functools.partial(adam_kernel, len(arrays), views, parts, rates, decays),
        in_specs=[place] * len(inputs),
        out_specs=[place] * len(outputs),
        out_shape=outputs,
        compiler_params=params(),
        name="adam",
    )(*inputs)
    return [done[4 * i : 4 * i + 4] for i in range(5)], done[-1][0, 0]


def body(plan, *args):
    inputs, cotangent, frames = args[:3]
    masters, firsts, seconds, shadows = args[3:8], args[8:13], args[13:18], args[18:23]
    w_qkv, w_out, w_up, w_down, norm_gains = masters
    block, ndev = plan.block, plan.ndev
    x = inputs[0]
    length = x.shape[0]
    own = D // ndev
    subs = FF // D
    tab = lax.dynamic_index_in_dim(jnp.asarray(plan.tab), lax.axis_index("dp"), 0, keepdims=False)

    wide = D // GROUPS
    pairs = wide // LANES
    columns = 3 * wide
    every = D // LANES
    qkv_low = w_qkv.astype(bf16).reshape(own, 3, every, LANES).transpose(0, 2, 1, 3).reshape(own, 3 * D)
    gain_cols = jnp.pad(norm_gains.astype(bf16).T, ((0, 0), (0, LANES - 2)))
    local_q0 = jnp.concatenate([qkv_low[:, :columns], gain_cols], axis=1)
    up_low = w_up.astype(bf16).reshape(own, ndev, subs, own).transpose(2, 0, 1, 3).reshape(subs, own, D)
    down_low = w_down.astype(bf16).reshape(subs, own, D)
    local_mlp = [v for q in range(subs) for v in (up_low[q], down_low[q])]
    early = jnp.concatenate([qkv_low[:, columns:], w_out.astype(bf16)] + local_mlp[:2], axis=1)
    late = jnp.concatenate(local_mlp[2:], axis=1)
    keep = (jnp.arange(length) < frames[0])[:, None]
    g_low = jnp.where(keep, cotangent[0], jnp.zeros((), bf16))

    flow = Flow(plan)
    step = flow.step
    reach = lambda v: lax.all_gather(v, "fsdp", axis=0, tiled=True)
    early = reach(early)
    flow.gather("q0", reach(local_q0))
    step(None, ["q0"])
    late = reach(late)
    flow.gather("q1", early, 0, columns)
    flow.gather("o", early, columns, D)
    flow.gather("m0", early, columns + D, 2 * D)
    for k in range(1, subs):
        flow.gather(f"m{k}", late, 2 * (k - 1) * D, 2 * D)
    g_low = step(g_low, ["q0"])
    step(None, ["q0"])
    flow.until(None, ["q0"])
    step(None, ["q1", "o", "m0"])
    qkv0, u_one, gains, u_one_t = project_qkv(tab, x, flow.done["q0"], block, columns, True)
    qkv0, u_one = step((qkv0, u_one), ["q1", "o"])
    o0, lse0 = attend(frames, qkv0)
    o0, u_one = step((o0, u_one), ["q1", "o", "m0", "m1"])
    u_one = flow.until(u_one, ["q1"])
    (qkv1,) = project_qkv(tab, u_one, flow.done["q1"], block, columns, False)
    qkv1 = step(qkv1, ["o", "m1", "m2"])
    o1, lse1 = attend(frames, qkv1)
    qkv, o, lse = [qkv0, qkv1], [o0, o1], [lse0, lse1]
    o = step(o, ["o", "m0", "m2"])
    o = flow.until(o, ["o"])
    full_out = flow.done["o"]
    mid, u_two, u_two_t = middle(tab, o, x, gains, full_out, block)
    u_two = step(u_two, ["m0", "m1", "m3"])
    held = [mid, None]
    plans = [["m1", "m2", "m3", "g0"], ["m2", "m3", "g0", "g1"], ["m3", "g0", "g1", "g2"]]
    for k in range(subs):
        u_two = flow.until(u_two, [f"m{k}"])
        last = (mid, gains, o, full_out) if k == subs - 1 else None
        out, held_du, *more, sent, kept = feed_forward(
            tab, u_two, u_two_t, g_low, [flow.done[f"m{k}"]], held, block, k == 0, last
        )
        flow.scatter(f"g{k}", sent, kept, kind=bf16 if last else f32)
        if last:
            dmid, (d_o,) = held_du, more
        else:
            held = [out, step(held_du, plans[k])]
    d_o = step(d_o, ["g0", "g1", "g2", "g3"])
    d_o = flow.until(d_o, ["g0"])
    flow.own_rows("g0")
    sizes = [pairs] + [pairs // 2] * (2 * (GROUPS - 1))
    calls = len(sizes)
    starts = [sum(sizes[:i]) for i in range(calls)]
    plans = [["g1", "g2", "g3", "gq0"], ["g2", "g3", "gq0", "gq1"]]
    d_qkv = []
    for i in range(calls):
        group, at = divmod(starts[i], pairs)
        d, sent, kept = attend_back(
            frames, tab, qkv[group], d_o, lse[group], u_one_t, starts[i], at, sizes[i], block
        )
        d_qkv.append(d)
        flow.scatter(f"gq{i}", sent, kept, True)
        if i < calls - 1:
            d_o = step(d_o, plans[i], [f"g{i - 1}"] if i > 0 else [])
            d_o = flow.until(d_o, [f"g{i + 1}"])
            flow.own_rows(f"g{i + 1}")
    some = ["g3", "gq0"]
    dmid, d_qkv = step((dmid, d_qkv), some + ["gq1", "gq2"], ["g1"])
    dmid = flow.until(dmid, some)
    flow.own_rows("g3")
    flow.own_rows("gq0")
    blocks = length // 256
    held_q = [flow.done["q0"], flow.done["q1"]]
    top = input_grad(tab, d_qkv, dmid, x, gains, held_q, block, 0, blocks // 2)
    top, dmid = step((top, dmid), ["gq1", "gq2"], ["g2"])
    grad_in = input_grad(tab, d_qkv, dmid, x, gains, held_q, block, blocks // 2, blocks, (top,))
    grad_in = step(grad_in, ["gq2"], ["g3"])
    flow.until(None, list(flow.live))
    width = [3 * n * LANES for n in sizes]
    at = [3 * n * LANES for n in starts]
    late_parts = [plan.own_rows(flow.done[f"gq{i}"], True) for i in range(1, calls)]
    arrays = [flow.shards[n] for n in ("g3", "g0", "g1", "g2", "gq0")] + late_parts
    views = [(4 + i, 0, width[i]) for i in range(calls)]
    views += [(0, 2 * D, D)] + [(1 + k, 0, 2 * D) for k in range(subs - 1)] + [(0, 0, 2 * D)]
    weights = [qkv_low[:, a : a + w] for a, w in zip(at, width)] + list(up_low)
    sums, gain_shard = square_sums(arrays, views, calls, weights, norm_gains, ndev)
    everyone = lax.all_to_all(sums, AXES, 0, 0)
    rates = (0.6 / D**0.5, 0.6 / FANO**0.5, 0.6 / D**0.5, 0.6 / FF**0.5, 1.0)
    decays = (0.1, 0.1, 0.1, 0.1, 0.0)
    states = [(masters[i], firsts[i], seconds[i], shadows[i]) for i in range(5)]
    updated, grad_norm = adam(
        everyone, arrays, views, calls, gain_shard, states, rates, decays
    )
    return (
        out[None],
        grad_in[None],
        grad_norm,
        *(updated[i][part] for part in range(4) for i in range(5)),
    )


def solution(mesh):
    plan = Plan(mesh)
    split = P(AXES, None)
    lanes = P(None, AXES)
    weights = (split, split, split, split, lanes)
    return jax.shard_map(
        functools.partial(body, plan),
        mesh=mesh,
        in_specs=(P(AXES, None, None), P(AXES, None, None), P(AXES)) + weights * 4,
        out_specs=(P(AXES, None, None), P(AXES, None, None), P()) + weights * 4,
        check_vma=False,
    )
```
